32 devices in a mesh: branch: 2 (over x), mp: 2 (over y), dp: 8 (over z, core).
Axes of the slice: x: 2, y: 2, z: 4, core: 2. Of those that a mesh axis runs over, the one named last changes fastest.
Arguments:
- block_input: bfloat16 [16, 512, 2048], P('dp'), may hold values from -6 to 6
- cotangent: bfloat16 [16, 512, 2048], P('dp', None, ('branch', 'mp')), may hold values from -6 to 6
- segments: int32 [16, 512], P('dp'), may hold values from 0 to 3, never falling along the last dimension, each value on 1 to 256 neighbouring positions
- attend_gain: float32 [2048], replicated, may hold values from 0.5 to 1.5
- attend_shift: float32 [2048], replicated, may hold values from -0.8 to 0.8
- joined_weight: bfloat16 [2048, 6144], P('dp', 'mp'), may hold values from -0.125 to 0.125
- joined_bias: float32 [6144], replicated, may hold values from -0.5 to 0.5
- dense_weight: bfloat16 [2048, 2048], P(('mp', 'dp')), may hold values from -0.5 to 0.5
- dense_bias: float32 [2048], replicated, may hold values from -1.2 to 1.2
- expand_gain: float32 [2048], replicated, may hold values from 0.5 to 1.5
- expand_shift: float32 [2048], replicated, may hold values from -0.8 to 0.8
- up_weight: bfloat16 [2048, 8192], P('dp', 'mp'), may hold values from -0.125 to 0.125
- up_bias: float32 [8192], replicated, may hold values from -1.2 to 1.2
- down_weight: bfloat16 [8192, 2048], P(('mp', 'dp')), may hold values from -0.0625 to 0.0625
- down_bias: float32 [2048], replicated, may hold values from -1.2 to 1.2
Outputs:
- block_output: bfloat16 [16, 512, 2048], P('dp', None, ('branch', 'mp'))
- input_gradient: bfloat16 [16, 512, 2048], P('dp', None, ('branch', 'mp'))
- attend_gain_gradient: float32 [2048], replicated
- attend_shift_gradient: float32 [2048], replicated
- joined_weight_gradient: float32 [2048, 6144], P(('branch', 'dp'), 'mp')
- joined_bias_gradient: float32 [6144], replicated
- dense_weight_gradient: float32 [2048, 2048], P('mp', ('branch', 'dp'))
- dense_bias_gradient: float32 [2048], replicated
- expand_gain_gradient: float32 [2048], replicated
- expand_shift_gradient: float32 [2048], replicated
- up_weight_gradient: float32 [2048, 8192], P(('branch', 'dp'), 'mp')
- up_bias_gradient: float32 [8192], replicated
- down_weight_gradient: float32 [8192, 2048], P('mp', ('branch', 'dp'))
- down_bias_gradient: float32 [2048], replicated
The draws below stay inside these ranges and needn't reach their ends.
Inputs may be any that keep to these rules, and one draw needn't show every extreme that they name: `segments`: along a row the ids never fall and each id holds 1 to 256 of the row's tokens.
All inputs are finite; a program needn't handle non-finite values.
Results may differ from the reference program's by a relative error of at most 0.0092.
Values may be sent and summed in bfloat16 or wider, within the bound.
No kernel may reach another device: no remote copies, remote signals or barrier semaphores. Data moves between devices by JAX's collectives and lax.ppermute only.
A program may use at most 576 MiB of HBM per device.

```python
import math
import jax
import jax.numpy as jnp
import numpy as np
from jax import lax

D = 2048
HEADS = 8
HEAD = 256
ROT = 64
FF = 8192
SEQ = 512
DOCS = 4
ROWS = 16


def with_spikes(array, own_key, source, target, shards_of, factor):
    def block_of(position):
        return (jnp.arange(array.shape[position]) // (array.shape[position] // shards_of)).reshape((-1,) + (1,) * (array.ndim - 1 - position))

    first = jax.random.permutation(own_key, shards_of)[block_of(target)]
    other_side = (block_of(target) + shards_of // 2) % shards_of
    return jnp.where((block_of(source) == first) | (block_of(source) == other_side), factor * array, array)


def block_levels(rng, extent, shards, least, top_value):
    def one(dim, blocks):
        steps = jax.random.uniform(jax.random.fold_in(jax.random.fold_in(rng, 6), dim), (blocks,), jnp.float32, least / len(shards), top_value / len(shards))
        return jnp.repeat(jnp.exp(steps), extent[dim] // blocks).reshape((-1,) + (1,) * (len(extent) - dim - 1))

    loudness = one(*shards[0])
    for cut in shards[1:]:
        loudness = loudness * one(*cut)
    return loudness


def split_up(amount, total, reach, skew):
    loads = [(1 << 20) // math.isqrt(standing ** skew) + 1 for standing in range(2, amount + 1)]
    rest, given = total - reach - (amount - 1), [1] * (amount - 1)
    while rest > 0:
        candidates = [i for i in range(amount - 1) if given[i] < reach]
        mass, remaining = sum([loads[i] for i in candidates]), rest
        for i in candidates:
            extra = min(reach - given[i], max(1, remaining * loads[i] // mass), rest)
            given[i] = given[i] + extra
            rest = rest - extra
    return np.array([reach] + given)


def ragged_sizes(stream_key, count, total, limit, slope):
    if count == 2:
        one = jax.random.randint(stream_key, (), max(1, total - limit), min(limit, total - 1) + 1)
        return jnp.stack([one, total - one])
    sizes = jnp.asarray(split_up(count, total, limit, slope), jnp.int32)
    twos = (count - 1) // 2
    giver, taker = sizes[1:1 + 2 * twos:2], sizes[2:2 + 2 * twos:2]
    slack = jnp.minimum(giver - 1, limit - taker)
    moved = jax.random.randint(jax.random.fold_in(stream_key, 1), (twos,), 0, 1 << 20) % (slack + 1)
    sizes = sizes.at[1:1 + 2 * twos:2].set(giver - moved).at[2:2 + 2 * twos:2].set(taker + moved)
    return sizes[jax.random.permutation(jax.random.fold_in(stream_key, 2), count)]


def centred(own_key, dims, scale, bound, pieces=(), kind=jnp.bfloat16):
    gain = block_levels(own_key, dims, pieces, -0.22, 0.18) if pieces else 1.0
    array = jax.random.normal(own_key, dims, jnp.float32) * scale * gain
    return jnp.minimum(jnp.maximum(array, -bound), bound).astype(kind)


def gaussian_with(rng, shape, scale, most, shards, heavy, kind=jnp.bfloat16):
    array = scale * jax.random.normal(rng, shape, jnp.float32)
    if shards:
        array = array * block_levels(rng, shape, shards, -0.22, 0.18)
    return jnp.clip(with_spikes(array, jax.random.fold_in(rng, 3), *heavy), -most, most).astype(kind)


def setup_inputs(seed: int = 0) -> dict:
    key_of = jax.random.split(jax.random.key(seed), 16)
    return {
        "block_input": gaussian_with(key_of[0], (ROWS, SEQ, D), 1.0, 6.0, ((0, 8),), (0, 2, 8, 2.0)),
        "cotangent": centred(key_of[1], (ROWS, SEQ, D), 1.0, 6.0, ((0, 8), (2, 4))),
        "segments": jax.vmap(lambda own: jnp.searchsorted(jnp.cumsum(ragged_sizes(own, DOCS, SEQ, SEQ // 2, 2)), jnp.arange(SEQ), side="right"))(jax.random.split(key_of[2], ROWS)).reshape((ROWS, SEQ)).astype(jnp.int32),
        "attend_gain": jnp.clip(1.0 + 0.1 * jax.random.normal(key_of[3], (D,), jnp.float32), 0.5, 1.5),
        "attend_shift": centred(key_of[4], (D,), 0.2, 0.8, (), jnp.float32),
        "joined_weight": centred(key_of[5], (D, 3 * D), D ** -0.5, 0.125, ((0, 8), (1, 2))),
        "joined_bias": centred(key_of[6], (3 * D,), 0.1, 0.5, (), jnp.float32),
        "dense_weight": centred(key_of[7], (D, D), (D // 16) ** -0.5, 0.5, ((0, 16),)),
        "dense_bias": centred(key_of[8], (D,), 0.3, 1.2, (), jnp.float32),
        "expand_gain": jnp.clip(1.0 + 0.1 * jax.random.normal(key_of[9], (D,), jnp.float32), 0.5, 1.5),
        "expand_shift": centred(key_of[10], (D,), 0.2, 0.8, (), jnp.float32),
        "up_weight": centred(key_of[11], (D, FF), D ** -0.5, 0.125, ((0, 8), (1, 2))),
        "up_bias": centred(key_of[12], (FF,), 0.3, 1.2, (), jnp.float32),
        "down_weight": centred(key_of[13], (FF, D), FF ** -0.5, 0.0625, ((0, 16),)),
        "down_bias": centred(key_of[14], (D,), 0.3, 1.2, (), jnp.float32),
    }


@jax.custom_vjp
def low(v):
    return lax.optimization_barrier(v.astype(jnp.bfloat16)).astype(jnp.float32)

@jax.custom_vjp
def low_back(v):
    return v

def low_keep(v):
    return (low(v), None)

def low_pass(kept, grad):
    return (grad,)

def back_keep(v):
    return (v, None)

def back_low(kept, grad):
    return (low(grad),)
low.defvjp(low_keep, low_pass)
low_back.defvjp(back_keep, back_low)

def layer_norm(values, gain_vector, shift_vector):
    center = values - lax.optimization_barrier(jnp.mean(values, axis=-1, keepdims=True))
    spread = lax.optimization_barrier(jnp.mean(center * center, axis=-1, keepdims=True))
    return center * lax.rsqrt(spread + 1e-05) * gain_vector + shift_vector

def rotary_tables(segment_row):
    length = segment_row.shape[0]
    before = lax.optimization_barrier(jnp.sum((segment_row[None, :] < segment_row[:, None]).astype(jnp.int32), axis=1))
    places = (jnp.arange(length, dtype=jnp.int32) - before).astype(jnp.float32)
    frequency = 10000.0 ** (-jnp.arange(0, ROT, 2).astype(jnp.float32) / ROT)
    angles = places[:, None] * frequency[None, :]
    return (jnp.cos(angles)[:, None, :], jnp.sin(angles)[:, None, :])

def allowed_pairs(segment_row):
    token_index = jnp.arange(segment_row.shape[0], dtype=jnp.int32)
    return (segment_row[:, None] == segment_row[None, :]) & (token_index[None, :] <= token_index[:, None])

def rotate(values, cosine_table, sine_table):
    half_width = ROT // 2
    first_half = values[..., :half_width]
    second = values[..., half_width:ROT]
    return jnp.concatenate([first_half * cosine_table - second * sine_table, second * cosine_table + first_half * sine_table, values[..., ROT:]], axis=-1)

def matmul(left_side, right_side):
    return jnp.dot(left_side, right_side, precision=lax.Precision.HIGHEST)

def layer(block_row, params, segment_row):
    attend_gain, attend_shift, joined_weight, joined_bias, dense_weight, dense_bias, expand_gain, expand_shift, up_weight, up_bias, down_weight, down_bias = params
    length = block_row.shape[0]
    cosine_table, sine_table = rotary_tables(segment_row)
    allowed = allowed_pairs(segment_row)
    normed = low(layer_norm(block_row, attend_gain, attend_shift))
    joined_raw = low_back(matmul(normed, joined_weight) + joined_bias).reshape(length, HEADS, 3, HEAD)
    queries = low(rotate(joined_raw[:, :, 0], cosine_table, sine_table) * (1.0 / math.sqrt(HEAD)))
    keyset = low(rotate(joined_raw[:, :, 1], cosine_table, sine_table))
    valueset = low(joined_raw[:, :, 2])
    scores = low_back(jnp.einsum('qhd,khd->hqk', queries, keyset, precision=lax.Precision.HIGHEST))
    scores = jnp.where(allowed[None], scores, -1e+30)
    shifted = jnp.exp(scores - lax.optimization_barrier(jnp.max(scores, axis=-1, keepdims=True)))
    probs_low = low(shifted / lax.optimization_barrier(jnp.sum(shifted, axis=-1, keepdims=True)))
    mixed_heads = jnp.einsum('hqk,khd->qhd', probs_low, valueset, precision=lax.Precision.HIGHEST).reshape(length, HEADS * HEAD)
    mixed_heads = low(low_back(mixed_heads))
    attended = matmul(mixed_heads, dense_weight) + dense_bias
    expanded = low(layer_norm(block_row, expand_gain, expand_shift))
    hidden = low_back(matmul(expanded, up_weight) + up_bias)
    activated = low(jax.nn.gelu(hidden, approximate=False))
    return block_row + attended + matmul(activated, down_weight) + down_bias

def reference(block_input, cotangent, segments, attend_gain, attend_shift, joined_weight, joined_bias, dense_weight, dense_bias, expand_gain, expand_shift, up_weight, up_bias, down_weight, down_bias):
    params = tuple((member.astype(jnp.float32) for member in (attend_gain, attend_shift, joined_weight, joined_bias, dense_weight, dense_bias, expand_gain, expand_shift, up_weight, up_bias, down_weight, down_bias)))

    def one_row(totals, row_items):
        block_row, cotangent_row, segment_row = row_items
        output_row, pullback = jax.vjp(lambda values, weights: layer(values, weights, segment_row), block_row.astype(jnp.float32), params)
        input_row, weight_grads = pullback(cotangent_row.astype(jnp.float32))
        totals = jax.tree.map(jnp.add, totals, weight_grads)
        return (totals, (output_row.astype(jnp.bfloat16), input_row.astype(jnp.bfloat16)))
    totals, (block_output, input_gradient) = lax.scan(one_row, jax.tree.map(jnp.zeros_like, params), (block_input, cotangent, segments))
    return (block_output, input_gradient, totals[0], totals[1], totals[2], totals[3], totals[4], totals[5], totals[6], totals[7], totals[8], totals[9], totals[10], totals[11])
```

```python
import math

import jax
import jax.numpy as jnp
from jax import lax
from jax.sharding import Mesh, PartitionSpec as P

HEAD = 256
ROT = 64
NEGATIVE = -1e30
F32 = jnp.float32
BF16 = jnp.bfloat16


def rotary_tables(segment_rows):
    length = segment_rows.shape[1]
    before = jnp.sum(
        (segment_rows[:, None, :] < segment_rows[:, :, None]).astype(jnp.int32), axis=2
    )
    places = (jnp.arange(length, dtype=jnp.int32)[None] - before).astype(F32)
    frequency = 10000.0 ** (-jnp.arange(0, ROT, 2).astype(F32) / ROT)
    angles = places[:, :, None] * frequency
    return jnp.cos(angles), jnp.sin(angles)


def allowed_pairs(segment_rows):
    token_index = jnp.arange(segment_rows.shape[1], dtype=jnp.int32)
    return (segment_rows[:, :, None] == segment_rows[:, None, :]) & (
        token_index[None, :] <= token_index[:, None]
    )


def rotate(values, cosine_table, sine_table):
    half = ROT // 2
    first, second = values[..., :half], values[..., half:ROT]
    return jnp.concatenate(
        [
            first * cosine_table - second * sine_table,
            second * cosine_table + first * sine_table,
            values[..., ROT:],
        ],
        axis=-1,
    )


def dot(left, right, left_dim, right_dim):
    return lax.dot_general(
        left, right, (((left_dim,), (right_dim,)), ((), ())), preferred_element_type=F32
    )


def pick(array, index, axis):
    return lax.dynamic_index_in_dim(array, index, axis, keepdims=False)


def add_low(left, right):
    return (left.astype(F32) + right.astype(F32)).astype(BF16)


SWAP = [(0, 1), (1, 0)]


def chain_sum(parts, index, count):
    from_left = from_right = None
    for step in range(1, count):
        to_right = parts(jnp.clip(index + count - step, 0, count - 1))
        to_left = parts(jnp.clip(index - count + step, 0, count - 1))
        if from_left is not None:
            to_right = add_low(to_right, from_left)
            to_left = add_low(to_left, from_right)
        from_left = lax.ppermute(to_right, "z", [(i, i + 1) for i in range(step)])
        from_right = lax.ppermute(to_left, "z", [(count - 1 - i, count - 2 - i) for i in range(step)])
    total = parts(index).astype(F32)
    if from_left is not None:
        total = total + from_left.astype(F32) + from_right.astype(F32)
    return total


def solution(mesh):
    branches, models, datas = (mesh.shape[name] for name in ("branch", "mp", "dp"))
    cores = 2
    chips = datas // cores
    fine = Mesh(
        mesh.devices.reshape(branches, models, chips, cores), ("branch", "mp", "z", "core")
    )

    def on_device(
        block_input,
        cotangent,
        segments,
        attend_gain,
        attend_shift,
        joined_weight,
        joined_bias,
        dense_weight,
        dense_bias,
        expand_gain,
        expand_shift,
        up_weight,
        up_bias,
        down_weight,
        down_bias,
    ):
        rows, length, width = block_input.shape
        b, m, z, c = (lax.axis_index(name) for name in ("branch", "mp", "z", "core"))
        tokens = rows * length
        span = width // (branches * models)
        column_start = (b * models + m) * span
        heads = branches * cores
        head_columns = joined_weight.shape[1] // heads
        hidden_columns = up_weight.shape[1]
        part = down_weight.shape[0] // branches
        head_slot = b * cores + c

        def swap_core(array):
            return lax.ppermute(array, "core", SWAP)

        def both_cores_columns(mine, theirs):
            other = swap_core(theirs)
            return jnp.where(c == 0, jnp.concatenate([mine, other]), jnp.concatenate([other, mine]))

        by_head = joined_weight.reshape(-1, heads, head_columns)
        joined_piece = both_cores_columns(
            pick(by_head, head_slot, 1), pick(by_head, b * cores + 1 - c, 1)
        )
        by_unit = up_weight.reshape(-1, chips, cores, branches, part)
        mine = pick(pick(by_unit, b, 3), c, 2).reshape(-1, chips * part)
        theirs = pick(pick(by_unit, b, 3), 1 - c, 2).reshape(-1, chips * part)
        up_piece = both_cores_columns(mine, theirs)
        joined_full = lax.all_gather(joined_piece, "z", axis=0, tiled=True)
        dense_full = lax.all_gather(dense_weight, ("z", "core"), axis=0, tiled=True)
        dense_full = lax.dynamic_slice_in_dim(dense_full, head_slot * HEAD, HEAD, 0)
        up_full = lax.all_gather(up_piece, "z", axis=0, tiled=True)
        down_piece = lax.dynamic_slice_in_dim(down_weight, b * part, part, 0)
        down_full = lax.all_gather(down_piece, "z", axis=0, tiled=True)

        joined_bias_here = lax.dynamic_slice_in_dim(
            joined_bias, (m * heads + head_slot) * head_columns, head_columns
        )
        bias_units = up_bias.reshape(models, chips, cores, branches, part)
        up_bias_here = pick(pick(pick(bias_units, b, 3), c, 2), m, 0).reshape(-1)

        x_own = block_input.reshape(tokens, width)
        x = jnp.concatenate([x_own, swap_core(x_own)])
        segment_rows = jnp.concatenate([segments, swap_core(segments)])
        g_piece = cotangent.reshape(tokens, span)
        g_own = jnp.zeros((tokens, width), BF16)
        for db in range(branches):
            for dm in range(models):
                axes = ([("branch", branches)] if db else []) + ([("mp", models)] if dm else [])
                piece = g_piece
                if axes:
                    count = math.prod(size for _, size in axes)
                    piece = lax.ppermute(
                        piece,
                        tuple(name for name, _ in axes),
                        [(i, count - 1 - i) for i in range(count)],
                    )
                start = ((b ^ db) * models + (m ^ dm)) * span
                g_own = lax.dynamic_update_slice(g_own, piece, (0, start))
        g = jnp.concatenate([g_own, swap_core(g_own)])

        xf = x.astype(F32)
        mean = jnp.mean(xf, axis=-1, keepdims=True)
        center = xf - mean
        inverse = lax.rsqrt(jnp.mean(center * center, axis=-1, keepdims=True) + 1e-05)
        hat = center * inverse
        normed = (hat * attend_gain + attend_shift).astype(BF16)
        expanded = (hat * expand_gain + expand_shift).astype(BF16)

        all_rows = 2 * rows
        joined_raw = (dot(normed, joined_full, 1, 0) + joined_bias_here).reshape(
            all_rows, length, 3, HEAD
        )
        cosine, sine = rotary_tables(segment_rows)
        allowed = allowed_pairs(segment_rows)
        scale = 1.0 / math.sqrt(HEAD)
        queries = (rotate(joined_raw[:, :, 0], cosine, sine) * scale).astype(BF16)
        keyset = rotate(joined_raw[:, :, 1], cosine, sine).astype(BF16)
        valueset = joined_raw[:, :, 2].astype(BF16)

        def ein(spec, left, right):
            return jnp.einsum(spec, left, right, preferred_element_type=F32)

        scores = jnp.where(allowed, ein("rqd,rkd->rqk", queries, keyset), NEGATIVE)
        shifted = jnp.exp(scores - jnp.max(scores, axis=-1, keepdims=True))
        probs = shifted / jnp.sum(shifted, axis=-1, keepdims=True)
        probs_low = probs.astype(BF16)
        mixed = ein("rqk,rkd->rqd", probs_low, valueset).astype(BF16).reshape(-1, HEAD)
        mixed_grad = dot(g, dense_full, 1, 1).astype(BF16).reshape(all_rows, length, HEAD)
        probs_grad = ein("rqd,rkd->rqk", mixed_grad, valueset)
        value_grad = ein("rqk,rqd->rkd", probs_low, mixed_grad)
        inner = jnp.sum(probs_grad * probs, axis=-1, keepdims=True)
        score_grad = (probs * (probs_grad - inner)).astype(BF16)
        query_grad = rotate(ein("rqk,rkd->rqd", score_grad, keyset), cosine, -sine) * scale
        key_grad = rotate(ein("rqk,rqd->rkd", score_grad, queries), cosine, -sine)
        joined_grad = (
            jnp.stack([query_grad, key_grad, value_grad], axis=2)
            .reshape(-1, head_columns)
            .astype(BF16)
        )
        dense_part = dot(g, mixed, 0, 0).astype(BF16)
        joined_part = dot(normed, joined_grad, 0, 0).astype(BF16)
        joined_bias_grad = jnp.sum(joined_grad.astype(F32), axis=0)
        normed_grad = dot(joined_grad, joined_full, 1, 1)

        hidden = dot(expanded, up_full, 1, 0) + up_bias_here
        activated_float, gelu_back = jax.vjp(lambda t: jax.nn.gelu(t, approximate=False), hidden)
        activated = activated_float.astype(BF16)
        down_part = dot(g, activated, 0, 0).astype(BF16)
        hidden_grad = gelu_back(dot(g, down_full, 1, 1))[0].astype(BF16)
        up_part = dot(expanded, hidden_grad, 0, 0).astype(BF16)
        up_bias_grad = jnp.sum(hidden_grad.astype(F32), axis=0)
        expanded_grad = dot(hidden_grad, up_full, 1, 1)

        def token_sum(term):
            mine, theirs = term[:tokens], term[tokens:]
            half = tokens // 2
            total = add_low(mine, swap_core(theirs)).reshape(2, half, branches, models, span)
            first, second = total[0], total[1]
            first_in = lax.ppermute(pick(first, 1 - b, 1), "branch", SWAP)
            second_in = lax.ppermute(pick(second, 1 - m, 2), "mp", SWAP)
            first = add_low(pick(first, b, 1), first_in)
            second = add_low(pick(second, m, 2), second_in)
            first_in = lax.ppermute(pick(first, 1 - m, 1), "mp", SWAP)
            second_in = lax.ppermute(pick(second, 1 - b, 1), "branch", SWAP)
            first = pick(first, m, 1).astype(F32) + first_in.astype(F32)
            second = pick(second, b, 1).astype(F32) + second_in.astype(F32)
            return jnp.concatenate([first, second])

        forward = (dot(mixed, dense_full, 1, 0) + dot(activated, down_full, 1, 0)).astype(BF16)
        forward_sum = token_sum(forward)
        residual = lax.dynamic_slice_in_dim(x_own, column_start, span, 1).astype(F32)
        column_bias = lax.dynamic_slice_in_dim(dense_bias + down_bias, column_start, span)
        block_output = (residual + forward_sum + column_bias).astype(BF16)

        weighted = normed_grad * attend_gain + expanded_grad * expand_gain
        input_term = inverse * (
            weighted
            - jnp.mean(weighted, axis=-1, keepdims=True)
            - hat * jnp.mean(weighted * hat, axis=-1, keepdims=True)
        )
        input_sum = token_sum(input_term.astype(BF16))
        g_float = g_piece.astype(F32)
        input_gradient = (g_float + input_sum).astype(BF16)

        row_share = width // (branches * datas)

        def weight_sum(term):
            columns = term.shape[1]
            view = term.reshape(branches, chips, cores * row_share, columns)
            share = chain_sum(lambda j: pick(view, j, 1), z, chips)
            share = share.astype(BF16).reshape(branches, cores, row_share, columns)
            out = jnp.zeros((branches, cores, row_share, columns), BF16)
            for db in range(branches):
                for dc in range(cores):
                    piece = pick(pick(share, b ^ db, 0), c ^ dc, 0)
                    axes = ([("branch", branches)] if db else []) + ([("core", cores)] if dc else [])
                    if axes:
                        count = math.prod(size for _, size in axes)
                        piece = lax.ppermute(
                            piece,
                            tuple(name for name, _ in axes),
                            [(i, count - 1 - i) for i in range(count)],
                        )
                    out = lax.dynamic_update_slice(
                        out, piece[None, None], (b ^ db, c ^ dc, 0, 0)
                    )
            return out.astype(F32)

        dense_sum = weight_sum(dense_part)
        joined_sum = weight_sum(joined_part)
        down_sum = weight_sum(down_part)
        up_sum = weight_sum(up_part)
        joined_out = joined_sum.transpose(2, 0, 1, 3).reshape(row_share, -1)
        dense_out = dense_sum.transpose(0, 1, 3, 2).reshape(-1, row_share)
        up_out = (
            up_sum.reshape(branches, cores, row_share, chips, part)
            .transpose(2, 3, 1, 0, 4)
            .reshape(row_share, hidden_columns)
        )
        down_out = (
            down_sum.reshape(branches, cores, row_share, chips, part)
            .transpose(3, 1, 0, 4, 2)
            .reshape(hidden_columns, row_share)
        )

        attend_gain_grad = jnp.sum(normed_grad * hat, axis=0)
        attend_shift_grad = jnp.sum(normed_grad, axis=0)
        expand_gain_grad = jnp.sum(expanded_grad * hat, axis=0)
        expand_shift_grad = jnp.sum(expanded_grad, axis=0)
        joined_slot = lax.dynamic_update_slice(
            jnp.zeros_like(joined_bias),
            joined_bias_grad,
            ((m * heads + head_slot) * head_columns,),
        )
        up_slot = lax.dynamic_update_slice(
            jnp.zeros((models, chips, cores, branches, part), F32),
            up_bias_grad.reshape(1, chips, 1, 1, part),
            (m, 0, c, b, 0),
        ).reshape(-1)
        out_slot = lax.dynamic_update_slice(
            jnp.zeros((width,), F32), jnp.sum(g_float, axis=0), (column_start,)
        )
        small = jnp.concatenate(
            [
                attend_gain_grad,
                attend_shift_grad,
                expand_gain_grad,
                expand_shift_grad,
                out_slot,
                joined_slot,
                up_slot,
            ]
        )
        small = lax.psum(small, ("branch", "mp", "z", "core"))
        w = width
        joined_end = 5 * w + joined_bias.shape[0]
        return (
            block_output.reshape(rows, length, span),
            input_gradient.reshape(rows, length, span),
            small[:w],
            small[w : 2 * w],
            joined_out,
            small[5 * w : joined_end],
            dense_out,
            small[4 * w : 5 * w],
            small[2 * w : 3 * w],
            small[3 * w : 4 * w],
            up_out,
            small[joined_end:],
            down_out,
            small[4 * w : 5 * w],
        )

    data = ("z", "core")
    everything = ("branch", "z", "core")
    in_specs = (
        P(data, None, None),
        P(data, None, ("branch", "mp")),
        P(data, None),
        P(),
        P(),
        P(data, "mp"),
        P(),
        P(("mp", "z", "core"), None),
        P(),
        P(),
        P(),
        P(data, "mp"),
        P(),
        P(("mp", "z", "core"), None),
        P(),
    )
    out_specs = (
        P(data, None, ("branch", "mp")),
        P(data, None, ("branch", "mp")),
        P(),
        P(),
        P(everything, "mp"),
        P(),
        P("mp", everything),
        P(),
        P(),
        P(),
        P(everything, "mp"),
        P(),
        P("mp", everything),
        P(),
    )
    return jax.shard_map(
        on_device, mesh=fine, in_specs=in_specs, out_specs=out_specs, check_vma=False
    )
```

```python
import functools
import math

import jax
import jax.numpy as jnp
from jax import lax
from jax.experimental import pallas as pl
from jax.experimental.pallas import tpu as pltpu
from jax.sharding import Mesh, PartitionSpec as P

HEAD = 256
ROT = 64
LANES = 128
NEGATIVE = -1e30
VMEM_BYTES = 56 * 1024 * 1024
F32 = jnp.float32
BF16 = jnp.bfloat16


def rotary_tables(segment_rows):
    length = segment_rows.shape[1]
    before = jnp.sum(
        (segment_rows[:, None, :] < segment_rows[:, :, None]).astype(jnp.int32), axis=2
    )
    places = (jnp.arange(length, dtype=jnp.int32)[None] - before).astype(F32)
    frequency = 10000.0 ** (-jnp.arange(0, ROT, 2).astype(F32) / ROT)
    angles = (places[:, :, None] * frequency).reshape(-1, ROT // 2)
    cosine, sine = jnp.cos(angles), jnp.sin(angles)
    none = jnp.zeros_like(sine)
    rest = jnp.zeros((angles.shape[0], LANES - ROT), F32)
    return (
        jnp.concatenate([cosine, cosine, rest + 1.0], axis=1),
        jnp.concatenate([-sine, none, rest], axis=1),
        jnp.concatenate([none, sine, rest], axis=1),
    )


def rotate(values, self_factor, right_factor, left_factor):
    half = ROT // 2
    front = values[:, :LANES]
    turned = (
        front * self_factor
        + pltpu.roll(front, LANES - half, 1) * right_factor
        + pltpu.roll(front, half, 1) * left_factor
    )
    return jnp.concatenate([turned, values[:, LANES:]], axis=1)


def dot(left, right, left_dim, right_dim):
    return lax.dot_general(
        left, right, (((left_dim,), (right_dim,)), ((), ())), preferred_element_type=F32
    )


def whole(shape):
    return pl.BlockSpec(shape, lambda i: (0,) * len(shape), pipeline_mode=pl.Buffered(1))


def tile(rows, columns):
    return pl.BlockSpec((rows, columns), lambda i: (i, 0))


def run(body, steps, ins, outs, args, flops, transcendentals=0):
    shapes = [jax.ShapeDtypeStruct(shape, dtype) for _, shape, dtype in outs]
    moved = sum(a.size * a.dtype.itemsize for a in list(args) + shapes)
    return pl.pallas_call(
        body,
        grid=(steps,),
        in_specs=ins,
        out_specs=[spec for spec, _, _ in outs],
        out_shape=shapes,
        cost_estimate=pl.CostEstimate(
            flops=flops, bytes_accessed=moved, transcendentals=transcendentals
        ),
        compiler_params=pltpu.CompilerParams(vmem_limit_bytes=VMEM_BYTES),
    )(*args)


def statistics(x):
    center = x - jnp.mean(x, axis=-1, keepdims=True)
    inverse = lax.rsqrt(jnp.mean(center * center, axis=-1, keepdims=True) + 1e-05)
    return center * inverse, inverse


def either(steps, mine_ref, other_ref):
    return jnp.where(pl.program_id(0) < steps, mine_ref[...], other_ref[...])


def halves(rows, columns, steps):
    return [
        pl.BlockSpec((rows, columns), lambda i: (jnp.minimum(i, steps - 1), 0)),
        pl.BlockSpec((rows, columns), lambda i: (jnp.maximum(i - steps, 0), 0)),
    ]


def norm_body(steps, mine_ref, other_ref, gain_a, shift_a, gain_e, shift_e, normed_ref, expanded_ref):
    hat, _ = statistics(either(steps, mine_ref, other_ref).astype(F32))
    normed_ref[...] = (hat * gain_a[...] + shift_a[...]).astype(BF16)
    expanded_ref[...] = (hat * gain_e[...] + shift_e[...]).astype(BF16)


def gather_body(steps, starts_ref, *refs):
    pieces, out_ref = refs[:-1], refs[-1]
    span = pieces[0].shape[1]
    for k in range(len(pieces) // 2):
        columns = pl.ds(pl.multiple_of(starts_ref[k], span), span)
        out_ref[:, columns] = either(steps, pieces[2 * k], pieces[2 * k + 1])


def accumulate(ref, value):
    @pl.when(pl.program_id(0) == 0)
    def _():
        ref[...] = value

    @pl.when(pl.program_id(0) != 0)
    def _():
        ref[...] += value


def attention_body(
    normed_ref, joined_ref, bias_ref, self_ref, right_ref, left_ref, column_ref, row_ref, g_ref, dense_ref,
    mixed_ref, grad_ref, bias_grad_ref,
):
    length = normed_ref.shape[0]
    scale = 1.0 / math.sqrt(HEAD)
    factors = self_ref[...], right_ref[...], left_ref[...]
    raw = dot(normed_ref[...], joined_ref[...], 1, 0) + bias_ref[...]
    queries = (rotate(raw[:, :HEAD], *factors) * scale).astype(BF16)
    keyset = rotate(raw[:, HEAD : 2 * HEAD], *factors).astype(BF16)
    valueset = raw[:, 2 * HEAD :].astype(BF16)
    query_index = lax.broadcasted_iota(jnp.int32, (length, length), 0)
    key_index = lax.broadcasted_iota(jnp.int32, (length, length), 1)
    allowed = (column_ref[0] == row_ref[0]) & (key_index <= query_index)
    scores = jnp.where(allowed, dot(queries, keyset, 1, 1), NEGATIVE)
    shifted = jnp.exp(scores - jnp.max(scores, axis=-1, keepdims=True))
    probs = shifted / jnp.sum(shifted, axis=-1, keepdims=True)
    low = probs.astype(BF16)
    mixed_ref[...] = dot(low, valueset, 1, 0).astype(BF16)
    mixed_grad = dot(g_ref[...], dense_ref[...], 1, 1).astype(BF16)
    probs_grad = dot(mixed_grad, valueset, 1, 1)
    value_grad = dot(low, mixed_grad, 0, 0)
    inner = jnp.sum(probs_grad * probs, axis=-1, keepdims=True)
    score_grad = (probs * (probs_grad - inner)).astype(BF16)
    query_grad = rotate(dot(score_grad, keyset, 1, 0) * scale, *back_factors(factors))
    key_grad = rotate(dot(score_grad, queries, 0, 0), *back_factors(factors))
    joined_grad = jnp.concatenate([query_grad, key_grad, value_grad], axis=1).astype(BF16)
    grad_ref[...] = joined_grad
    accumulate(bias_grad_ref, jnp.sum(joined_grad.astype(F32), axis=0, keepdims=True))


def back_factors(factors):
    return factors[0], -factors[1], -factors[2]


def hidden_body(expanded_ref, up_ref, bias_ref, activated_ref, slope_ref):
    block = up_ref.shape[1] // 4
    for k in range(4):
        columns = pl.ds(k * block, block)
        hidden = dot(expanded_ref[...], up_ref[:, columns], 1, 0) + bias_ref[:, columns]
        below = 0.5 * (1.0 + lax.erf(hidden * math.sqrt(0.5)))
        density = jnp.exp(hidden * hidden * -0.5) * (1.0 / math.sqrt(2.0 * math.pi))
        activated_ref[:, columns] = (hidden * below).astype(BF16)
        slope_ref[:, columns] = (below + hidden * density).astype(BF16)


def terms_body(*refs):
    out_ref, start = refs[-1], 0
    for left_ref, right_ref in zip(refs[:-1:2], refs[1:-1:2]):
        stop = start + right_ref.shape[1]
        term = dot(left_ref[...], right_ref[...], 0, 0).astype(BF16)
        out_ref[:, :, :, start:stop] = term.reshape(*out_ref.shape[:3], stop - start)
        start = stop


def hidden_grad_body(g_ref, down_ref, slope_ref, grad_ref, bias_grad_ref):
    grad = dot(g_ref[...], down_ref[...], 1, 1) * slope_ref[...].astype(F32)
    grad = grad.astype(BF16)
    grad_ref[...] = grad
    accumulate(bias_grad_ref, jnp.sum(grad.astype(F32), axis=0, keepdims=True))


def store_blocks(ref, values):
    blocks, span = ref.shape[0], ref.shape[2]
    for k in range(blocks):
        ref[k] = values[:, k * span : (k + 1) * span].astype(BF16)


def forward_body(mixed_ref, dense_ref, active_ref, down_ref, out_ref):
    total = dot(mixed_ref[...], dense_ref[...], 1, 0)
    total += dot(active_ref[...], down_ref[...], 1, 0)
    store_blocks(out_ref, total)


def input_body(
    x_ref, joined_grad_ref, joined_ref, hidden_grad_ref, up_ref, gain_a, gain_e, out_ref, sums_ref
):
    normed_grad = dot(joined_grad_ref[...], joined_ref[...], 1, 1)
    expanded_grad = dot(hidden_grad_ref[...], up_ref[...], 1, 1)
    hat, inverse = statistics(x_ref[...].astype(F32))
    weighted = normed_grad * gain_a[...] + expanded_grad * gain_e[...]
    weighted_mean = jnp.mean(weighted, axis=-1, keepdims=True)
    along = jnp.mean(weighted * hat, axis=-1, keepdims=True)
    store_blocks(out_ref, inverse * (weighted - weighted_mean - hat * along))

    def down(values):
        return jnp.sum(values, axis=0, keepdims=True)

    sums = jnp.concatenate(
        [down(normed_grad * hat), down(normed_grad), down(expanded_grad * hat), down(expanded_grad)]
    )
    accumulate(sums_ref, sums)


def pick(array, index, axis):
    return lax.dynamic_index_in_dim(array, index, axis, keepdims=False)


def add_low(left, right):
    return (left.astype(F32) + right.astype(F32)).astype(BF16)


SWAP = [(0, 1), (1, 0)]


class Chain:
    def __init__(self, view, index, count):
        self.view, self.index, self.count, self.step = view, index, count, 0
        self.held = self.flight = ()

    def term(self, share):
        return pick(self.view, jnp.clip(share, 0, self.count - 1), 0)

    def send(self):
        self.step += 1
        step, count = self.step, self.count
        out = [self.term(self.index + count - step), self.term(self.index - count + step)]
        if self.held:
            out = [add_low(one, two) for one, two in zip(out, self.held)]
        self.flight = (
            lax.ppermute(out[0], "z", [(i, i + 1) for i in range(step)]),
            lax.ppermute(out[1], "z", [(count - 1 - i, count - 2 - i) for i in range(step)]),
        )

    def total(self):
        own = self.term(self.index).astype(F32)
        return (own + self.held[0].astype(F32) + self.held[1].astype(F32)).astype(BF16)


fence = lax.optimization_barrier


def solution(mesh):
    branches, models, datas = (mesh.shape[name] for name in ("branch", "mp", "dp"))
    cores = 2
    chips = datas // cores
    fine = Mesh(
        mesh.devices.reshape(branches, models, chips, cores), ("branch", "mp", "z", "core")
    )

    def on_device(
        block_input,
        cotangent,
        segments,
        attend_gain,
        attend_shift,
        joined_weight,
        joined_bias,
        dense_weight,
        dense_bias,
        expand_gain,
        expand_shift,
        up_weight,
        up_bias,
        down_weight,
        down_bias,
    ):
        rows, length, width = block_input.shape
        b, m, z, c = (lax.axis_index(name) for name in ("branch", "mp", "z", "core"))
        tokens = rows * length
        span = width // (branches * models)
        column_start = (b * models + m) * span
        heads = branches * cores
        head_columns = joined_weight.shape[1] // heads
        hidden_columns = up_weight.shape[1]
        part = down_weight.shape[0] // branches
        units = chips * part
        head_slot = b * cores + c
        row_share = width // (branches * datas)

        def partner(array, **flips):
            names = tuple(name for name, flip in flips.items() if flip)
            if not names:
                return array
            count = 2 ** len(names)
            return lax.ppermute(array, names, [(i, count - 1 - i) for i in range(count)])

        def swap_core(array):
            return partner(array, core=1)

        def in_core_order(mine, other):
            return jnp.where(c == 0, jnp.concatenate([mine, other]), jnp.concatenate([other, mine]))

        def columns_of(array, start, size):
            return lax.dynamic_slice_in_dim(array, start, size, array.ndim - 1)

        def unit_columns(array, core):
            return jnp.concatenate(
                [
                    columns_of(array, ((k * cores + core) * branches + b) * part, part)
                    for k in range(chips)
                ],
                axis=-1,
            )

        def gather(piece):
            return lax.all_gather(piece, "z", axis=0, tiled=True)

        x_own = block_input.reshape(tokens, width)
        g_piece = cotangent.reshape(tokens, span)
        joined_piece = in_core_order(
            columns_of(joined_weight, head_slot * head_columns, head_columns),
            swap_core(columns_of(joined_weight, (b * cores + 1 - c) * head_columns, head_columns)),
        )
        flips = [(db, dm) for db in range(2) for dm in range(2)]
        g_mine = [partner(g_piece, branch=db, mp=dm) for db, dm in flips]
        x_other = swap_core(x_own)
        segment_rows = jnp.concatenate([segments, swap_core(segments)])
        joined_piece, dense_weight = fence((joined_piece, dense_weight))
        spread_dense = chips == heads and HEAD == cores * dense_weight.shape[0]
        if spread_dense:
            few = HEAD // chips
            per_core = chips // cores
            dense_piece = 0
            for j in range(per_core):
                moves = [
                    (
                        (one * chips + one * cores + to) * cores + at,
                        (one * chips + at * per_core + j) * cores + to,
                    )
                    for one in range(branches)
                    for to in range(cores)
                    for at in range(cores)
                ]
                dense_piece = dense_piece + lax.ppermute(
                    dense_weight[j * few : (j + 1) * few], ("branch", "z", "core"), moves
                )
        else:
            dense_piece = dense_weight

        joined_bias_here = columns_of(joined_bias, (m * heads + head_slot) * head_columns, head_columns)
        up_bias_here = unit_columns(columns_of(up_bias, m * hidden_columns, hidden_columns), c)
        down_piece = lax.dynamic_slice_in_dim(down_weight, b * part, part, 0)

        def flat(vector):
            return vector.reshape(1, -1)

        all_tokens = 2 * tokens
        gains = flat(attend_gain), flat(expand_gain)
        small_tile = min(256, length)
        half_steps = tokens // small_tile
        joined_full = gather(joined_piece)
        x_other, joined_piece, up_weight, dense_piece = fence(
            (x_other, joined_piece, up_weight, dense_piece)
        )
        if spread_dense:
            dense_full = gather(dense_piece)
        else:
            dense_full = lax.all_gather(dense_piece, ("z", "core"), axis=0, tiled=True)
            dense_full = lax.dynamic_slice_in_dim(dense_full, head_slot * HEAD, HEAD, 0)
        up_piece = in_core_order(unit_columns(up_weight, c), swap_core(unit_columns(up_weight, 1 - c)))
        normed, expanded = run(
            functools.partial(norm_body, half_steps),
            2 * half_steps,
            halves(small_tile, width, half_steps) + [whole((1, width))] * 4,
            [(tile(small_tile, width), (all_tokens, width), BF16)] * 2,
            (x_own, x_other, gains[0], flat(attend_shift), gains[1], flat(expand_shift)),
            20 * all_tokens * width,
        )
        rotary = rotary_tables(segment_rows)
        normed, expanded, rotary, g_mine, up_piece, down_piece = fence(
            (normed, expanded, rotary, g_mine, up_piece, down_piece)
        )
        g_other = [swap_core(piece) for piece in g_mine]
        starts = jnp.stack([((b ^ db) * models + (m ^ dm)) * span for db, dm in flips])
        (g,) = run(
            functools.partial(gather_body, half_steps),
            2 * half_steps,
            [pl.BlockSpec(memory_space=pltpu.SMEM)]
            + [spec for _ in flips for spec in halves(small_tile, span, half_steps)],
            [(tile(small_tile, width), (all_tokens, width), BF16)],
            (starts, *[piece for pair in zip(g_mine, g_other) for piece in pair]),
            all_tokens * width,
        )
        normed, expanded, rotary, g, up_piece, down_piece = fence(
            (normed, expanded, rotary, g, up_piece, down_piece)
        )
        up_full = gather(up_piece)

        all_rows = 2 * rows
        mixed, joined_grad, joined_bias_grad = run(
            attention_body,
            all_rows,
            [
                tile(length, width),
                whole((width, head_columns)),
                whole((1, head_columns)),
                tile(length, LANES),
                tile(length, LANES),
                tile(length, LANES),
                pl.BlockSpec((1, length, 1), lambda i: (i, 0, 0)),
                pl.BlockSpec((1, 1, length), lambda i: (i, 0, 0)),
                tile(length, width),
                whole((HEAD, width)),
            ],
            [
                (tile(length, HEAD), (all_tokens, HEAD), BF16),
                (tile(length, head_columns), (all_tokens, head_columns), BF16),
                (whole((1, head_columns)), (1, head_columns), F32),
            ],
            (
                normed,
                joined_full,
                flat(joined_bias_here),
                *rotary,
                segment_rows[:, :, None],
                segment_rows[:, None, :],
                g,
                dense_full,
            ),
            2 * all_tokens * (width * (head_columns + HEAD) + 7 * length * HEAD),
            all_tokens * length,
        )

        live = dict(
            mixed=mixed, joined_grad=joined_grad, normed=normed, expanded=expanded, g=g, down=down_piece
        )

        def step(*landing):
            fresh, held, views = fence(
                (dict(live), [chain.flight for chain in landing], [chain.view for chain in waiting])
            )
            live.update(fresh)
            for chain, one in zip(landing, held):
                chain.held, chain.flight = one, ()
            for chain, view in zip(waiting, views):
                chain.view = view
            waiting.clear()

        waiting = []
        share_rows = cores * row_share

        def terms(*pairs):
            rows_tile = max(256, share_rows)
            group = rows_tile // share_rows
            groups = chips // group
            columns = sum(right.shape[1] for _, right in pairs)
            ins, args = [], []
            for left, right in pairs:
                ins += [pl.BlockSpec((all_tokens, rows_tile), lambda i: (0, i)), whole(right.shape)]
                args += [left, right]
            (view,) = run(
                terms_body,
                branches * groups,
                ins,
                [
                    (
                        pl.BlockSpec(
                            (group, 1, share_rows, columns), lambda i: (i % groups, i // groups, 0, 0)
                        ),
                        (chips, branches, share_rows, columns),
                        BF16,
                    )
                ],
                args,
                2 * all_tokens * width * columns,
            )
            chain = Chain(view, z, chips)
            waiting.append(chain)
            return chain

        def spread(chain):
            share = chain.total().reshape(branches, cores, row_share, -1)
            pieces = {}
            for db in range(2):
                for dc in range(2):
                    piece = pick(pick(share, b ^ db, 0), c ^ dc, 0)
                    pieces[db, dc] = partner(piece, branch=db, core=dc)
            return pieces

        def from_device(pieces, branch, core):
            same_core = c == core
            return jnp.where(
                b == branch,
                jnp.where(same_core, pieces[0, 0], pieces[0, 1]),
                jnp.where(same_core, pieces[1, 0], pieces[1, 1]),
            ).astype(F32)

        unit_flops = 2 * all_tokens * width * units
        big_tile = min(512, length)

        def hidden_values():
            return run(
                hidden_body,
                all_tokens // big_tile,
                [tile(big_tile, width), whole((width, units)), whole((1, units))],
                [(tile(big_tile, units), (all_tokens, units), BF16)] * 2,
                (live["expanded"], up_full, flat(up_bias_here)),
                unit_flops,
                2 * all_tokens * units,
            )

        def hidden_gradient():
            return run(
                hidden_grad_body,
                all_tokens // big_tile,
                [tile(big_tile, width), whole((units, width)), tile(big_tile, units)],
                [
                    (tile(big_tile, units), (all_tokens, units), BF16),
                    (whole((1, units)), (1, units), F32),
                ],
                (live["g"], down_full, live.pop("slope")),
                unit_flops,
            )

        blocks = branches * models

        def of_core(core, columns):
            return pl.BlockSpec((small_tile, columns), lambda i: (core * half_steps + i, 0))

        out_blocks = (
            pl.BlockSpec((blocks, small_tile, span), lambda i: (0, i, 0)),
            (blocks, tokens, span),
            BF16,
        )

        def input_terms(core):
            return run(
                input_body,
                half_steps,
                [
                    tile(small_tile, width),
                    of_core(core, head_columns),
                    whole((width, head_columns)),
                    of_core(core, units),
                    whole((width, units)),
                    whole((1, width)),
                    whole((1, width)),
                ],
                [out_blocks, (whole((4, width)), (4, width), F32)],
                (
                    (x_own, x_other)[core],
                    live["joined_grad"],
                    joined_full,
                    live["grad"],
                    up_full,
                    *gains,
                ),
                unit_flops // 2 + all_tokens * width * head_columns,
            )

        def forward_terms(core):
            return run(
                forward_body,
                half_steps,
                [
                    of_core(core, HEAD),
                    whole((HEAD, width)),
                    of_core(core, units),
                    whole((units, width)),
                ],
                [out_blocks],
                (live["mixed"], dense_full, live["active"], down_full),
                unit_flops // 2 + all_tokens * width * HEAD,
            )[0]

        def core_sum(mine, theirs):
            total = add_low(mine, theirs).reshape(branches, models, 2, tokens // 2, span)
            return total[:, :, 0], total[:, :, 1]

        def first_sum(pair):
            one, two = pair
            return (
                add_low(pick(one, b, 0), partner(pick(one, 1 - b, 0), branch=1)),
                add_low(pick(two, m, 1), partner(pick(two, 1 - m, 1), mp=1)),
            )

        def second_sum(pair):
            one, two = pair
            return jnp.concatenate(
                [
                    pick(one, m, 0).astype(F32) + partner(pick(one, 1 - m, 0), mp=1).astype(F32),
                    pick(two, b, 0).astype(F32) + partner(pick(two, 1 - b, 0), branch=1).astype(F32),
                ]
            )

        joined_chain = terms((normed, joined_grad), (g, mixed))
        step()
        down_full = gather(live.pop("down"))
        live.pop("normed")
        for _ in range(chips - 3):
            joined_chain.send()
            step(joined_chain)
        joined_chain.send()
        live["active"], live["slope"] = hidden_values()
        step(joined_chain)
        joined_chain.send()
        down_chain = terms((live["g"], live["active"]))
        step(joined_chain)
        joined_pieces = spread(joined_chain)
        for _ in range(chips - 4):
            down_chain.send()
            step(down_chain)
        down_chain.send()
        live["grad"], live["bias"] = hidden_gradient()
        step(down_chain)
        down_chain.send()
        up_chain = terms((live.pop("expanded"), live["grad"]))
        live.pop("g")
        step(down_chain)
        down_chain.send()
        for _ in range(chips - 3):
            up_chain.send()
            live["out_other"] = forward_terms(1)
            live["out_own"] = forward_terms(0)
            step(*([down_chain] if down_chain.flight else []), up_chain)
        up_chain.send()
        down_pieces = spread(down_chain)
        live["out_other"] = swap_core(live["out_other"])
        live["in_other"], live["sums_other"] = input_terms(1)
        step(up_chain)
        live["out"] = core_sum(live.pop("out_own"), live.pop("out_other"))
        up_chain.send()
        live["out"] = first_sum(live["out"])
        live["in_other"] = swap_core(live["in_other"])
        live["in_own"], live["sums_own"] = input_terms(0)
        step(up_chain)
        live["in"] = core_sum(live.pop("in_own"), live.pop("in_other"))
        live["in"] = first_sum(live["in"])
        up_pieces = spread(up_chain)
        forward_sum = second_sum(live.pop("out"))

        g_float = g_piece.astype(F32)
        joined_slot = lax.dynamic_update_slice(
            jnp.zeros_like(joined_bias),
            joined_bias_grad.reshape(-1),
            ((m * heads + head_slot) * head_columns,),
        )
        up_slot = lax.dynamic_update_slice(
            jnp.zeros((models, chips, cores, branches, part), F32),
            live.pop("bias").reshape(1, chips, 1, 1, part),
            (m, 0, c, b, 0),
        ).reshape(-1)
        out_slot = lax.dynamic_update_slice(
            jnp.zeros((width,), F32), jnp.sum(g_float, axis=0), (column_start,)
        )
        small = jnp.concatenate(
            [
                (live.pop("sums_own") + live.pop("sums_other")).reshape(-1),
                out_slot,
                joined_slot,
                up_slot,
            ]
        )
        small = small + partner(small, core=1)
        small = small + partner(small, branch=1)
        small = small + partner(small, mp=1)
        flip = 1
        while flip < chips:
            small = small + lax.ppermute(small, "z", [(i, i ^ flip) for i in range(chips)])
            flip *= 2
        input_sum = second_sum(live.pop("in"))

        residual = columns_of(x_own, column_start, span).astype(F32)
        column_bias = columns_of(dense_bias + down_bias, column_start, span)
        block_output = (residual + forward_sum + column_bias).astype(BF16)
        input_gradient = (g_float + input_sum).astype(BF16)

        def by_device(pieces):
            return jnp.stack(
                [
                    jnp.stack([from_device(pieces, one, core) for one in range(branches)])
                    for core in range(cores)
                ]
            )

        joined_out = jnp.concatenate(
            [from_device(joined_pieces, *divmod(k, cores))[:, :head_columns] for k in range(heads)],
            axis=1,
        )
        dense_out = jnp.concatenate(
            [from_device(joined_pieces, *divmod(k, cores))[:, head_columns:].T for k in range(heads)]
        )
        up_out = by_device(up_pieces).reshape(cores, branches, row_share, chips, part)
        up_out = up_out.transpose(2, 3, 0, 1, 4).reshape(row_share, hidden_columns)
        down_out = by_device(down_pieces).reshape(cores, branches, row_share, chips, part)
        down_out = down_out.transpose(3, 0, 1, 4, 2).reshape(hidden_columns, row_share)
        w = width
        joined_end = 5 * w + joined_bias.shape[0]
        return (
            block_output.reshape(rows, length, span),
            input_gradient.reshape(rows, length, span),
            small[:w],
            small[w : 2 * w],
            joined_out,
            small[5 * w : joined_end],
            dense_out,
            small[4 * w : 5 * w],
            small[2 * w : 3 * w],
            small[3 * w : 4 * w],
            up_out,
            small[joined_end:],
            down_out,
            small[4 * w : 5 * w],
        )

    data = ("z", "core")
    everything = ("branch", "z", "core")
    in_specs = (
        P(data, None, None),
        P(data, None, ("branch", "mp")),
        P(data, None),
        P(),
        P(),
        P(data, "mp"),
        P(),
        P(("mp", "z", "core"), None),
        P(),
        P(),
        P(),
        P(data, "mp"),
        P(),
        P(("mp", "z", "core"), None),
        P(),
    )
    out_specs = (
        P(data, None, ("branch", "mp")),
        P(data, None, ("branch", "mp")),
        P(),
        P(),
        P(everything, "mp"),
        P(),
        P("mp", everything),
        P(),
        P(),
        P(),
        P(everything, "mp"),
        P(),
        P("mp", everything),
        P(),
    )
    return jax.shard_map(
        on_device, mesh=fine, in_specs=in_specs, out_specs=out_specs, check_vma=False
    )
```

```python
import functools
import math

import jax
import jax.numpy as jnp
from jax import lax
from jax.experimental import pallas as pl
from jax.experimental.pallas import tpu as pltpu
from jax.sharding import Mesh, PartitionSpec as P

HEAD = 256
ROT = 64
LANES = 128
NEGATIVE = -1e30
VMEM_BYTES = 56 * 1024 * 1024
F32 = jnp.float32
BF16 = jnp.bfloat16


def rotary_tables(segment_rows):
    length = segment_rows.shape[1]
    before = jnp.sum(
        (segment_rows[:, None, :] < segment_rows[:, :, None]).astype(jnp.int32), axis=2
    )
    places = (jnp.arange(length, dtype=jnp.int32)[None] - before).astype(F32)
    frequency = 10000.0 ** (-jnp.arange(0, ROT, 2).astype(F32) / ROT)
    angles = (places[:, :, None] * frequency).reshape(-1, ROT // 2)
    cosine, sine = jnp.cos(angles), jnp.sin(angles)
    none = jnp.zeros_like(sine)
    rest = jnp.zeros((angles.shape[0], LANES - ROT), F32)
    return (
        jnp.concatenate([cosine, cosine, rest + 1.0], axis=1),
        jnp.concatenate([-sine, none, rest], axis=1),
        jnp.concatenate([none, sine, rest], axis=1),
    )


def rotate(values, self_factor, right_factor, left_factor):
    half = ROT // 2
    front = values[:, :LANES]
    turned = (
        front * self_factor
        + pltpu.roll(front, LANES - half, 1) * right_factor
        + pltpu.roll(front, half, 1) * left_factor
    )
    return jnp.concatenate([turned, values[:, LANES:]], axis=1)


def dot(left, right, left_dim, right_dim):
    return lax.dot_general(
        left, right, (((left_dim,), (right_dim,)), ((), ())), preferred_element_type=F32
    )


def whole(shape):
    return pl.BlockSpec(shape, lambda i: (0,) * len(shape), pipeline_mode=pl.Buffered(1))


def tile(rows, columns):
    return pl.BlockSpec((rows, columns), lambda i: (i, 0))


def run(body, steps, ins, outs, args, flops, transcendentals=0):
    scratch = []
    if any(isinstance(arg, Line) for arg in args):
        body, ins, args, scratch = put_together(body, ins, args)
    shapes = [jax.ShapeDtypeStruct(shape, dtype) for _, shape, dtype in outs]
    moved = sum(a.size * a.dtype.itemsize for a in list(args) + shapes)
    return pl.pallas_call(
        body,
        grid=(steps,),
        in_specs=ins,
        out_specs=[spec for spec, _, _ in outs],
        out_shape=shapes,
        scratch_shapes=scratch,
        cost_estimate=pl.CostEstimate(
            flops=flops // 64, bytes_accessed=moved // 64, transcendentals=transcendentals // 64
        ),
        compiler_params=pltpu.CompilerParams(vmem_limit_bytes=VMEM_BYTES),
    )(*args)


def put_together(body, ins, args):
    new_ins, new_args, places, scratch = [], [], [], []
    for spec, arg in zip(ins, args):
        if not isinstance(arg, Line):
            new_ins.append(spec)
            new_args.append(arg)
            places.append(None)
        elif arg.full is not None:
            new_ins.append(spec)
            new_args.append(arg.full)
            places.append(None)
        else:
            slots = arg.slots()
            rows, columns = slots[0].shape
            new_ins += [pl.BlockSpec(memory_space=pl.ANY)] * len(slots)
            new_args += slots
            places.append((len(slots), rows, arg.count))
            scratch += [
                pltpu.VMEM((arg.count * rows, columns), slots[0].dtype),
                pltpu.SemaphoreType.DMA((arg.count,)),
            ]
            index = arg.index
    if not scratch:
        return body, new_ins, new_args, []

    def whole_body(index_ref, *refs):
        kept, held = refs[: len(refs) - len(scratch)], refs[len(refs) - len(scratch) :]
        inner, lines, at = [], [], 0
        for place in places:
            if place is None:
                inner.append(kept[at])
                at += 1
            else:
                full_ref, sems = held[2 * len(lines) : 2 * len(lines) + 2]
                lines.append((kept[at : at + place[0]], full_ref, sems, place))
                inner.append(full_ref)
                at += place[0]

        @pl.when(pl.program_id(0) == 0)
        def _():
            for blocks, full_ref, sems, (_, rows, count) in lines:
                for j in range(count):
                    for k, block in enumerate(blocks):

                        @pl.when(count - 1 - index_ref[0] + j == k)
                        def _():
                            pltpu.make_async_copy(
                                block, full_ref.at[pl.ds(j * rows, rows)], sems.at[j]
                            ).start()

            for blocks, full_ref, sems, (_, rows, count) in lines:
                for j in range(count):
                    pltpu.make_async_copy(
                        blocks[0], full_ref.at[pl.ds(j * rows, rows)], sems.at[j]
                    ).wait()

        body(*inner, *kept[at:])

    return (
        whole_body,
        [pl.BlockSpec(memory_space=pltpu.SMEM)] + new_ins,
        [index.reshape(1)] + new_args,
        scratch,
    )


def statistics(x):
    center = x - jnp.mean(x, axis=-1, keepdims=True)
    inverse = lax.rsqrt(jnp.mean(center * center, axis=-1, keepdims=True) + 1e-05)
    return center * inverse, inverse


def either(steps, mine_ref, other_ref):
    return jnp.where(pl.program_id(0) < steps, mine_ref[...], other_ref[...])


def halves(rows, columns, steps):
    return [
        pl.BlockSpec((rows, columns), lambda i: (jnp.minimum(i, steps - 1), 0)),
        pl.BlockSpec((rows, columns), lambda i: (jnp.maximum(i - steps, 0), 0)),
    ]


def norm_body(steps, mine_ref, other_ref, gain_a, shift_a, gain_e, shift_e, normed_ref, expanded_ref):
    hat, _ = statistics(either(steps, mine_ref, other_ref).astype(F32))
    normed_ref[...] = (hat * gain_a[...] + shift_a[...]).astype(BF16)
    expanded_ref[...] = (hat * gain_e[...] + shift_e[...]).astype(BF16)


def gather_body(steps, starts_ref, *refs):
    pieces, out_ref = refs[:-1], refs[-1]
    span = pieces[0].shape[1]
    for k in range(len(pieces) // 2):
        columns = pl.ds(pl.multiple_of(starts_ref[k], span), span)
        out_ref[:, columns] = either(steps, pieces[2 * k], pieces[2 * k + 1])


def accumulate(ref, value):
    @pl.when(pl.program_id(0) == 0)
    def _():
        ref[...] = value

    @pl.when(pl.program_id(0) != 0)
    def _():
        ref[...] += value


def attention_body(
    normed_ref, joined_ref, bias_ref, self_ref, right_ref, left_ref, column_ref, row_ref, g_ref, dense_ref,
    mixed_ref, grad_ref, bias_grad_ref,
):
    length = normed_ref.shape[0]
    scale = 1.0 / math.sqrt(HEAD)
    factors = self_ref[...], right_ref[...], left_ref[...]
    raw = dot(normed_ref[...], joined_ref[...], 1, 0) + bias_ref[...]
    queries = (rotate(raw[:, :HEAD], *factors) * scale).astype(BF16)
    keyset = rotate(raw[:, HEAD : 2 * HEAD], *factors).astype(BF16)
    valueset = raw[:, 2 * HEAD :].astype(BF16)
    query_index = lax.broadcasted_iota(jnp.int32, (length, length), 0)
    key_index = lax.broadcasted_iota(jnp.int32, (length, length), 1)
    allowed = (column_ref[0] == row_ref[0]) & (key_index <= query_index)
    scores = jnp.where(allowed, dot(queries, keyset, 1, 1), NEGATIVE)
    shifted = jnp.exp(scores - jnp.max(scores, axis=-1, keepdims=True))
    probs = shifted / jnp.sum(shifted, axis=-1, keepdims=True)
    low = probs.astype(BF16)
    mixed_ref[...] = dot(low, valueset, 1, 0).astype(BF16)
    mixed_grad = dot(g_ref[...], dense_ref[...], 1, 1).astype(BF16)
    probs_grad = dot(mixed_grad, valueset, 1, 1)
    value_grad = dot(low, mixed_grad, 0, 0)
    inner = jnp.sum(probs_grad * probs, axis=-1, keepdims=True)
    score_grad = (probs * (probs_grad - inner)).astype(BF16)
    query_grad = rotate(dot(score_grad, keyset, 1, 0) * scale, *back_factors(factors))
    key_grad = rotate(dot(score_grad, queries, 0, 0), *back_factors(factors))
    joined_grad = jnp.concatenate([query_grad, key_grad, value_grad], axis=1).astype(BF16)
    grad_ref[...] = joined_grad
    accumulate(bias_grad_ref, jnp.sum(joined_grad.astype(F32), axis=0, keepdims=True))


def back_factors(factors):
    return factors[0], -factors[1], -factors[2]


def hidden_body(expanded_ref, up_ref, bias_ref, activated_ref, slope_ref):
    block = up_ref.shape[1] // 4
    for k in range(4):
        columns = pl.ds(k * block, block)
        hidden = dot(expanded_ref[...], up_ref[:, columns], 1, 0) + bias_ref[:, columns]
        below = 0.5 * (1.0 + lax.erf(hidden * math.sqrt(0.5)))
        density = jnp.exp(hidden * hidden * -0.5) * (1.0 / math.sqrt(2.0 * math.pi))
        activated_ref[:, columns] = (hidden * below).astype(BF16)
        slope_ref[:, columns] = (below + hidden * density).astype(BF16)


def terms_body(*refs):
    out_ref, start = refs[-1], 0
    for left_ref, right_ref in zip(refs[:-1:2], refs[1:-1:2]):
        stop = start + right_ref.shape[1]
        term = dot(left_ref[...], right_ref[...], 0, 0).astype(BF16)
        out_ref[:, :, :, start:stop] = term.reshape(*out_ref.shape[:3], stop - start)
        start = stop


def hidden_grad_body(g_ref, down_ref, slope_ref, grad_ref, bias_grad_ref):
    grad = dot(g_ref[...], down_ref[...], 1, 1) * slope_ref[...].astype(F32)
    grad = grad.astype(BF16)
    grad_ref[...] = grad
    accumulate(bias_grad_ref, jnp.sum(grad.astype(F32), axis=0, keepdims=True))


def store_blocks(out_ref, values, got_refs):
    blocks, span = out_ref.shape[1], out_ref.shape[3]
    for k in range(blocks):
        block = values[:, k * span : (k + 1) * span]
        for got_ref in got_refs:
            block = block + got_ref[0, k].astype(F32)
        out_ref[0, k] = block.astype(BF16)


def forward_body(mixed_ref, dense_ref, active_ref, down_ref, *refs):
    total = dot(mixed_ref[...], dense_ref[...], 1, 0)
    total += dot(active_ref[...], down_ref[...], 1, 0)
    store_blocks(refs[-1], total, refs[:-1])


def input_body(
    x_ref, joined_grad_ref, joined_ref, hidden_grad_ref, up_ref, gain_a, gain_e, *refs
):
    got_refs, (out_ref, sums_ref) = refs[:-2], refs[-2:]
    normed_grad = dot(joined_grad_ref[...], joined_ref[...], 1, 1)
    expanded_grad = dot(hidden_grad_ref[...], up_ref[...], 1, 1)
    hat, inverse = statistics(x_ref[...].astype(F32))
    weighted = normed_grad * gain_a[...] + expanded_grad * gain_e[...]
    weighted_mean = jnp.mean(weighted, axis=-1, keepdims=True)
    along = jnp.mean(weighted * hat, axis=-1, keepdims=True)
    store_blocks(out_ref, inverse * (weighted - weighted_mean - hat * along), got_refs)

    def down(values):
        return jnp.sum(values, axis=0, keepdims=True)

    sums = jnp.concatenate(
        [down(normed_grad * hat), down(normed_grad), down(expanded_grad * hat), down(expanded_grad)]
    )
    accumulate(sums_ref, sums)


def place_body(layouts, pieces_ref, *outs):
    for device in range(pieces_ref.shape[0]):
        for start, size, target, where, turned in layouts:
            offset = where(device) * size
            values = pieces_ref[device, :, start : start + size].astype(F32)
            if turned:
                outs[target][offset : offset + size, :] = values.T
            else:
                outs[target][:, offset : offset + size] = values


def pick(array, index, axis):
    return lax.dynamic_index_in_dim(array, index, axis, keepdims=False)


def add_low(left, right):
    return (left.astype(F32) + right.astype(F32)).astype(BF16)


SWAP = [(0, 1), (1, 0)]


class Chain:
    def __init__(self, view, index, count):
        self.view, self.index, self.count, self.step = view, index, count, 0
        self.held = self.flight = ()
        self.out = []

    def term(self, share):
        return pick(self.view, jnp.clip(share, 0, self.count - 1), 0)

    def prepare(self):
        if self.step == self.count - 1:
            return
        self.step += 1
        step, count = self.step, self.count
        self.out = [self.term(self.index + count - step), self.term(self.index - count + step)]
        if self.held:
            self.out = [add_low(one, two) for one, two in zip(self.out, self.held)]

    def send(self):
        if not self.out:
            self.prepare()
        if not self.out:
            return
        step, count = self.step, self.count
        self.flight = (
            lax.ppermute(self.out[0], "z", [(i, i + 1) for i in range(step)]),
            lax.ppermute(self.out[1], "z", [(count - 1 - i, count - 2 - i) for i in range(step)]),
        )
        self.out = []

    def land(self, values):
        if values:
            self.held, self.flight = values, ()

    def total(self):
        own = self.term(self.index).astype(F32)
        return (own + self.held[0].astype(F32) + self.held[1].astype(F32)).astype(BF16)


class Line:
    def __init__(self, piece, index, count):
        self.index, self.count, self.step, self.flight = index, count, 0, ()
        self.from_left, self.from_right, self.own, self.full = [], [], piece, None
        if count > 4:
            self.full = lax.all_gather(piece, "z", axis=0, tiled=True)

    def send(self):
        if self.full is not None or self.step == self.count - 1:
            return
        step, count = self.step, self.count
        right, left = (self.from_left[-1], self.from_right[-1]) if step else (self.own, self.own)
        self.flight = (
            lax.ppermute(right, "z", [(i, i + 1) for i in range(step, count - 1)]),
            lax.ppermute(left, "z", [(i + 1, i) for i in range(count - 1 - step)]),
        )
        self.step += 1

    def land(self, values):
        if values:
            self.from_left.append(values[0])
            self.from_right.append(values[1])
            self.flight = ()

    def slots(self):
        return [*self.from_left[::-1], self.own, *self.from_right]


fence = lax.optimization_barrier


def solution(mesh):
    branches, models, datas = (mesh.shape[name] for name in ("branch", "mp", "dp"))
    cores = 2
    chips = datas // cores
    fine = Mesh(
        mesh.devices.reshape(branches, models, chips, cores), ("branch", "mp", "z", "core")
    )

    def on_device(
        block_input,
        cotangent,
        segments,
        attend_gain,
        attend_shift,
        joined_weight,
        joined_bias,
        dense_weight,
        dense_bias,
        expand_gain,
        expand_shift,
        up_weight,
        up_bias,
        down_weight,
        down_bias,
    ):
        rows, length, width = block_input.shape
        b, m, z, c = (lax.axis_index(name) for name in ("branch", "mp", "z", "core"))
        tokens = rows * length
        span = width // (branches * models)
        column_start = (b * models + m) * span
        heads = branches * cores
        head_columns = joined_weight.shape[1] // heads
        hidden_columns = up_weight.shape[1]
        part = down_weight.shape[0] // branches
        units = chips * part
        head_slot = b * cores + c
        row_share = width // (branches * datas)

        def partner(array, **flips):
            names = tuple(name for name, flip in flips.items() if flip)
            if not names:
                return array
            count = 2 ** len(names)
            return lax.ppermute(array, names, [(i, count - 1 - i) for i in range(count)])

        def swap_core(array):
            return partner(array, core=1)

        def in_core_order(mine, other):
            return jnp.where(c == 0, jnp.concatenate([mine, other]), jnp.concatenate([other, mine]))

        def columns_of(array, start, size):
            return lax.dynamic_slice_in_dim(array, start, size, array.ndim - 1)

        def unit_columns(array, core):
            return jnp.concatenate(
                [
                    columns_of(array, ((k * cores + core) * branches + b) * part, part)
                    for k in range(chips)
                ],
                axis=-1,
            )

        def gather(piece):
            return lax.all_gather(piece, "z", axis=0, tiled=True)

        x_own = block_input.reshape(tokens, width)
        g_piece = cotangent.reshape(tokens, span)
        joined_piece = in_core_order(
            columns_of(joined_weight, head_slot * head_columns, head_columns),
            swap_core(columns_of(joined_weight, (b * cores + 1 - c) * head_columns, head_columns)),
        )
        flips = [(db, dm) for db in range(2) for dm in range(2)]
        g_mine = [partner(g_piece, branch=db, mp=dm) for db, dm in flips]
        x_other = swap_core(x_own)
        segment_rows = jnp.concatenate([segments, swap_core(segments)])
        joined_piece, dense_weight = fence((joined_piece, dense_weight))
        spread_dense = chips == heads and HEAD == cores * dense_weight.shape[0]
        if spread_dense:
            few = HEAD // chips
            per_core = chips // cores
            dense_piece = 0
            for j in range(per_core):
                moves = [
                    (
                        (one * chips + one * cores + to) * cores + at,
                        (one * chips + at * per_core + j) * cores + to,
                    )
                    for one in range(branches)
                    for to in range(cores)
                    for at in range(cores)
                ]
                dense_piece = dense_piece + lax.ppermute(
                    dense_weight[j * few : (j + 1) * few], ("branch", "z", "core"), moves
                )
        else:
            dense_piece = dense_weight

        joined_bias_here = columns_of(joined_bias, (m * heads + head_slot) * head_columns, head_columns)
        up_bias_here = unit_columns(columns_of(up_bias, m * hidden_columns, hidden_columns), c)
        down_piece = lax.dynamic_slice_in_dim(down_weight, b * part, part, 0)

        def flat(vector):
            return vector.reshape(1, -1)

        all_tokens = 2 * tokens
        gains = flat(attend_gain), flat(expand_gain)
        small_tile = min(256, length)
        half_steps = tokens // small_tile
        joined_full = gather(joined_piece)
        x_other, joined_piece, up_weight, dense_piece = fence(
            (x_other, joined_piece, up_weight, dense_piece)
        )
        if spread_dense:
            dense_full = gather(dense_piece)
        else:
            dense_full = lax.all_gather(dense_piece, ("z", "core"), axis=0, tiled=True)
            dense_full = lax.dynamic_slice_in_dim(dense_full, head_slot * HEAD, HEAD, 0)
        up_piece = in_core_order(unit_columns(up_weight, c), swap_core(unit_columns(up_weight, 1 - c)))
        normed, expanded = run(
            functools.partial(norm_body, half_steps),
            2 * half_steps,
            halves(small_tile, width, half_steps) + [whole((1, width))] * 4,
            [(tile(small_tile, width), (all_tokens, width), BF16)] * 2,
            (x_own, x_other, gains[0], flat(attend_shift), gains[1], flat(expand_shift)),
            20 * all_tokens * width,
        )
        rotary = rotary_tables(segment_rows)
        normed, expanded, rotary, g_mine, up_piece, down_piece = fence(
            (normed, expanded, rotary, g_mine, up_piece, down_piece)
        )
        g_other = [swap_core(piece) for piece in g_mine]
        starts = jnp.stack([((b ^ db) * models + (m ^ dm)) * span for db, dm in flips])
        (g,) = run(
            functools.partial(gather_body, half_steps),
            2 * half_steps,
            [pl.BlockSpec(memory_space=pltpu.SMEM)]
            + [spec for _ in flips for spec in halves(small_tile, span, half_steps)],
            [(tile(small_tile, width), (all_tokens, width), BF16)],
            (starts, *[piece for pair in zip(g_mine, g_other) for piece in pair]),
            all_tokens * width,
        )
        normed, expanded, rotary, g, up_piece, down_piece, joined_full, dense_full = fence(
            (normed, expanded, rotary, g, up_piece, down_piece, joined_full, dense_full)
        )
        up_line = Line(up_piece, z, chips)
        up_line.send()

        all_rows = 2 * rows
        mixed, joined_grad, joined_bias_grad = run(
            attention_body,
            all_rows,
            [
                tile(length, width),
                whole((width, head_columns)),
                whole((1, head_columns)),
                tile(length, LANES),
                tile(length, LANES),
                tile(length, LANES),
                pl.BlockSpec((1, length, 1), lambda i: (i, 0, 0)),
                pl.BlockSpec((1, 1, length), lambda i: (i, 0, 0)),
                tile(length, width),
                whole((HEAD, width)),
            ],
            [
                (tile(length, HEAD), (all_tokens, HEAD), BF16),
                (tile(length, head_columns), (all_tokens, head_columns), BF16),
                (whole((1, head_columns)), (1, head_columns), F32),
            ],
            (
                normed,
                joined_full,
                flat(joined_bias_here),
                *rotary,
                segment_rows[:, :, None],
                segment_rows[:, None, :],
                g,
                dense_full,
            ),
            2 * all_tokens * (width * (head_columns + HEAD) + 7 * length * HEAD),
            all_tokens * length,
        )

        live = dict(
            mixed=mixed, joined_grad=joined_grad, normed=normed, expanded=expanded, g=g, down=down_piece
        )

        def step(*landing):
            fresh, held, views, outs = fence(
                (
                    dict(live),
                    [chain.flight for chain in landing],
                    [chain.view for chain in waiting],
                    [chain.out for chain in chains],
                )
            )
            for chain, out in zip(chains, outs):
                chain.out = out
            live.update(fresh)
            for chain, one in zip(landing, held):
                chain.land(one)
            for chain, view in zip(waiting, views):
                chain.view = view
            waiting.clear()

        waiting, chains = [], []
        share_rows = cores * row_share

        def terms(*pairs):
            rows_tile = max(256, share_rows)
            group = rows_tile // share_rows
            groups = chips // group
            columns = sum(right.shape[1] for _, right in pairs)
            ins, args = [], []
            for left, right in pairs:
                ins += [pl.BlockSpec((all_tokens, rows_tile), lambda i: (0, i)), whole(right.shape)]
                args += [left, right]
            (view,) = run(
                terms_body,
                branches * groups,
                ins,
                [
                    (
                        pl.BlockSpec(
                            (group, 1, share_rows, columns), lambda i: (i % groups, i // groups, 0, 0)
                        ),
                        (chips, branches, share_rows, columns),
                        BF16,
                    )
                ],
                args,
                2 * all_tokens * width * columns,
            )
            chain = Chain(view, z, chips)
            waiting.append(chain)
            chains.append(chain)
            return chain

        def spread(chain):
            share = chain.total().reshape(branches * cores * row_share, -1)
            pieces = lax.all_to_all(share, ("branch", "core"), 0, 0, tiled=True)
            return pieces.reshape(branches * cores, row_share, -1)

        unit_flops = 2 * all_tokens * width * units
        big_tile = min(512, length)

        def hidden_values():
            return run(
                hidden_body,
                all_tokens // big_tile,
                [tile(big_tile, width), whole((width, units)), whole((1, units))],
                [(tile(big_tile, units), (all_tokens, units), BF16)] * 2,
                (live["expanded"], up_line, flat(up_bias_here)),
                unit_flops,
                2 * all_tokens * units,
            )

        def hidden_gradient():
            return run(
                hidden_grad_body,
                all_tokens // big_tile,
                [tile(big_tile, width), whole((units, width)), tile(big_tile, units)],
                [
                    (tile(big_tile, units), (all_tokens, units), BF16),
                    (whole((1, units)), (1, units), F32),
                ],
                (live["g"], down_line, live.pop("slope")),
                unit_flops,
            )

        blocks = branches * models

        def of_core(core, columns):
            return pl.BlockSpec((small_tile, columns), lambda i: (core * half_steps + i, 0))

        def out_blocks(pieces):
            steps = half_steps // pieces
            return (
                pl.BlockSpec((1, blocks, small_tile, span), lambda i: (i // steps, 0, i % steps, 0)),
                (pieces, blocks, tokens // pieces, span),
                BF16,
            )

        def input_terms(core, *got):
            return run(
                input_body,
                half_steps,
                [
                    tile(small_tile, width),
                    of_core(core, head_columns),
                    whole((width, head_columns)),
                    of_core(core, units),
                    whole((width, units)),
                    whole((1, width)),
                    whole((1, width)),
                    *[out_blocks(2)[0]] * len(got),
                ],
                [out_blocks(2), (whole((4, width)), (4, width), F32)],
                (
                    (x_own, x_other)[core],
                    live["joined_grad"],
                    joined_full,
                    live["grad"],
                    up_line,
                    *gains,
                    *got,
                ),
                unit_flops // 2 + all_tokens * width * head_columns,
            )

        def forward_terms(core, *got):
            return run(
                forward_body,
                half_steps,
                [
                    of_core(core, HEAD),
                    whole((HEAD, width)),
                    of_core(core, units),
                    whole((units, width)),
                    *[out_blocks(1)[0]] * len(got),
                ],
                [out_blocks(1)],
                (live["mixed"], dense_full, live["active"], down_line, *got),
                unit_flops // 2 + all_tokens * width * HEAD,
            )[0]

        def block_sum(blocks):
            return lax.psum_scatter(blocks[0], ("branch", "mp"), scatter_dimension=0, tiled=True)[0]

        def first_sends(term):
            one, two = (term[h].reshape(branches, models, tokens // 2, span) for h in range(2))
            return partner(pick(one, 1 - b, 0), branch=1), partner(pick(two, 1 - m, 1), mp=1)

        def first_sum(term, got):
            one, two = (term[h].reshape(branches, models, tokens // 2, span) for h in range(2))
            return add_low(pick(one, b, 0), got[0]), add_low(pick(two, m, 1), got[1])

        def second_sends(pair):
            one, two = pair
            return partner(pick(one, 1 - m, 0), mp=1), partner(pick(two, 1 - b, 0), branch=1)

        def second_sum(pair, got):
            one, two = pair
            return jnp.concatenate(
                [
                    pick(one, m, 0).astype(F32) + got[0].astype(F32),
                    pick(two, b, 0).astype(F32) + got[1].astype(F32),
                ]
            )

        def finish(chain):
            while chain.step < chips - 1:
                chain.send()
                step(chain)
            return spread(chain)

        step(up_line)
        up_line.send()
        joined_chain = terms((live.pop("normed"), live["joined_grad"]), (live["g"], live["mixed"]))
        step(up_line)
        up_line.send()
        joined_chain.send()
        step(up_line, joined_chain)
        down_line = Line(live.pop("down"), z, chips)
        down_line.send()
        live["active"], live["slope"] = hidden_values()
        down_chain = terms((live["g"], live["active"]))
        down_chain.prepare()
        step(down_line)
        down_line.send()
        down_chain.send()
        joined_chain.prepare()
        g_float = g_piece.astype(F32)
        out_slot = lax.dynamic_update_slice(
            jnp.zeros((width,), F32), jnp.sum(g_float, axis=0), (column_start,)
        )
        joined_slot = lax.dynamic_update_slice(
            jnp.zeros_like(joined_bias),
            joined_bias_grad.reshape(-1),
            ((m * heads + head_slot) * head_columns,),
        )
        live["slots"] = jnp.concatenate([out_slot, joined_slot])
        step(down_line, down_chain)
        down_line.send()
        joined_chain.send()
        down_chain.prepare()
        step(down_line, joined_chain)
        joined_chain.send()
        live["grad"], live["bias"] = hidden_gradient()
        live["out_other"] = forward_terms(1)
        step(joined_chain)
        down_chain.send()
        live["out_got"] = swap_core(live.pop("out_other"))
        live["joined_pieces"] = finish(joined_chain)
        up_chain = terms((live.pop("expanded"), live["grad"]))
        live.pop("g")
        up_chain.prepare()
        step(down_chain)
        up_chain.send()
        down_chain.prepare()
        live["out"] = forward_terms(0, live.pop("out_got"))
        live["in_other"], live["sums_other"] = input_terms(1)
        step(up_chain)
        forward_sum = block_sum(live.pop("out"))
        down_chain.send()
        live["in_got"] = swap_core(live.pop("in_other"))
        up_chain.prepare()
        live["in"], live["sums_own"] = input_terms(0, live.pop("in_got"))
        step(down_chain)
        up_chain.send()
        up_slot = lax.dynamic_update_slice(
            jnp.zeros((models, chips, cores, branches, part), F32),
            live.pop("bias").reshape(1, chips, 1, 1, part),
            (m, 0, c, b, 0),
        ).reshape(-1)
        sums = live.pop("sums_own") + live.pop("sums_other")
        small = jnp.concatenate([sums.reshape(-1), live.pop("slots"), up_slot])
        live["in_got"] = first_sends(live["in"])
        live["small"] = (
            small
            + partner(small, core=1)
            + partner(small, branch=1)
            + partner(small, branch=1, core=1)
        )
        step(up_chain)
        up_chain.send()
        live["in"] = first_sum(live["in"], live.pop("in_got"))
        live["in_got"] = second_sends(live["in"])
        small = live["small"]
        near = lax.ppermute(small, "z", [(i, i ^ 1) for i in range(chips)])
        far = [
            lax.ppermute(
                small,
                ("mp", "z"),
                [
                    (one * chips + i, (1 - one) * chips + (i ^ flip))
                    for one in range(models)
                    for i in range(chips)
                ],
            )
            for flip in range(2)
        ]
        live["small"] = small + near + far[0] + far[1]
        live["down_pieces"] = finish(down_chain)
        step(up_chain)
        live["up_pieces"] = finish(up_chain)
        small = live["small"]
        flip = 2
        while flip < chips:
            small = small + lax.ppermute(small, "z", [(i, i ^ flip) for i in range(chips)])
            flip *= 2
        input_sum = second_sum(live.pop("in"), live.pop("in_got"))
        joined_pieces, down_pieces, up_pieces = (
            live[name] for name in ("joined_pieces", "down_pieces", "up_pieces")
        )

        residual = columns_of(x_own, column_start, span).astype(F32)
        column_bias = columns_of(dense_bias + down_bias, column_start, span)
        block_output = (residual + forward_sum + column_bias).astype(BF16)
        input_gradient = (g_float + input_sum).astype(BF16)

        if part % LANES == 0 and row_share % 8 == 0:

            def put(pieces, shapes, layouts):
                return run(
                    functools.partial(place_body, layouts),
                    1,
                    [whole(pieces.shape)],
                    [(whole(shape), shape, F32) for shape in shapes],
                    [pieces],
                    0,
                )

            def unit_layouts(turned):
                return [
                    (
                        k * part,
                        part,
                        0,
                        lambda device, k=k: (k * cores + device % cores) * branches + device // cores,
                        turned,
                    )
                    for k in range(chips)
                ]

            def same(device):
                return device

            joined_out, dense_out = put(
                joined_pieces,
                [(row_share, heads * head_columns), (heads * HEAD, row_share)],
                [(0, head_columns, 0, same, False), (head_columns, HEAD, 1, same, True)],
            )
            (down_out,) = put(down_pieces, [(hidden_columns, row_share)], unit_layouts(True))
            (up_out,) = put(up_pieces, [(row_share, hidden_columns)], unit_layouts(False))
        else:
            joined_pieces, down_pieces, up_pieces = (
                pieces.astype(F32) for pieces in (joined_pieces, down_pieces, up_pieces)
            )
            joined_out = joined_pieces[:, :, :head_columns].transpose(1, 0, 2).reshape(row_share, -1)
            dense_out = joined_pieces[:, :, head_columns:].transpose(0, 2, 1).reshape(-1, row_share)
            up_out = up_pieces.reshape(branches, cores, row_share, chips, part)
            up_out = up_out.transpose(2, 3, 1, 0, 4).reshape(row_share, hidden_columns)
            down_out = down_pieces.reshape(branches, cores, row_share, chips, part)
            down_out = down_out.transpose(3, 1, 0, 4, 2).reshape(hidden_columns, row_share)
        w = width
        joined_end = 5 * w + joined_bias.shape[0]
        return (
            block_output.reshape(rows, length, span),
            input_gradient.reshape(rows, length, span),
            small[:w],
            small[w : 2 * w],
            joined_out,
            small[5 * w : joined_end],
            dense_out,
            small[4 * w : 5 * w],
            small[2 * w : 3 * w],
            small[3 * w : 4 * w],
            up_out,
            small[joined_end:],
            down_out,
            small[4 * w : 5 * w],
        )

    data = ("z", "core")
    everything = ("branch", "z", "core")
    in_specs = (
        P(data, None, None),
        P(data, None, ("branch", "mp")),
        P(data, None),
        P(),
        P(),
        P(data, "mp"),
        P(),
        P(("mp", "z", "core"), None),
        P(),
        P(),
        P(),
        P(data, "mp"),
        P(),
        P(("mp", "z", "core"), None),
        P(),
    )
    out_specs = (
        P(data, None, ("branch", "mp")),
        P(data, None, ("branch", "mp")),
        P(),
        P(),
        P(everything, "mp"),
        P(),
        P("mp", everything),
        P(),
        P(),
        P(),
        P(everything, "mp"),
        P(),
        P("mp", everything),
        P(),
    )
    return jax.shard_map(
        on_device, mesh=fine, in_specs=in_specs, out_specs=out_specs, check_vma=False
    )
```

```python
import functools
import math

import jax
import jax.numpy as jnp
from jax import lax
from jax.experimental import pallas as pl
from jax.experimental.pallas import tpu as pltpu
from jax.sharding import Mesh, PartitionSpec as P

HEAD = 256
ROT = 64
LANES = 128
NEGATIVE = -1e30
VMEM_BYTES = 56 * 1024 * 1024
F32 = jnp.float32
BF16 = jnp.bfloat16


def rotary_tables(segment_rows):
    length = segment_rows.shape[1]
    before = jnp.sum(
        (segment_rows[:, None, :] < segment_rows[:, :, None]).astype(jnp.int32), axis=2
    )
    places = (jnp.arange(length, dtype=jnp.int32)[None] - before).astype(F32)
    frequency = 10000.0 ** (-jnp.arange(0, ROT, 2).astype(F32) / ROT)
    angles = (places[:, :, None] * frequency).reshape(-1, ROT // 2)
    cosine, sine = jnp.cos(angles), jnp.sin(angles)
    none = jnp.zeros_like(sine)
    rest = jnp.zeros((angles.shape[0], LANES - ROT), F32)
    return (
        jnp.concatenate([cosine, cosine, rest + 1.0], axis=1),
        jnp.concatenate([-sine, none, rest], axis=1),
        jnp.concatenate([none, sine, rest], axis=1),
    )


def rotate(values, self_factor, right_factor, left_factor):
    half = ROT // 2
    front = values[:, :LANES]
    turned = (
        front * self_factor
        + pltpu.roll(front, LANES - half, 1) * right_factor
        + pltpu.roll(front, half, 1) * left_factor
    )
    return jnp.concatenate([turned, values[:, LANES:]], axis=1)


def dot(left, right, left_dim, right_dim):
    return lax.dot_general(
        left, right, (((left_dim,), (right_dim,)), ((), ())), preferred_element_type=F32
    )


def whole(shape):
    return pl.BlockSpec(shape, lambda i: (0,) * len(shape), pipeline_mode=pl.Buffered(1))


def tile(rows, columns):
    return pl.BlockSpec((rows, columns), lambda i: (i, 0))


def run(body, steps, ins, outs, args, flops, transcendentals=0):
    scratch = []
    if any(isinstance(arg, Line) for arg in args):
        body, ins, args, scratch = put_together(body, ins, args)
    shapes = [jax.ShapeDtypeStruct(shape, dtype) for _, shape, dtype in outs]
    moved = sum(a.size * a.dtype.itemsize for a in list(args) + shapes)
    return pl.pallas_call(
        body,
        grid=(steps,),
        in_specs=ins,
        out_specs=[spec for spec, _, _ in outs],
        out_shape=shapes,
        scratch_shapes=scratch,
        cost_estimate=pl.CostEstimate(
            flops=flops // 64, bytes_accessed=moved // 64, transcendentals=transcendentals // 64
        ),
        compiler_params=pltpu.CompilerParams(vmem_limit_bytes=VMEM_BYTES),
    )(*args)


def put_together(body, ins, args):
    new_ins, new_args, places, scratch = [], [], [], []
    for spec, arg in zip(ins, args):
        if not isinstance(arg, Line):
            new_ins.append(spec)
            new_args.append(arg)
            places.append(None)
        elif arg.full is not None:
            new_ins.append(spec)
            new_args.append(arg.full)
            places.append(None)
        else:
            slots = arg.slots()
            rows, columns = slots[0].shape
            new_ins += [pl.BlockSpec(memory_space=pl.ANY)] * len(slots)
            new_args += slots
            places.append((len(slots), rows, arg.count))
            scratch += [
                pltpu.VMEM((arg.count * rows, columns), slots[0].dtype),
                pltpu.SemaphoreType.DMA((arg.count,)),
            ]
            index = arg.index
    if not scratch:
        return body, new_ins, new_args, []

    def whole_body(index_ref, *refs):
        kept, held = refs[: len(refs) - len(scratch)], refs[len(refs) - len(scratch) :]
        inner, lines, at = [], [], 0
        for place in places:
            if place is None:
                inner.append(kept[at])
                at += 1
            else:
                full_ref, sems = held[2 * len(lines) : 2 * len(lines) + 2]
                lines.append((kept[at : at + place[0]], full_ref, sems, place))
                inner.append(full_ref)
                at += place[0]

        @pl.when(pl.program_id(0) == 0)
        def _():
            for blocks, full_ref, sems, (_, rows, count) in lines:
                for j in range(count):
                    for k, block in enumerate(blocks):

                        @pl.when(count - 1 - index_ref[0] + j == k)
                        def _():
                            pltpu.make_async_copy(
                                block, full_ref.at[pl.ds(j * rows, rows)], sems.at[j]
                            ).start()

            for blocks, full_ref, sems, (_, rows, count) in lines:
                for j in range(count):
                    pltpu.make_async_copy(
                        blocks[0], full_ref.at[pl.ds(j * rows, rows)], sems.at[j]
                    ).wait()

        body(*inner, *kept[at:])

    return (
        whole_body,
        [pl.BlockSpec(memory_space=pltpu.SMEM)] + new_ins,
        [index.reshape(1)] + new_args,
        scratch,
    )


def statistics(x):
    mean = jnp.mean(x, axis=-1, keepdims=True)
    center = x - mean
    inverse = lax.rsqrt(jnp.mean(center * center, axis=-1, keepdims=True) + 1e-05)
    return center * inverse, mean, inverse


def either(steps, mine_ref, other_ref):
    return jnp.where(pl.program_id(0) < steps, mine_ref[...], other_ref[...])


def halves(rows, columns, steps):
    return [
        pl.BlockSpec((rows, columns), lambda i: (jnp.minimum(i, steps - 1), 0)),
        pl.BlockSpec((rows, columns), lambda i: (jnp.maximum(i - steps, 0), 0)),
    ]


def norm_body(steps, mine_ref, other_ref, gain_a, shift_a, gain_e, shift_e, normed_ref, expanded_ref, stats_ref):
    hat, mean, inverse = statistics(either(steps, mine_ref, other_ref).astype(F32))
    lane = lax.broadcasted_iota(jnp.int32, stats_ref.shape, 1)
    stats_ref[...] = jnp.where(lane == 0, mean, inverse)
    normed_ref[...] = (hat * gain_a[...] + shift_a[...]).astype(BF16)
    expanded_ref[...] = (hat * gain_e[...] + shift_e[...]).astype(BF16)


def gather_body(steps, starts_ref, *refs):
    pieces, out_ref = refs[:-1], refs[-1]
    span = pieces[0].shape[1]
    for k in range(len(pieces) // 2):
        columns = pl.ds(pl.multiple_of(starts_ref[k], span), span)
        out_ref[:, columns] = either(steps, pieces[2 * k], pieces[2 * k + 1])


def accumulate(ref, value):
    @pl.when(pl.program_id(0) == 0)
    def _():
        ref[...] = value

    @pl.when(pl.program_id(0) != 0)
    def _():
        ref[...] += value


def attention_body(
    normed_ref, joined_ref, bias_ref, self_ref, right_ref, left_ref, column_ref, row_ref, g_ref, dense_ref,
    mixed_ref, grad_ref, bias_grad_ref,
):
    length = normed_ref.shape[0]
    scale = 1.0 / math.sqrt(HEAD)
    factors = self_ref[...], right_ref[...], left_ref[...]
    raw = dot(normed_ref[...], joined_ref[...], 1, 0) + bias_ref[...]
    queries = (rotate(raw[:, :HEAD], *factors) * scale).astype(BF16)
    keyset = rotate(raw[:, HEAD : 2 * HEAD], *factors).astype(BF16)
    valueset = raw[:, 2 * HEAD :].astype(BF16)
    query_index = lax.broadcasted_iota(jnp.int32, (length, length), 0)
    key_index = lax.broadcasted_iota(jnp.int32, (length, length), 1)
    allowed = (column_ref[0] == row_ref[0]) & (key_index <= query_index)
    scores = jnp.where(allowed, dot(queries, keyset, 1, 1), NEGATIVE)
    shifted = jnp.exp(scores - jnp.max(scores, axis=-1, keepdims=True))
    probs = shifted / jnp.sum(shifted, axis=-1, keepdims=True)
    low = probs.astype(BF16)
    mixed_ref[...] = dot(low, valueset, 1, 0).astype(BF16)
    mixed_grad = dot(g_ref[...], dense_ref[...], 1, 1).astype(BF16)
    probs_grad = dot(mixed_grad, valueset, 1, 1)
    value_grad = dot(low, mixed_grad, 0, 0)
    inner = jnp.sum(probs_grad * probs, axis=-1, keepdims=True)
    score_grad = (probs * (probs_grad - inner)).astype(BF16)
    query_grad = rotate(dot(score_grad, keyset, 1, 0) * scale, *back_factors(factors))
    key_grad = rotate(dot(score_grad, queries, 0, 0), *back_factors(factors))
    joined_grad = jnp.concatenate([query_grad, key_grad, value_grad], axis=1).astype(BF16)
    grad_ref[...] = joined_grad
    accumulate(bias_grad_ref, jnp.sum(joined_grad.astype(F32), axis=0, keepdims=True))


def back_factors(factors):
    return factors[0], -factors[1], -factors[2]


def hidden_body(expanded_ref, up_ref, bias_ref, activated_ref, slope_ref):
    block = up_ref.shape[1] // 4
    for k in range(4):
        columns = pl.ds(k * block, block)
        hidden = dot(expanded_ref[...], up_ref[:, columns], 1, 0) + bias_ref[:, columns]
        below = 0.5 * (1.0 + lax.erf(hidden * math.sqrt(0.5)))
        density = jnp.exp(hidden * hidden * -0.5) * (1.0 / math.sqrt(2.0 * math.pi))
        activated_ref[:, columns] = (hidden * below).astype(BF16)
        slope_ref[:, columns] = (below + hidden * density).astype(BF16)


def terms_body(*refs):
    out_ref, start = refs[-1], 0
    for left_ref, right_ref in zip(refs[:-1:2], refs[1:-1:2]):
        stop = start + right_ref.shape[1]
        term = dot(left_ref[...], right_ref[...], 0, 0).astype(BF16)
        out_ref[:, :, :, start:stop] = term.reshape(*out_ref.shape[:3], stop - start)
        start = stop


def hidden_grad_body(g_ref, down_ref, slope_ref, grad_ref, bias_grad_ref):
    grad = dot(g_ref[...], down_ref[...], 1, 1) * slope_ref[...].astype(F32)
    grad = grad.astype(BF16)
    grad_ref[...] = grad
    accumulate(bias_grad_ref, jnp.sum(grad.astype(F32), axis=0, keepdims=True))


def store_blocks(out_ref, values, got_refs):
    blocks, span = out_ref.shape[1], out_ref.shape[3]
    for k in range(blocks):
        block = values[:, k * span : (k + 1) * span]
        for got_ref in got_refs:
            block = block + got_ref[0, k].astype(F32)
        out_ref[0, k] = block.astype(BF16)


def forward_body(mixed_ref, dense_ref, active_ref, down_ref, *refs):
    total = dot(mixed_ref[...], dense_ref[...], 1, 0)
    total += dot(active_ref[...], down_ref[...], 1, 0)
    store_blocks(refs[-1], total, refs[:-1])


def input_body(
    x_ref, stats_ref, joined_grad_ref, joined_ref, hidden_grad_ref, up_ref, gain_a, gain_e, *refs
):
    got_refs, (out_ref, sums_ref) = refs[:-2], refs[-2:]
    normed_grad = dot(joined_grad_ref[...], joined_ref[...], 1, 1)
    expanded_grad = dot(hidden_grad_ref[...], up_ref[...], 1, 1)
    mean, inverse = stats_ref[:, 0:1], stats_ref[:, 1:2]
    hat = (x_ref[...].astype(F32) - mean) * inverse
    weighted = normed_grad * gain_a[...] + expanded_grad * gain_e[...]
    weighted_mean = jnp.mean(weighted, axis=-1, keepdims=True)
    along = jnp.mean(weighted * hat, axis=-1, keepdims=True)
    store_blocks(out_ref, inverse * (weighted - weighted_mean - hat * along), got_refs)

    def down(values):
        return jnp.sum(values, axis=0, keepdims=True)

    sums = jnp.concatenate(
        [down(normed_grad * hat), down(normed_grad), down(expanded_grad * hat), down(expanded_grad)]
    )
    accumulate(sums_ref, sums)


def place_body(layouts, pieces_ref, *outs):
    for device in range(pieces_ref.shape[0]):
        for start, size, target, where, turned in layouts:
            offset = where(device) * size
            values = pieces_ref[device, :, start : start + size].astype(F32)
            if turned:
                outs[target][offset : offset + size, :] = values.T
            else:
                outs[target][:, offset : offset + size] = values


def pick(array, index, axis):
    return lax.dynamic_index_in_dim(array, index, axis, keepdims=False)


def add_low(left, right):
    return (left.astype(F32) + right.astype(F32)).astype(BF16)


SWAP = [(0, 1), (1, 0)]


class Chain:
    def __init__(self, view, index, count):
        self.view, self.index, self.count, self.step = view, index, count, 0
        self.held = self.flight = ()
        self.out = []

    def term(self, share):
        return pick(self.view, jnp.clip(share, 0, self.count - 1), 0)

    def prepare(self):
        if self.step == self.count - 1:
            return
        self.step += 1
        step, count = self.step, self.count
        self.out = [self.term(self.index + count - step), self.term(self.index - count + step)]
        if self.held:
            self.out = [add_low(one, two) for one, two in zip(self.out, self.held)]

    def send(self):
        if not self.out:
            self.prepare()
        if not self.out:
            return
        step, count = self.step, self.count
        self.flight = (
            lax.ppermute(self.out[0], "z", [(i, i + 1) for i in range(step)]),
            lax.ppermute(self.out[1], "z", [(count - 1 - i, count - 2 - i) for i in range(step)]),
        )
        self.out = []

    def land(self, values):
        if values:
            self.held, self.flight = values, ()

    def total(self):
        own = self.term(self.index).astype(F32)
        return (own + self.held[0].astype(F32) + self.held[1].astype(F32)).astype(BF16)


class Line:
    def __init__(self, piece, index, count):
        self.index, self.count, self.step, self.flight = index, count, 0, ()
        self.from_left, self.from_right, self.own, self.full = [], [], piece, None
        if count > 4:
            self.full = lax.all_gather(piece, "z", axis=0, tiled=True)

    def send(self):
        if self.full is not None or self.step == self.count - 1:
            return
        step, count = self.step, self.count
        right, left = (self.from_left[-1], self.from_right[-1]) if step else (self.own, self.own)
        self.flight = (
            lax.ppermute(right, "z", [(i, i + 1) for i in range(step, count - 1)]),
            lax.ppermute(left, "z", [(i + 1, i) for i in range(count - 1 - step)]),
        )
        self.step += 1

    def land(self, values):
        if values:
            self.from_left.append(values[0])
            self.from_right.append(values[1])
            self.flight = ()

    def slots(self):
        return [*self.from_left[::-1], self.own, *self.from_right]


fence = lax.optimization_barrier


def solution(mesh):
    branches, models, datas = (mesh.shape[name] for name in ("branch", "mp", "dp"))
    cores = 2
    chips = datas // cores
    fine = Mesh(
        mesh.devices.reshape(branches, models, chips, cores), ("branch", "mp", "z", "core")
    )

    def on_device(
        block_input,
        cotangent,
        segments,
        attend_gain,
        attend_shift,
        joined_weight,
        joined_bias,
        dense_weight,
        dense_bias,
        expand_gain,
        expand_shift,
        up_weight,
        up_bias,
        down_weight,
        down_bias,
    ):
        rows, length, width = block_input.shape
        b, m, z, c = (lax.axis_index(name) for name in ("branch", "mp", "z", "core"))
        tokens = rows * length
        span = width // (branches * models)
        column_start = (b * models + m) * span
        heads = branches * cores
        head_columns = joined_weight.shape[1] // heads
        hidden_columns = up_weight.shape[1]
        part = down_weight.shape[0] // branches
        units = chips * part
        head_slot = b * cores + c
        row_share = width // (branches * datas)

        def partner(array, **flips):
            names = tuple(name for name, flip in flips.items() if flip)
            if not names:
                return array
            count = 2 ** len(names)
            return lax.ppermute(array, names, [(i, count - 1 - i) for i in range(count)])

        def swap_core(array):
            return partner(array, core=1)

        def in_core_order(mine, other):
            return jnp.where(c == 0, jnp.concatenate([mine, other]), jnp.concatenate([other, mine]))

        def columns_of(array, start, size):
            return lax.dynamic_slice_in_dim(array, start, size, array.ndim - 1)

        def unit_columns(array, core):
            return jnp.concatenate(
                [
                    columns_of(array, ((k * cores + core) * branches + b) * part, part)
                    for k in range(chips)
                ],
                axis=-1,
            )

        def gather(piece):
            return lax.all_gather(piece, "z", axis=0, tiled=True)

        x_own = block_input.reshape(tokens, width)
        g_piece = cotangent.reshape(tokens, span)
        joined_piece = in_core_order(
            columns_of(joined_weight, head_slot * head_columns, head_columns),
            swap_core(columns_of(joined_weight, (b * cores + 1 - c) * head_columns, head_columns)),
        )
        flips = [(db, dm) for db in range(2) for dm in range(2)]
        g_mine = [partner(g_piece, branch=db, mp=dm) for db, dm in flips]
        x_other = swap_core(x_own)
        segment_rows = jnp.concatenate([segments, swap_core(segments)])
        joined_piece, dense_weight = fence((joined_piece, dense_weight))
        spread_dense = chips == heads and HEAD == cores * dense_weight.shape[0]
        if spread_dense:
            few = HEAD // chips
            per_core = chips // cores
            dense_piece = 0
            for j in range(per_core):
                moves = [
                    (
                        (one * chips + one * cores + to) * cores + at,
                        (one * chips + at * per_core + j) * cores + to,
                    )
                    for one in range(branches)
                    for to in range(cores)
                    for at in range(cores)
                ]
                dense_piece = dense_piece + lax.ppermute(
                    dense_weight[j * few : (j + 1) * few], ("branch", "z", "core"), moves
                )
        else:
            dense_piece = dense_weight

        joined_bias_here = columns_of(joined_bias, (m * heads + head_slot) * head_columns, head_columns)
        up_bias_here = unit_columns(columns_of(up_bias, m * hidden_columns, hidden_columns), c)
        down_piece = lax.dynamic_slice_in_dim(down_weight, b * part, part, 0)

        def flat(vector):
            return vector.reshape(1, -1)

        all_tokens = 2 * tokens
        gains = flat(attend_gain), flat(expand_gain)
        small_tile = min(256, length)
        half_steps = tokens // small_tile
        joined_full = gather(joined_piece)
        x_other, joined_piece, up_weight, dense_piece = fence(
            (x_other, joined_piece, up_weight, dense_piece)
        )
        if spread_dense:
            dense_full = gather(dense_piece)
        else:
            dense_full = lax.all_gather(dense_piece, ("z", "core"), axis=0, tiled=True)
            dense_full = lax.dynamic_slice_in_dim(dense_full, head_slot * HEAD, HEAD, 0)
        up_piece = in_core_order(unit_columns(up_weight, c), swap_core(unit_columns(up_weight, 1 - c)))
        normed, expanded, stats = run(
            functools.partial(norm_body, half_steps),
            2 * half_steps,
            halves(small_tile, width, half_steps) + [whole((1, width))] * 4,
            [(tile(small_tile, width), (all_tokens, width), BF16)] * 2
            + [(tile(small_tile, LANES), (all_tokens, LANES), F32)],
            (x_own, x_other, gains[0], flat(attend_shift), gains[1], flat(expand_shift)),
            20 * all_tokens * width,
        )
        rotary = rotary_tables(segment_rows)
        normed, expanded, rotary, g_mine, up_piece, down_piece = fence(
            (normed, expanded, rotary, g_mine, up_piece, down_piece)
        )
        up_line = Line(up_piece, z, chips)
        up_line.send()
        g_other = [swap_core(piece) for piece in g_mine]
        starts = jnp.stack([((b ^ db) * models + (m ^ dm)) * span for db, dm in flips])
        (g,) = run(
            functools.partial(gather_body, half_steps),
            2 * half_steps,
            [pl.BlockSpec(memory_space=pltpu.SMEM)]
            + [spec for _ in flips for spec in halves(small_tile, span, half_steps)],
            [(tile(small_tile, width), (all_tokens, width), BF16)],
            (starts, *[piece for pair in zip(g_mine, g_other) for piece in pair]),
            all_tokens * width,
        )
        up_line.flight, g, down_piece, joined_full, dense_full = fence(
            (up_line.flight, g, down_piece, joined_full, dense_full)
        )
        up_line.land(up_line.flight)
        up_line.send()

        all_rows = 2 * rows
        mixed, joined_grad, joined_bias_grad = run(
            attention_body,
            all_rows,
            [
                tile(length, width),
                whole((width, head_columns)),
                whole((1, head_columns)),
                tile(length, LANES),
                tile(length, LANES),
                tile(length, LANES),
                pl.BlockSpec((1, length, 1), lambda i: (i, 0, 0)),
                pl.BlockSpec((1, 1, length), lambda i: (i, 0, 0)),
                tile(length, width),
                whole((HEAD, width)),
            ],
            [
                (tile(length, HEAD), (all_tokens, HEAD), BF16),
                (tile(length, head_columns), (all_tokens, head_columns), BF16),
                (whole((1, head_columns)), (1, head_columns), F32),
            ],
            (
                normed,
                joined_full,
                flat(joined_bias_here),
                *rotary,
                segment_rows[:, :, None],
                segment_rows[:, None, :],
                g,
                dense_full,
            ),
            2 * all_tokens * (width * (head_columns + HEAD) + 7 * length * HEAD),
            all_tokens * length,
        )

        live = dict(
            mixed=mixed, joined_grad=joined_grad, normed=normed, expanded=expanded, g=g, down=down_piece
        )

        def step(*landing, hold=()):
            fresh, held, views, outs, kept = fence(
                (
                    dict(live),
                    [chain.flight for chain in landing],
                    [chain.view for chain in waiting],
                    [chain.out for chain in chains],
                    [chain.held for chain in hold],
                )
            )
            for chain, one in zip(hold, kept):
                chain.held = one
            for chain, out in zip(chains, outs):
                chain.out = out
            live.update(fresh)
            for chain, one in zip(landing, held):
                chain.land(one)
            for chain, view in zip(waiting, views):
                chain.view = view
            waiting.clear()

        waiting, chains = [], []
        share_rows = cores * row_share

        def terms(*pairs):
            rows_tile = max(256, share_rows)
            group = rows_tile // share_rows
            groups = chips // group
            columns = sum(right.shape[1] for _, right in pairs)
            ins, args = [], []
            for left, right in pairs:
                ins += [pl.BlockSpec((all_tokens, rows_tile), lambda i: (0, i)), whole(right.shape)]
                args += [left, right]
            (view,) = run(
                terms_body,
                branches * groups,
                ins,
                [
                    (
                        pl.BlockSpec(
                            (group, 1, share_rows, columns), lambda i: (i % groups, i // groups, 0, 0)
                        ),
                        (chips, branches, share_rows, columns),
                        BF16,
                    )
                ],
                args,
                2 * all_tokens * width * columns,
            )
            chain = Chain(view, z, chips)
            waiting.append(chain)
            chains.append(chain)
            return chain

        def spread(chain):
            share = chain.total().reshape(branches * cores * row_share, -1)
            pieces = lax.all_to_all(share, ("branch", "core"), 0, 0, tiled=True)
            return pieces.reshape(branches * cores, row_share, -1)

        unit_flops = 2 * all_tokens * width * units
        big_tile = min(512, length)

        def hidden_values():
            return run(
                hidden_body,
                all_tokens // big_tile,
                [tile(big_tile, width), whole((width, units)), whole((1, units))],
                [(tile(big_tile, units), (all_tokens, units), BF16)] * 2,
                (live["expanded"], up_line, flat(up_bias_here)),
                unit_flops,
                2 * all_tokens * units,
            )

        def hidden_gradient():
            return run(
                hidden_grad_body,
                all_tokens // big_tile,
                [tile(big_tile, width), whole((units, width)), tile(big_tile, units)],
                [
                    (tile(big_tile, units), (all_tokens, units), BF16),
                    (whole((1, units)), (1, units), F32),
                ],
                (live["g"], down_line, live.pop("slope")),
                unit_flops,
            )

        blocks = branches * models

        def of_core(core, columns):
            return pl.BlockSpec((small_tile, columns), lambda i: (core * half_steps + i, 0))

        def out_blocks(pieces):
            steps = half_steps // pieces
            return (
                pl.BlockSpec((1, blocks, small_tile, span), lambda i: (i // steps, 0, i % steps, 0)),
                (pieces, blocks, tokens // pieces, span),
                BF16,
            )

        def input_terms(core, *got):
            return run(
                input_body,
                half_steps,
                [
                    tile(small_tile, width),
                    of_core(core, LANES),
                    of_core(core, head_columns),
                    whole((width, head_columns)),
                    of_core(core, units),
                    whole((width, units)),
                    whole((1, width)),
                    whole((1, width)),
                    *[out_blocks(2)[0]] * len(got),
                ],
                [out_blocks(2), (whole((4, width)), (4, width), F32)],
                (
                    (x_own, x_other)[core],
                    stats,
                    live["joined_grad"],
                    joined_full,
                    live["grad"],
                    up_line,
                    *gains,
                    *got,
                ),
                unit_flops // 2 + all_tokens * width * head_columns,
            )

        def forward_terms(core, *got):
            return run(
                forward_body,
                half_steps,
                [
                    of_core(core, HEAD),
                    whole((HEAD, width)),
                    of_core(core, units),
                    whole((units, width)),
                    *[out_blocks(1)[0]] * len(got),
                ],
                [out_blocks(1)],
                (live["mixed"], dense_full, live["active"], down_line, *got),
                unit_flops // 2 + all_tokens * width * HEAD,
            )[0]

        def block_sum(blocks):
            return lax.psum_scatter(blocks[0], ("branch", "mp"), scatter_dimension=0, tiled=True)[0]

        def first_sends(term):
            one, two = (term[h].reshape(branches, models, tokens // 2, span) for h in range(2))
            return partner(pick(one, 1 - b, 0), branch=1), partner(pick(two, 1 - m, 1), mp=1)

        def first_sum(term, got):
            one, two = (term[h].reshape(branches, models, tokens // 2, span) for h in range(2))
            return add_low(pick(one, b, 0), got[0]), add_low(pick(two, m, 1), got[1])

        def second_sends(pair):
            one, two = pair
            return partner(pick(one, 1 - m, 0), mp=1), partner(pick(two, 1 - b, 0), branch=1)

        def second_sum(pair, got):
            one, two = pair
            return jnp.concatenate(
                [
                    pick(one, m, 0).astype(F32) + got[0].astype(F32),
                    pick(two, b, 0).astype(F32) + got[1].astype(F32),
                ]
            )

        def put(pieces, shapes, layouts):
            return run(
                functools.partial(place_body, layouts),
                1,
                [whole(pieces.shape)],
                [(whole(shape), shape, F32) for shape in shapes],
                [pieces],
                0,
            )

        def unit_layouts(turned):
            return [
                (
                    k * part,
                    part,
                    0,
                    lambda device, k=k: (k * cores + device % cores) * branches + device // cores,
                    turned,
                )
                for k in range(chips)
            ]

        simple = part % LANES != 0 or row_share % 8 != 0

        def place_joined(pieces):
            if simple:
                pieces = pieces.astype(F32)
                joined = pieces[:, :, :head_columns].transpose(1, 0, 2).reshape(row_share, -1)
                return joined, pieces[:, :, head_columns:].transpose(0, 2, 1).reshape(-1, row_share)
            return put(
                pieces,
                [(row_share, heads * head_columns), (heads * HEAD, row_share)],
                [
                    (0, head_columns, 0, lambda device: device, False),
                    (head_columns, HEAD, 1, lambda device: device, True),
                ],
            )

        def place_units(pieces, turned):
            if not simple:
                shape = (hidden_columns, row_share) if turned else (row_share, hidden_columns)
                return put(pieces, [shape], unit_layouts(turned))[0]
            pieces = pieces.astype(F32).reshape(branches, cores, row_share, chips, part)
            if turned:
                return pieces.transpose(3, 1, 0, 4, 2).reshape(hidden_columns, row_share)
            return pieces.transpose(2, 3, 1, 0, 4).reshape(row_share, hidden_columns)

        def finish(chain):
            while chain.step < chips - 1:
                chain.send()
                step(chain)
            return spread(chain)

        step(up_line)
        up_line.send()
        joined_chain = terms((live.pop("normed"), live["joined_grad"]), (live["g"], live["mixed"]))
        joined_chain.send()
        step(up_line)
        down_line = Line(live.pop("down"), z, chips)
        down_line.send()
        live["active"], live["slope"] = hidden_values()
        down_chain = terms((live["g"], live["active"]))
        down_chain.prepare()
        step(down_line, joined_chain)
        down_line.send()
        down_chain.send()
        joined_chain.prepare()
        g_float = g_piece.astype(F32)
        out_slot = lax.dynamic_update_slice(
            jnp.zeros((width,), F32), jnp.sum(g_float, axis=0), (column_start,)
        )
        joined_slot = lax.dynamic_update_slice(
            jnp.zeros_like(joined_bias),
            joined_bias_grad.reshape(-1),
            ((m * heads + head_slot) * head_columns,),
        )
        live["slots"] = jnp.concatenate([out_slot, joined_slot])
        step(down_line, down_chain)
        down_line.send()
        joined_chain.send()
        down_chain.prepare()
        step(down_line, joined_chain)
        joined_chain.send()
        live["out_other"] = forward_terms(1)
        live["grad"], live["bias"] = hidden_gradient()
        step(joined_chain)
        down_chain.send()
        live["out_got"] = swap_core(live.pop("out_other"))
        live["joined_pieces"] = finish(joined_chain)
        up_chain = terms((live.pop("expanded"), live["grad"]))
        live.pop("g")
        up_chain.prepare()
        live["out"] = forward_terms(0, live.pop("out_got"))
        step(down_chain)
        forward_sum = block_sum(live.pop("out"))
        up_chain.send()
        down_chain.prepare()
        live["in_other"], live["sums_other"] = input_terms(1)
        step(up_chain)
        live["forward_sum"] = forward_sum
        down_chain.send()
        live["in_got"] = swap_core(live.pop("in_other"))
        up_chain.prepare()
        live["in"], live["sums_own"] = input_terms(0, live.pop("in_got"))
        up_slot = lax.dynamic_update_slice(
            jnp.zeros((models, chips, cores, branches, part), F32),
            live.pop("bias").reshape(1, chips, 1, 1, part),
            (m, 0, c, b, 0),
        ).reshape(-1)
        live["slots"] = jnp.concatenate([live["slots"], up_slot])
        step(down_chain)
        up_chain.send()
        live["in_got"] = first_sends(live["in"])
        sums = live.pop("sums_own") + live.pop("sums_other")
        small = jnp.concatenate([sums.reshape(-1), live.pop("slots")])
        small = (
            small
            + partner(small, core=1)
            + partner(small, branch=1)
            + partner(small, branch=1, core=1)
        )
        live["joined_out"], live["dense_out"] = place_joined(live.pop("joined_pieces"))
        down_pieces = finish(down_chain)
        step(up_chain)
        up_chain.prepare()
        step()
        live["down_pieces"] = down_pieces
        up_chain.send()
        live["in"] = first_sum(live["in"], live.pop("in_got"))
        live["in_got"] = second_sends(live["in"])
        near = lax.ppermute(small, "z", [(i, i ^ 1) for i in range(chips)])
        far = [
            lax.ppermute(
                small,
                ("mp", "z"),
                [
                    (one * chips + i, (1 - one) * chips + (i ^ flip))
                    for one in range(models)
                    for i in range(chips)
                ],
            )
            for flip in range(2)
        ]
        live["small"] = small + near + far[0] + far[1]
        forward_sum = live["forward_sum"]
        residual = columns_of(x_own, column_start, span).astype(F32)
        column_bias = columns_of(dense_bias + down_bias, column_start, span)
        block_output = (residual + forward_sum + column_bias).astype(BF16)
        live["block_output"] = block_output
        step(up_chain)
        block_output = live["block_output"]
        up_pieces = finish(up_chain)
        small = live["small"]
        flip = 2
        while flip < chips:
            small = small + lax.ppermute(small, "z", [(i, i ^ flip) for i in range(chips)])
            flip *= 2
        input_sum = second_sum(live.pop("in"), live.pop("in_got"))
        joined_out, dense_out = live["joined_out"], live["dense_out"]
        down_out, up_out = place_units(live["down_pieces"], True), place_units(up_pieces, False)

        input_gradient = (g_float + input_sum).astype(BF16)

        w = width
        joined_end = 5 * w + joined_bias.shape[0]
        return (
            block_output.reshape(rows, length, span),
            input_gradient.reshape(rows, length, span),
            small[:w],
            small[w : 2 * w],
            joined_out,
            small[5 * w : joined_end],
            dense_out,
            small[4 * w : 5 * w],
            small[2 * w : 3 * w],
            small[3 * w : 4 * w],
            up_out,
            small[joined_end:],
            down_out,
            small[4 * w : 5 * w],
        )

    data = ("z", "core")
    everything = ("branch", "z", "core")
    in_specs = (
        P(data, None, None),
        P(data, None, ("branch", "mp")),
        P(data, None),
        P(),
        P(),
        P(data, "mp"),
        P(),
        P(("mp", "z", "core"), None),
        P(),
        P(),
        P(),
        P(data, "mp"),
        P(),
        P(("mp", "z", "core"), None),
        P(),
    )
    out_specs = (
        P(data, None, ("branch", "mp")),
        P(data, None, ("branch", "mp")),
        P(),
        P(),
        P(everything, "mp"),
        P(),
        P("mp", everything),
        P(),
        P(),
        P(),
        P(everything, "mp"),
        P(),
        P("mp", everything),
        P(),
    )
    return jax.shard_map(
        on_device, mesh=fine, in_specs=in_specs, out_specs=out_specs, check_vma=False
    )
```

```python
import functools
import math

import jax
import jax.numpy as jnp
from jax import lax
from jax.experimental import pallas as pl
from jax.experimental.pallas import tpu as pltpu
from jax.sharding import Mesh, PartitionSpec as P

HEAD = 256
ROT = 64
LANES = 128
NEGATIVE = -1e30
VMEM_BYTES = 56 * 1024 * 1024
F32 = jnp.float32
BF16 = jnp.bfloat16


def rotary_tables(segment_rows):
    length = segment_rows.shape[1]
    before = jnp.sum(
        (segment_rows[:, None, :] < segment_rows[:, :, None]).astype(jnp.int32), axis=2
    )
    places = (jnp.arange(length, dtype=jnp.int32)[None] - before).astype(F32)
    frequency = 10000.0 ** (-jnp.arange(0, ROT, 2).astype(F32) / ROT)
    angles = (places[:, :, None] * frequency).reshape(-1, ROT // 2)
    cosine, sine = jnp.cos(angles), jnp.sin(angles)
    none = jnp.zeros_like(sine)
    rest = jnp.zeros((angles.shape[0], LANES - ROT), F32)
    return (
        jnp.concatenate([cosine, cosine, rest + 1.0], axis=1),
        jnp.concatenate([-sine, none, rest], axis=1),
        jnp.concatenate([none, sine, rest], axis=1),
    )


def rotate(values, self_factor, right_factor, left_factor):
    half = ROT // 2
    front = values[:, :LANES]
    turned = (
        front * self_factor
        + pltpu.roll(front, LANES - half, 1) * right_factor
        + pltpu.roll(front, half, 1) * left_factor
    )
    return jnp.concatenate([turned, values[:, LANES:]], axis=1)


def dot(left, right, left_dim, right_dim):
    return lax.dot_general(
        left, right, (((left_dim,), (right_dim,)), ((), ())), preferred_element_type=F32
    )


def whole(shape):
    return pl.BlockSpec(shape, lambda i: (0,) * len(shape), pipeline_mode=pl.Buffered(1))


def tile(rows, columns):
    return pl.BlockSpec((rows, columns), lambda i: (i, 0))


def run(body, steps, ins, outs, args, flops, transcendentals=0):
    scratch = []
    if any(isinstance(arg, Line) for arg in args):
        body, ins, args, scratch = put_together(body, ins, args)
    shapes = [jax.ShapeDtypeStruct(shape, dtype) for _, shape, dtype in outs]
    moved = sum(a.size * a.dtype.itemsize for a in list(args) + shapes)
    return pl.pallas_call(
        body,
        grid=(steps,),
        in_specs=ins,
        out_specs=[spec for spec, _, _ in outs],
        out_shape=shapes,
        scratch_shapes=scratch,
        cost_estimate=pl.CostEstimate(
            flops=flops // 64, bytes_accessed=moved // 64, transcendentals=transcendentals // 64
        ),
        compiler_params=pltpu.CompilerParams(vmem_limit_bytes=VMEM_BYTES),
    )(*args)


def put_together(body, ins, args):
    new_ins, new_args, places, scratch = [], [], [], []
    for spec, arg in zip(ins, args):
        if not isinstance(arg, Line):
            new_ins.append(spec)
            new_args.append(arg)
            places.append(None)
        elif arg.full is not None:
            new_ins.append(spec)
            new_args.append(arg.full)
            places.append(None)
        else:
            slots = arg.slots()
            rows, columns = slots[0].shape
            new_ins += [pl.BlockSpec(memory_space=pl.ANY)] * len(slots)
            new_args += slots
            places.append((len(slots), rows, arg.count))
            scratch += [
                pltpu.VMEM((arg.count * rows, columns), slots[0].dtype),
                pltpu.SemaphoreType.DMA((arg.count,)),
            ]
            index = arg.index
    if not scratch:
        return body, new_ins, new_args, []

    def whole_body(index_ref, *refs):
        kept, held = refs[: len(refs) - len(scratch)], refs[len(refs) - len(scratch) :]
        inner, lines, at = [], [], 0
        for place in places:
            if place is None:
                inner.append(kept[at])
                at += 1
            else:
                full_ref, sems = held[2 * len(lines) : 2 * len(lines) + 2]
                lines.append((kept[at : at + place[0]], full_ref, sems, place))
                inner.append(full_ref)
                at += place[0]

        @pl.when(pl.program_id(0) == 0)
        def _():
            for blocks, full_ref, sems, (_, rows, count) in lines:
                for j in range(count):
                    for k, block in enumerate(blocks):

                        @pl.when(count - 1 - index_ref[0] + j == k)
                        def _():
                            pltpu.make_async_copy(
                                block, full_ref.at[pl.ds(j * rows, rows)], sems.at[j]
                            ).start()

            for blocks, full_ref, sems, (_, rows, count) in lines:
                for j in range(count):
                    pltpu.make_async_copy(
                        blocks[0], full_ref.at[pl.ds(j * rows, rows)], sems.at[j]
                    ).wait()

        body(*inner, *kept[at:])

    return (
        whole_body,
        [pl.BlockSpec(memory_space=pltpu.SMEM)] + new_ins,
        [index.reshape(1)] + new_args,
        scratch,
    )


def statistics(x):
    mean = jnp.mean(x, axis=-1, keepdims=True)
    center = x - mean
    inverse = lax.rsqrt(jnp.mean(center * center, axis=-1, keepdims=True) + 1e-05)
    return center * inverse, mean, inverse


def either(steps, mine_ref, other_ref):
    return jnp.where(pl.program_id(0) < steps, mine_ref[...], other_ref[...])


def halves(rows, columns, steps):
    return [
        pl.BlockSpec((rows, columns), lambda i: (jnp.minimum(i, steps - 1), 0)),
        pl.BlockSpec((rows, columns), lambda i: (jnp.maximum(i - steps, 0), 0)),
    ]


def norm_body(steps, mine_ref, other_ref, gain_a, shift_a, gain_e, shift_e, normed_ref, expanded_ref, stats_ref):
    hat, mean, inverse = statistics(either(steps, mine_ref, other_ref).astype(F32))
    lane = lax.broadcasted_iota(jnp.int32, stats_ref.shape, 1)
    stats_ref[...] = jnp.where(lane == 0, mean, inverse)
    normed_ref[...] = (hat * gain_a[...] + shift_a[...]).astype(BF16)
    expanded_ref[...] = (hat * gain_e[...] + shift_e[...]).astype(BF16)


def gather_body(steps, starts_ref, *refs):
    pieces, out_ref = refs[:-1], refs[-1]
    span = pieces[0].shape[1]
    for k in range(len(pieces) // 2):
        columns = pl.ds(pl.multiple_of(starts_ref[k], span), span)
        out_ref[:, columns] = either(steps, pieces[2 * k], pieces[2 * k + 1])


def accumulate(ref, value):
    @pl.when(pl.program_id(0) == 0)
    def _():
        ref[...] = value

    @pl.when(pl.program_id(0) != 0)
    def _():
        ref[...] += value


def attention_body(
    normed_ref, joined_ref, bias_ref, self_ref, right_ref, left_ref, column_ref, row_ref, g_ref, dense_ref,
    mixed_ref, grad_ref, bias_grad_ref,
):
    length = normed_ref.shape[0]
    scale = 1.0 / math.sqrt(HEAD)
    factors = self_ref[...], right_ref[...], left_ref[...]
    raw = dot(normed_ref[...], joined_ref[...], 1, 0) + bias_ref[...]
    queries = (rotate(raw[:, :HEAD], *factors) * scale).astype(BF16)
    keyset = rotate(raw[:, HEAD : 2 * HEAD], *factors).astype(BF16)
    valueset = raw[:, 2 * HEAD :].astype(BF16)
    query_index = lax.broadcasted_iota(jnp.int32, (length, length), 0)
    key_index = lax.broadcasted_iota(jnp.int32, (length, length), 1)
    allowed = (column_ref[0] == row_ref[0]) & (key_index <= query_index)
    scores = jnp.where(allowed, dot(queries, keyset, 1, 1), NEGATIVE)
    shifted = jnp.exp(scores - jnp.max(scores, axis=-1, keepdims=True))
    probs = shifted / jnp.sum(shifted, axis=-1, keepdims=True)
    low = probs.astype(BF16)
    mixed_ref[...] = dot(low, valueset, 1, 0).astype(BF16)
    mixed_grad = dot(g_ref[...], dense_ref[...], 1, 1).astype(BF16)
    probs_grad = dot(mixed_grad, valueset, 1, 1)
    value_grad = dot(low, mixed_grad, 0, 0)
    inner = jnp.sum(probs_grad * probs, axis=-1, keepdims=True)
    score_grad = (probs * (probs_grad - inner)).astype(BF16)
    query_grad = rotate(dot(score_grad, keyset, 1, 0) * scale, *back_factors(factors))
    key_grad = rotate(dot(score_grad, queries, 0, 0), *back_factors(factors))
    joined_grad = jnp.concatenate([query_grad, key_grad, value_grad], axis=1).astype(BF16)
    grad_ref[...] = joined_grad
    accumulate(bias_grad_ref, jnp.sum(joined_grad.astype(F32), axis=0, keepdims=True))


def back_factors(factors):
    return factors[0], -factors[1], -factors[2]


def hidden_body(expanded_ref, up_ref, bias_ref, activated_ref, slope_ref):
    block = up_ref.shape[1] // 4
    for k in range(4):
        columns = pl.ds(k * block, block)
        hidden = dot(expanded_ref[...], up_ref[:, columns], 1, 0) + bias_ref[:, columns]
        below = 0.5 * (1.0 + lax.erf(hidden * math.sqrt(0.5)))
        density = jnp.exp(hidden * hidden * -0.5) * (1.0 / math.sqrt(2.0 * math.pi))
        activated_ref[:, columns] = (hidden * below).astype(BF16)
        slope_ref[:, columns] = (below + hidden * density).astype(BF16)


def terms_body(*refs):
    out_ref, start = refs[-1], 0
    for left_ref, right_ref in zip(refs[:-1:2], refs[1:-1:2]):
        stop = start + right_ref.shape[1]
        term = dot(left_ref[...], right_ref[...], 0, 0).astype(BF16)
        out_ref[:, :, :, start:stop] = term.reshape(*out_ref.shape[:3], stop - start)
        start = stop


def hidden_grad_body(g_ref, down_ref, slope_ref, grad_ref, bias_grad_ref):
    grad = dot(g_ref[...], down_ref[...], 1, 1) * slope_ref[...].astype(F32)
    grad = grad.astype(BF16)
    grad_ref[...] = grad
    accumulate(bias_grad_ref, jnp.sum(grad.astype(F32), axis=0, keepdims=True))


def store_blocks(out_ref, values, got_refs):
    blocks, span = out_ref.shape[1], out_ref.shape[3]
    for k in range(blocks):
        block = values[:, k * span : (k + 1) * span]
        for got_ref in got_refs:
            block = block + got_ref[0, k].astype(F32)
        out_ref[0, k] = block.astype(BF16)


def forward_body(mixed_ref, dense_ref, active_ref, down_ref, *refs):
    total = dot(mixed_ref[...], dense_ref[...], 1, 0)
    total += dot(active_ref[...], down_ref[...], 1, 0)
    store_blocks(refs[-1], total, refs[:-1])


def input_body(
    x_ref, stats_ref, joined_grad_ref, joined_ref, hidden_grad_ref, up_ref, gain_a, gain_e, *refs
):
    got_refs, (out_ref, sums_ref) = refs[:-2], refs[-2:]
    normed_grad = dot(joined_grad_ref[...], joined_ref[...], 1, 1)
    expanded_grad = dot(hidden_grad_ref[...], up_ref[...], 1, 1)
    mean, inverse = stats_ref[:, 0:1], stats_ref[:, 1:2]
    hat = (x_ref[...].astype(F32) - mean) * inverse
    weighted = normed_grad * gain_a[...] + expanded_grad * gain_e[...]
    weighted_mean = jnp.mean(weighted, axis=-1, keepdims=True)
    along = jnp.mean(weighted * hat, axis=-1, keepdims=True)
    store_blocks(out_ref, inverse * (weighted - weighted_mean - hat * along), got_refs)

    def down(values):
        return jnp.sum(values, axis=0, keepdims=True)

    sums = jnp.concatenate(
        [down(normed_grad * hat), down(normed_grad), down(expanded_grad * hat), down(expanded_grad)]
    )
    accumulate(sums_ref, sums)


def place_body(layouts, pieces_ref, *outs):
    for device in range(pieces_ref.shape[0]):
        for start, size, target, where, turned in layouts:
            offset = where(device) * size
            values = pieces_ref[device, :, start : start + size].astype(F32)
            if turned:
                outs[target][offset : offset + size, :] = values.T
            else:
                outs[target][:, offset : offset + size] = values


def pick(array, index, axis):
    return lax.dynamic_index_in_dim(array, index, axis, keepdims=False)


def add_low(left, right):
    return (left.astype(F32) + right.astype(F32)).astype(BF16)


SWAP = [(0, 1), (1, 0)]


class Chain:
    def __init__(self, view, index, count):
        self.view, self.index, self.count, self.step = view, index, count, 0
        self.held = self.flight = ()
        self.out = []

    def term(self, share):
        return pick(self.view, jnp.clip(share, 0, self.count - 1), 0)

    def prepare(self):
        if self.step == self.count - 1:
            return
        self.step += 1
        step, count = self.step, self.count
        self.out = [self.term(self.index + count - step), self.term(self.index - count + step)]
        if self.held:
            self.out = [add_low(one, two) for one, two in zip(self.out, self.held)]

    def send(self):
        if not self.out:
            self.prepare()
        if not self.out:
            return
        step, count = self.step, self.count
        self.flight = (
            lax.ppermute(self.out[0], "z", [(i, i + 1) for i in range(step)]),
            lax.ppermute(self.out[1], "z", [(count - 1 - i, count - 2 - i) for i in range(step)]),
        )
        self.out = []

    def land(self, values):
        if values:
            self.held, self.flight = values, ()

    def total(self):
        own = self.term(self.index).astype(F32)
        return (own + self.held[0].astype(F32) + self.held[1].astype(F32)).astype(BF16)


class Line:
    def __init__(self, piece, index, count):
        self.index, self.count, self.step, self.flight = index, count, 0, ()
        self.from_left, self.from_right, self.own, self.full = [], [], piece, None
        if count > 4:
            self.full = lax.all_gather(piece, "z", axis=0, tiled=True)

    def send(self):
        if self.full is not None or self.step == self.count - 1:
            return
        step, count = self.step, self.count
        right, left = (self.from_left[-1], self.from_right[-1]) if step else (self.own, self.own)
        self.flight = (
            lax.ppermute(right, "z", [(i, i + 1) for i in range(step, count - 1)]),
            lax.ppermute(left, "z", [(i + 1, i) for i in range(count - 1 - step)]),
        )
        self.step += 1

    def land(self, values):
        if values:
            self.from_left.append(values[0])
            self.from_right.append(values[1])
            self.flight = ()

    def slots(self):
        return [*self.from_left[::-1], self.own, *self.from_right]


fence = lax.optimization_barrier


def solution(mesh):
    branches, models, datas = (mesh.shape[name] for name in ("branch", "mp", "dp"))
    cores = 2
    chips = datas // cores
    fine = Mesh(
        mesh.devices.reshape(branches, models, chips, cores), ("branch", "mp", "z", "core")
    )

    def on_device(
        block_input,
        cotangent,
        segments,
        attend_gain,
        attend_shift,
        joined_weight,
        joined_bias,
        dense_weight,
        dense_bias,
        expand_gain,
        expand_shift,
        up_weight,
        up_bias,
        down_weight,
        down_bias,
    ):
        rows, length, width = block_input.shape
        b, m, z, c = (lax.axis_index(name) for name in ("branch", "mp", "z", "core"))
        tokens = rows * length
        span = width // (branches * models)
        column_start = (b * models + m) * span
        heads = branches * cores
        head_columns = joined_weight.shape[1] // heads
        hidden_columns = up_weight.shape[1]
        part = down_weight.shape[0] // branches
        units = chips * part
        head_slot = b * cores + c
        row_share = width // (branches * datas)

        def partner(array, **flips):
            names = tuple(name for name, flip in flips.items() if flip)
            if not names:
                return array
            count = 2 ** len(names)
            return lax.ppermute(array, names, [(i, count - 1 - i) for i in range(count)])

        def swap_core(array):
            return partner(array, core=1)

        def in_core_order(mine, other):
            return jnp.where(c == 0, jnp.concatenate([mine, other]), jnp.concatenate([other, mine]))

        def columns_of(array, start, size):
            return lax.dynamic_slice_in_dim(array, start, size, array.ndim - 1)

        def unit_columns(array, core):
            return jnp.concatenate(
                [
                    columns_of(array, ((k * cores + core) * branches + b) * part, part)
                    for k in range(chips)
                ],
                axis=-1,
            )

        def gather(piece):
            return lax.all_gather(piece, "z", axis=0, tiled=True)

        x_own = block_input.reshape(tokens, width)
        g_piece = cotangent.reshape(tokens, span)
        joined_piece = in_core_order(
            columns_of(joined_weight, head_slot * head_columns, head_columns),
            swap_core(columns_of(joined_weight, (b * cores + 1 - c) * head_columns, head_columns)),
        )
        flips = [(db, dm) for db in range(2) for dm in range(2)]
        g_mine = [partner(g_piece, branch=db, mp=dm) for db, dm in flips]
        x_other = swap_core(x_own)
        segment_rows = jnp.concatenate([segments, swap_core(segments)])
        joined_piece, dense_weight = fence((joined_piece, dense_weight))
        spread_dense = chips == heads and HEAD == cores * dense_weight.shape[0]
        if spread_dense:
            few = HEAD // chips
            per_core = chips // cores
            dense_piece = 0
            for j in range(per_core):
                moves = [
                    (
                        (one * chips + one * cores + to) * cores + at,
                        (one * chips + at * per_core + j) * cores + to,
                    )
                    for one in range(branches)
                    for to in range(cores)
                    for at in range(cores)
                ]
                dense_piece = dense_piece + lax.ppermute(
                    dense_weight[j * few : (j + 1) * few], ("branch", "z", "core"), moves
                )
        else:
            dense_piece = dense_weight

        joined_bias_here = columns_of(joined_bias, (m * heads + head_slot) * head_columns, head_columns)
        up_bias_here = unit_columns(columns_of(up_bias, m * hidden_columns, hidden_columns), c)
        down_piece = lax.dynamic_slice_in_dim(down_weight, b * part, part, 0)

        def flat(vector):
            return vector.reshape(1, -1)

        all_tokens = 2 * tokens
        gains = flat(attend_gain), flat(expand_gain)
        small_tile = min(256, length)
        half_steps = tokens // small_tile
        joined_full = gather(joined_piece)
        x_other, joined_piece, up_weight, dense_piece = fence(
            (x_other, joined_piece, up_weight, dense_piece)
        )
        if spread_dense:
            dense_full = gather(dense_piece)
        else:
            dense_full = lax.all_gather(dense_piece, ("z", "core"), axis=0, tiled=True)
            dense_full = lax.dynamic_slice_in_dim(dense_full, head_slot * HEAD, HEAD, 0)
        up_piece = in_core_order(unit_columns(up_weight, c), swap_core(unit_columns(up_weight, 1 - c)))
        normed, expanded, stats = run(
            functools.partial(norm_body, half_steps),
            2 * half_steps,
            halves(small_tile, width, half_steps) + [whole((1, width))] * 4,
            [(tile(small_tile, width), (all_tokens, width), BF16)] * 2
            + [(tile(small_tile, LANES), (all_tokens, LANES), F32)],
            (x_own, x_other, gains[0], flat(attend_shift), gains[1], flat(expand_shift)),
            20 * all_tokens * width,
        )
        rotary = rotary_tables(segment_rows)
        normed, expanded, rotary, g_mine, up_piece, down_piece = fence(
            (normed, expanded, rotary, g_mine, up_piece, down_piece)
        )
        up_line = Line(up_piece, z, chips)
        up_line.send()
        g_other = [swap_core(piece) for piece in g_mine]
        starts = jnp.stack([((b ^ db) * models + (m ^ dm)) * span for db, dm in flips])
        (g,) = run(
            functools.partial(gather_body, half_steps),
            2 * half_steps,
            [pl.BlockSpec(memory_space=pltpu.SMEM)]
            + [spec for _ in flips for spec in halves(small_tile, span, half_steps)],
            [(tile(small_tile, width), (all_tokens, width), BF16)],
            (starts, *[piece for pair in zip(g_mine, g_other) for piece in pair]),
            all_tokens * width,
        )
        up_line.flight, g, down_piece, joined_full, dense_full = fence(
            (up_line.flight, g, down_piece, joined_full, dense_full)
        )
        up_line.land(up_line.flight)
        up_line.send()

        all_rows = 2 * rows
        mixed, joined_grad, joined_bias_grad = run(
            attention_body,
            all_rows,
            [
                tile(length, width),
                whole((width, head_columns)),
                whole((1, head_columns)),
                tile(length, LANES),
                tile(length, LANES),
                tile(length, LANES),
                pl.BlockSpec((1, length, 1), lambda i: (i, 0, 0)),
                pl.BlockSpec((1, 1, length), lambda i: (i, 0, 0)),
                tile(length, width),
                whole((HEAD, width)),
            ],
            [
                (tile(length, HEAD), (all_tokens, HEAD), BF16),
                (tile(length, head_columns), (all_tokens, head_columns), BF16),
                (whole((1, head_columns)), (1, head_columns), F32),
            ],
            (
                normed,
                joined_full,
                flat(joined_bias_here),
                *rotary,
                segment_rows[:, :, None],
                segment_rows[:, None, :],
                g,
                dense_full,
            ),
            2 * all_tokens * (width * (head_columns + HEAD) + 7 * length * HEAD),
            all_tokens * length,
        )

        live = dict(
            mixed=mixed, joined_grad=joined_grad, normed=normed, expanded=expanded, g=g, down=down_piece
        )

        def step(*landing, hold=()):
            fresh, held, views, outs, kept = fence(
                (
                    dict(live),
                    [chain.flight for chain in landing],
                    [chain.view for chain in waiting],
                    [chain.out for chain in chains],
                    [chain.held for chain in hold],
                )
            )
            for chain, one in zip(hold, kept):
                chain.held = one
            for chain, out in zip(chains, outs):
                chain.out = out
            live.update(fresh)
            for chain, one in zip(landing, held):
                chain.land(one)
            for chain, view in zip(waiting, views):
                chain.view = view
            waiting.clear()

        waiting, chains = [], []
        share_rows = cores * row_share

        def terms(*pairs):
            rows_tile = max(512, share_rows)
            group = rows_tile // share_rows
            groups = chips // group
            columns = sum(right.shape[1] for _, right in pairs)
            ins, args = [], []
            for left, right in pairs:
                ins += [pl.BlockSpec((all_tokens, rows_tile), lambda i: (0, i)), whole(right.shape)]
                args += [left, right]
            (view,) = run(
                terms_body,
                branches * groups,
                ins,
                [
                    (
                        pl.BlockSpec(
                            (group, 1, share_rows, columns), lambda i: (i % groups, i // groups, 0, 0)
                        ),
                        (chips, branches, share_rows, columns),
                        BF16,
                    )
                ],
                args,
                2 * all_tokens * width * columns,
            )
            chain = Chain(view, z, chips)
            waiting.append(chain)
            chains.append(chain)
            return chain

        def spread(chain):
            share = chain.total().reshape(branches * cores * row_share, -1)
            pieces = lax.all_to_all(share, ("branch", "core"), 0, 0, tiled=True)
            return pieces.reshape(branches * cores, row_share, -1)

        unit_flops = 2 * all_tokens * width * units
        big_tile = min(512, length)

        def hidden_values():
            return run(
                hidden_body,
                all_tokens // big_tile,
                [tile(big_tile, width), whole((width, units)), whole((1, units))],
                [(tile(big_tile, units), (all_tokens, units), BF16)] * 2,
                (live["expanded"], up_line, flat(up_bias_here)),
                unit_flops,
                2 * all_tokens * units,
            )

        def hidden_gradient():
            return run(
                hidden_grad_body,
                all_tokens // big_tile,
                [tile(big_tile, width), whole((units, width)), tile(big_tile, units)],
                [
                    (tile(big_tile, units), (all_tokens, units), BF16),
                    (whole((1, units)), (1, units), F32),
                ],
                (live["g"], down_line, live.pop("slope")),
                unit_flops,
            )

        blocks = branches * models

        def of_core(core, columns):
            return pl.BlockSpec((small_tile, columns), lambda i: (core * half_steps + i, 0))

        def out_blocks(pieces):
            steps = half_steps // pieces
            return (
                pl.BlockSpec((1, blocks, small_tile, span), lambda i: (i // steps, 0, i % steps, 0)),
                (pieces, blocks, tokens // pieces, span),
                BF16,
            )

        def input_terms(core, *got):
            return run(
                input_body,
                half_steps,
                [
                    tile(small_tile, width),
                    of_core(core, LANES),
                    of_core(core, head_columns),
                    whole((width, head_columns)),
                    of_core(core, units),
                    whole((width, units)),
                    whole((1, width)),
                    whole((1, width)),
                    *[out_blocks(2)[0]] * len(got),
                ],
                [out_blocks(2), (whole((4, width)), (4, width), F32)],
                (
                    (x_own, x_other)[core],
                    stats,
                    live["joined_grad"],
                    joined_full,
                    live["grad"],
                    up_line,
                    *gains,
                    *got,
                ),
                unit_flops // 2 + all_tokens * width * head_columns,
            )

        def forward_terms(core, *got):
            return run(
                forward_body,
                half_steps,
                [
                    of_core(core, HEAD),
                    whole((HEAD, width)),
                    of_core(core, units),
                    whole((units, width)),
                    *[out_blocks(1)[0]] * len(got),
                ],
                [out_blocks(1)],
                (live["mixed"], dense_full, live["active"], down_line, *got),
                unit_flops // 2 + all_tokens * width * HEAD,
            )[0]

        def block_sum(blocks):
            return lax.psum_scatter(blocks[0], ("branch", "mp"), scatter_dimension=0, tiled=True)[0]

        def first_sends(term):
            one, two = (term[h].reshape(branches, models, tokens // 2, span) for h in range(2))
            return partner(pick(one, 1 - b, 0), branch=1), partner(pick(two, 1 - m, 1), mp=1)

        def first_sum(term, got):
            one, two = (term[h].reshape(branches, models, tokens // 2, span) for h in range(2))
            return add_low(pick(one, b, 0), got[0]), add_low(pick(two, m, 1), got[1])

        def second_sends(pair):
            one, two = pair
            return partner(pick(one, 1 - m, 0), mp=1), partner(pick(two, 1 - b, 0), branch=1)

        def second_sum(pair, got):
            one, two = pair
            return jnp.concatenate(
                [
                    pick(one, m, 0).astype(F32) + got[0].astype(F32),
                    pick(two, b, 0).astype(F32) + got[1].astype(F32),
                ]
            )

        def put(pieces, shapes, layouts):
            return run(
                functools.partial(place_body, layouts),
                1,
                [whole(pieces.shape)],
                [(whole(shape), shape, F32) for shape in shapes],
                [pieces],
                0,
            )

        def unit_layouts(turned):
            return [
                (
                    k * part,
                    part,
                    0,
                    lambda device, k=k: (k * cores + device % cores) * branches + device // cores,
                    turned,
                )
                for k in range(chips)
            ]

        simple = part % LANES != 0 or row_share % 8 != 0

        def place_joined(pieces):
            if simple:
                pieces = pieces.astype(F32)
                joined = pieces[:, :, :head_columns].transpose(1, 0, 2).reshape(row_share, -1)
                return joined, pieces[:, :, head_columns:].transpose(0, 2, 1).reshape(-1, row_share)
            return put(
                pieces,
                [(row_share, heads * head_columns), (heads * HEAD, row_share)],
                [
                    (0, head_columns, 0, lambda device: device, False),
                    (head_columns, HEAD, 1, lambda device: device, True),
                ],
            )

        def place_units(pieces, turned):
            if not simple:
                shape = (hidden_columns, row_share) if turned else (row_share, hidden_columns)
                return put(pieces, [shape], unit_layouts(turned))[0]
            pieces = pieces.astype(F32).reshape(branches, cores, row_share, chips, part)
            if turned:
                return pieces.transpose(3, 1, 0, 4, 2).reshape(hidden_columns, row_share)
            return pieces.transpose(2, 3, 1, 0, 4).reshape(row_share, hidden_columns)

        def finish(chain):
            while chain.step < chips - 1:
                chain.send()
                step(chain)
            return spread(chain)

        step(up_line)
        up_line.send()
        joined_chain = terms((live.pop("normed"), live["joined_grad"]), (live["g"], live["mixed"]))
        joined_chain.send()
        step(up_line)
        down_line = Line(live.pop("down"), z, chips)
        down_line.send()
        live["active"], live["slope"] = hidden_values()
        down_chain = terms((live["g"], live["active"]))
        down_chain.prepare()
        step(down_line, joined_chain)
        down_line.send()
        down_chain.send()
        joined_chain.prepare()
        g_float = g_piece.astype(F32)
        out_slot = lax.dynamic_update_slice(
            jnp.zeros((width,), F32), jnp.sum(g_float, axis=0), (column_start,)
        )
        joined_slot = lax.dynamic_update_slice(
            jnp.zeros_like(joined_bias),
            joined_bias_grad.reshape(-1),
            ((m * heads + head_slot) * head_columns,),
        )
        live["slots"] = jnp.concatenate([out_slot, joined_slot])
        step(down_line, down_chain)
        down_line.send()
        joined_chain.send()
        down_chain.prepare()
        step(down_line, joined_chain)
        joined_chain.send()
        live["out_other"] = forward_terms(1)
        live["grad"], live["bias"] = hidden_gradient()
        step(joined_chain)
        down_chain.send()
        live["out_got"] = swap_core(live.pop("out_other"))
        live["joined_pieces"] = finish(joined_chain)
        up_chain = terms((live.pop("expanded"), live["grad"]))
        live.pop("g")
        up_chain.prepare()
        live["out"] = forward_terms(0, live.pop("out_got"))
        step(down_chain)
        forward_sum = block_sum(live.pop("out"))
        up_chain.send()
        down_chain.prepare()
        live["in_other"], live["sums_other"] = input_terms(1)
        step(up_chain)
        live["forward_sum"] = forward_sum
        down_chain.send()
        live["in_got"] = swap_core(live.pop("in_other"))
        up_chain.prepare()
        live["in"], live["sums_own"] = input_terms(0, live.pop("in_got"))
        up_slot = lax.dynamic_update_slice(
            jnp.zeros((models, chips, cores, branches, part), F32),
            live.pop("bias").reshape(1, chips, 1, 1, part),
            (m, 0, c, b, 0),
        ).reshape(-1)
        live["slots"] = jnp.concatenate([live["slots"], up_slot])
        step(down_chain)
        up_chain.send()
        live["in_got"] = first_sends(live["in"])
        sums = live.pop("sums_own") + live.pop("sums_other")
        small = jnp.concatenate([sums.reshape(-1), live.pop("slots")])
        small = (
            small
            + partner(small, core=1)
            + partner(small, branch=1)
            + partner(small, branch=1, core=1)
        )
        live["joined_out"], live["dense_out"] = place_joined(live.pop("joined_pieces"))
        down_pieces = finish(down_chain)
        step(up_chain)
        up_chain.prepare()
        step()
        live["down_pieces"] = down_pieces
        up_chain.send()
        live["in"] = first_sum(live["in"], live.pop("in_got"))
        live["in_got"] = second_sends(live["in"])
        near = lax.ppermute(small, "z", [(i, i ^ 1) for i in range(chips)])
        far = [
            lax.ppermute(
                small,
                ("mp", "z"),
                [
                    (one * chips + i, (1 - one) * chips + (i ^ flip))
                    for one in range(models)
                    for i in range(chips)
                ],
            )
            for flip in range(2)
        ]
        live["small"] = small + near + far[0] + far[1]
        forward_sum = live["forward_sum"]
        residual = columns_of(x_own, column_start, span).astype(F32)
        column_bias = columns_of(dense_bias + down_bias, column_start, span)
        block_output = (residual + forward_sum + column_bias).astype(BF16)
        live["block_output"] = block_output
        step(up_chain)
        block_output = live["block_output"]
        up_pieces = finish(up_chain)
        small = live["small"]
        flip = 2
        while flip < chips:
            small = small + lax.ppermute(small, "z", [(i, i ^ flip) for i in range(chips)])
            flip *= 2
        input_sum = second_sum(live.pop("in"), live.pop("in_got"))
        joined_out, dense_out = live["joined_out"], live["dense_out"]
        down_out, up_out = place_units(live["down_pieces"], True), place_units(up_pieces, False)

        input_gradient = (g_float + input_sum).astype(BF16)

        w = width
        joined_end = 5 * w + joined_bias.shape[0]
        return (
            block_output.reshape(rows, length, span),
            input_gradient.reshape(rows, length, span),
            small[:w],
            small[w : 2 * w],
            joined_out,
            small[5 * w : joined_end],
            dense_out,
            small[4 * w : 5 * w],
            small[2 * w : 3 * w],
            small[3 * w : 4 * w],
            up_out,
            small[joined_end:],
            down_out,
            small[4 * w : 5 * w],
        )

    data = ("z", "core")
    everything = ("branch", "z", "core")
    in_specs = (
        P(data, None, None),
        P(data, None, ("branch", "mp")),
        P(data, None),
        P(),
        P(),
        P(data, "mp"),
        P(),
        P(("mp", "z", "core"), None),
        P(),
        P(),
        P(),
        P(data, "mp"),
        P(),
        P(("mp", "z", "core"), None),
        P(),
    )
    out_specs = (
        P(data, None, ("branch", "mp")),
        P(data, None, ("branch", "mp")),
        P(),
        P(),
        P(everything, "mp"),
        P(),
        P("mp", everything),
        P(),
        P(),
        P(),
        P(everything, "mp"),
        P(),
        P("mp", everything),
        P(),
    )
    return jax.shard_map(
        on_device, mesh=fine, in_specs=in_specs, out_specs=out_specs, check_vma=False
    )
```

```python
import functools
import math

import jax
import jax.numpy as jnp
from jax import lax
from jax.experimental import pallas as pl
from jax.experimental.pallas import tpu as pltpu
from jax.sharding import Mesh, PartitionSpec as P

HEAD = 256
ROT = 64
LANES = 128
NEGATIVE = -1e30
VMEM_BYTES = 56 * 1024 * 1024
F32 = jnp.float32
BF16 = jnp.bfloat16


def rotary_tables(segment_rows):
    length = segment_rows.shape[1]
    before = jnp.sum(
        (segment_rows[:, None, :] < segment_rows[:, :, None]).astype(jnp.int32), axis=2
    )
    places = (jnp.arange(length, dtype=jnp.int32)[None] - before).astype(F32)
    frequency = 10000.0 ** (-jnp.arange(0, ROT, 2).astype(F32) / ROT)
    angles = (places[:, :, None] * frequency).reshape(-1, ROT // 2)
    cosine, sine = jnp.cos(angles), jnp.sin(angles)
    none = jnp.zeros_like(sine)
    rest = jnp.zeros((angles.shape[0], LANES - ROT), F32)
    return (
        jnp.concatenate([cosine, cosine, rest + 1.0], axis=1),
        jnp.concatenate([-sine, none, rest], axis=1),
        jnp.concatenate([none, sine, rest], axis=1),
    )


def rotate(values, self_factor, right_factor, left_factor):
    half = ROT // 2
    front = values[:, :LANES]
    turned = (
        front * self_factor
        + pltpu.roll(front, LANES - half, 1) * right_factor
        + pltpu.roll(front, half, 1) * left_factor
    )
    return jnp.concatenate([turned, values[:, LANES:]], axis=1)


def dot(left, right, left_dim, right_dim):
    return lax.dot_general(
        left, right, (((left_dim,), (right_dim,)), ((), ())), preferred_element_type=F32
    )


def whole(shape):
    return pl.BlockSpec(shape, lambda i: (0,) * len(shape), pipeline_mode=pl.Buffered(1))


def tile(rows, columns):
    return pl.BlockSpec((rows, columns), lambda i: (i, 0))


def run(body, steps, ins, outs, args, flops, transcendentals=0):
    scratch = []
    if any(isinstance(arg, Line) for arg in args):
        body, ins, args, scratch = put_together(body, ins, args)
    shapes = [jax.ShapeDtypeStruct(shape, dtype) for _, shape, dtype in outs]
    moved = sum(a.size * a.dtype.itemsize for a in list(args) + shapes)
    return pl.pallas_call(
        body,
        grid=(steps,),
        in_specs=ins,
        out_specs=[spec for spec, _, _ in outs],
        out_shape=shapes,
        scratch_shapes=scratch,
        cost_estimate=pl.CostEstimate(
            flops=3 * flops, bytes_accessed=moved, transcendentals=transcendentals
        ),
        compiler_params=pltpu.CompilerParams(vmem_limit_bytes=VMEM_BYTES),
    )(*args)


def put_together(body, ins, args):
    new_ins, new_args, places, scratch = [], [], [], []
    for spec, arg in zip(ins, args):
        if not isinstance(arg, Line):
            new_ins.append(spec)
            new_args.append(arg)
            places.append(None)
        elif arg.full is not None:
            new_ins.append(spec)
            new_args.append(arg.full)
            places.append(None)
        else:
            slots = arg.slots()
            rows, columns = slots[0].shape
            new_ins += [pl.BlockSpec(memory_space=pl.ANY)] * len(slots)
            new_args += slots
            places.append((len(slots), rows, arg.count))
            scratch += [
                pltpu.VMEM((arg.count * rows, columns), slots[0].dtype),
                pltpu.SemaphoreType.DMA((arg.count,)),
            ]
            index = arg.index
    if not scratch:
        return body, new_ins, new_args, []

    def whole_body(index_ref, *refs):
        kept, held = refs[: len(refs) - len(scratch)], refs[len(refs) - len(scratch) :]
        inner, lines, at = [], [], 0
        for place in places:
            if place is None:
                inner.append(kept[at])
                at += 1
            else:
                full_ref, sems = held[2 * len(lines) : 2 * len(lines) + 2]
                lines.append((kept[at : at + place[0]], full_ref, sems, place))
                inner.append(full_ref)
                at += place[0]

        @pl.when(pl.program_id(0) == 0)
        def _():
            for blocks, full_ref, sems, (_, rows, count) in lines:
                for j in range(count):
                    for k, block in enumerate(blocks):

                        @pl.when(count - 1 - index_ref[0] + j == k)
                        def _():
                            pltpu.make_async_copy(
                                block, full_ref.at[pl.ds(j * rows, rows)], sems.at[j]
                            ).start()

            for blocks, full_ref, sems, (_, rows, count) in lines:
                for j in range(count):
                    pltpu.make_async_copy(
                        blocks[0], full_ref.at[pl.ds(j * rows, rows)], sems.at[j]
                    ).wait()

        body(*inner, *kept[at:])

    return (
        whole_body,
        [pl.BlockSpec(memory_space=pltpu.SMEM)] + new_ins,
        [index.reshape(1)] + new_args,
        scratch,
    )


def statistics(x):
    mean = jnp.mean(x, axis=-1, keepdims=True)
    center = x - mean
    inverse = lax.rsqrt(jnp.mean(center * center, axis=-1, keepdims=True) + 1e-05)
    return center * inverse, mean, inverse


def either(steps, mine_ref, other_ref):
    return jnp.where(pl.program_id(0) < steps, mine_ref[...], other_ref[...])


def halves(rows, columns, steps):
    return [
        pl.BlockSpec((rows, columns), lambda i: (jnp.minimum(i, steps - 1), 0)),
        pl.BlockSpec((rows, columns), lambda i: (jnp.maximum(i - steps, 0), 0)),
    ]


def norm_body(steps, mine_ref, other_ref, gain_a, shift_a, gain_e, shift_e, normed_ref, expanded_ref, stats_ref):
    hat, mean, inverse = statistics(either(steps, mine_ref, other_ref).astype(F32))
    lane = lax.broadcasted_iota(jnp.int32, stats_ref.shape, 1)
    stats_ref[...] = jnp.where(lane == 0, mean, inverse)
    normed_ref[...] = (hat * gain_a[...] + shift_a[...]).astype(BF16)
    expanded_ref[...] = (hat * gain_e[...] + shift_e[...]).astype(BF16)


def gather_body(steps, starts_ref, *refs):
    pieces, out_ref = refs[:-1], refs[-1]
    span = pieces[0].shape[1]
    for k in range(len(pieces) // 2):
        columns = pl.ds(pl.multiple_of(starts_ref[k], span), span)
        out_ref[:, columns] = either(steps, pieces[2 * k], pieces[2 * k + 1])


def accumulate(ref, value):
    @pl.when(pl.program_id(0) == 0)
    def _():
        ref[...] = value

    @pl.when(pl.program_id(0) != 0)
    def _():
        ref[...] += value


def attention_body(
    normed_ref, joined_ref, bias_ref, self_ref, right_ref, left_ref, column_ref, row_ref, g_ref, dense_ref,
    mixed_ref, grad_ref, bias_grad_ref,
):
    length = normed_ref.shape[0]
    scale = 1.0 / math.sqrt(HEAD)
    factors = self_ref[...], right_ref[...], left_ref[...]
    raw = dot(normed_ref[...], joined_ref[...], 1, 0) + bias_ref[...]
    queries = (rotate(raw[:, :HEAD], *factors) * scale).astype(BF16)
    keyset = rotate(raw[:, HEAD : 2 * HEAD], *factors).astype(BF16)
    valueset = raw[:, 2 * HEAD :].astype(BF16)
    query_index = lax.broadcasted_iota(jnp.int32, (length, length), 0)
    key_index = lax.broadcasted_iota(jnp.int32, (length, length), 1)
    allowed = (column_ref[0] == row_ref[0]) & (key_index <= query_index)
    scores = jnp.where(allowed, dot(queries, keyset, 1, 1), NEGATIVE)
    shifted = jnp.exp(scores - jnp.max(scores, axis=-1, keepdims=True))
    probs = shifted / jnp.sum(shifted, axis=-1, keepdims=True)
    low = probs.astype(BF16)
    mixed_ref[...] = dot(low, valueset, 1, 0).astype(BF16)
    mixed_grad = dot(g_ref[...], dense_ref[...], 1, 1).astype(BF16)
    probs_grad = dot(mixed_grad, valueset, 1, 1)
    value_grad = dot(low, mixed_grad, 0, 0)
    inner = jnp.sum(probs_grad * probs, axis=-1, keepdims=True)
    score_grad = (probs * (probs_grad - inner)).astype(BF16)
    query_grad = rotate(dot(score_grad, keyset, 1, 0) * scale, *back_factors(factors))
    key_grad = rotate(dot(score_grad, queries, 0, 0), *back_factors(factors))
    joined_grad = jnp.concatenate([query_grad, key_grad, value_grad], axis=1).astype(BF16)
    grad_ref[...] = joined_grad
    accumulate(bias_grad_ref, jnp.sum(joined_grad.astype(F32), axis=0, keepdims=True))


def back_factors(factors):
    return factors[0], -factors[1], -factors[2]


def hidden_body(expanded_ref, up_ref, bias_ref, activated_ref, slope_ref):
    block = up_ref.shape[1] // 4
    for k in range(4):
        columns = pl.ds(k * block, block)
        hidden = dot(expanded_ref[...], up_ref[:, columns], 1, 0) + bias_ref[:, columns]
        below = 0.5 * (1.0 + lax.erf(hidden * math.sqrt(0.5)))
        density = jnp.exp(hidden * hidden * -0.5) * (1.0 / math.sqrt(2.0 * math.pi))
        activated_ref[:, columns] = (hidden * below).astype(BF16)
        slope_ref[:, columns] = (below + hidden * density).astype(BF16)


def terms_body(*refs):
    out_ref, start = refs[-1], 0
    for left_ref, right_ref in zip(refs[:-1:2], refs[1:-1:2]):
        stop = start + right_ref.shape[1]
        term = dot(left_ref[...], right_ref[...], 0, 0).astype(BF16)
        out_ref[:, :, :, start:stop] = term.reshape(*out_ref.shape[:3], stop - start)
        start = stop


def hidden_grad_body(g_ref, down_ref, slope_ref, grad_ref, bias_grad_ref):
    grad = dot(g_ref[...], down_ref[...], 1, 1) * slope_ref[...].astype(F32)
    grad = grad.astype(BF16)
    grad_ref[...] = grad
    accumulate(bias_grad_ref, jnp.sum(grad.astype(F32), axis=0, keepdims=True))


def store_blocks(out_ref, values, got_refs):
    blocks, span = out_ref.shape[1], out_ref.shape[3]
    for k in range(blocks):
        block = values[:, k * span : (k + 1) * span]
        for got_ref in got_refs:
            block = block + got_ref[0, k].astype(F32)
        out_ref[0, k] = block.astype(BF16)


def forward_body(mixed_ref, dense_ref, active_ref, down_ref, *refs):
    total = dot(mixed_ref[...], dense_ref[...], 1, 0)
    total += dot(active_ref[...], down_ref[...], 1, 0)
    store_blocks(refs[-1], total, refs[:-1])


def input_body(
    x_ref, stats_ref, joined_grad_ref, joined_ref, hidden_grad_ref, up_ref, gain_a, gain_e, *refs
):
    got_refs, (out_ref, sums_ref) = refs[:-2], refs[-2:]
    normed_grad = dot(joined_grad_ref[...], joined_ref[...], 1, 1)
    expanded_grad = dot(hidden_grad_ref[...], up_ref[...], 1, 1)
    mean, inverse = stats_ref[:, 0:1], stats_ref[:, 1:2]
    hat = (x_ref[...].astype(F32) - mean) * inverse
    weighted = normed_grad * gain_a[...] + expanded_grad * gain_e[...]
    weighted_mean = jnp.mean(weighted, axis=-1, keepdims=True)
    along = jnp.mean(weighted * hat, axis=-1, keepdims=True)
    store_blocks(out_ref, inverse * (weighted - weighted_mean - hat * along), got_refs)

    def down(values):
        return jnp.sum(values, axis=0, keepdims=True)

    sums = jnp.concatenate(
        [down(normed_grad * hat), down(normed_grad), down(expanded_grad * hat), down(expanded_grad)]
    )
    accumulate(sums_ref, sums)


def place_body(layouts, pieces_ref, *outs):
    for device in range(pieces_ref.shape[0]):
        for start, size, target, where, turned in layouts:
            offset = where(device) * size
            values = pieces_ref[device, :, start : start + size].astype(F32)
            if turned:
                outs[target][offset : offset + size, :] = values.T
            else:
                outs[target][:, offset : offset + size] = values


def pick(array, index, axis):
    return lax.dynamic_index_in_dim(array, index, axis, keepdims=False)


def add_low(left, right):
    return (left.astype(F32) + right.astype(F32)).astype(BF16)


SWAP = [(0, 1), (1, 0)]


class Chain:
    def __init__(self, view, index, count):
        self.view, self.index, self.count, self.step = view, index, count, 0
        self.held = self.flight = ()
        self.out = []

    def term(self, share):
        return pick(self.view, jnp.clip(share, 0, self.count - 1), 0)

    def prepare(self):
        if self.step == self.count - 1:
            return
        self.step += 1
        step, count = self.step, self.count
        self.out = [self.term(self.index + count - step), self.term(self.index - count + step)]
        if self.held:
            self.out = [add_low(one, two) for one, two in zip(self.out, self.held)]

    def send(self):
        if not self.out:
            self.prepare()
        if not self.out:
            return
        step, count = self.step, self.count
        self.flight = (
            lax.ppermute(self.out[0], "z", [(i, i + 1) for i in range(step)]),
            lax.ppermute(self.out[1], "z", [(count - 1 - i, count - 2 - i) for i in range(step)]),
        )
        self.out = []

    def land(self, values):
        if values:
            self.held, self.flight = values, ()

    def total(self):
        own = self.term(self.index).astype(F32)
        return (own + self.held[0].astype(F32) + self.held[1].astype(F32)).astype(BF16)


class Line:
    def __init__(self, piece, index, count):
        self.index, self.count, self.step, self.flight = index, count, 0, ()
        self.from_left, self.from_right, self.own, self.full = [], [], piece, None
        if count > 4:
            self.full = lax.all_gather(piece, "z", axis=0, tiled=True)

    def send(self):
        if self.full is not None or self.step == self.count - 1:
            return
        step, count = self.step, self.count
        right, left = (self.from_left[-1], self.from_right[-1]) if step else (self.own, self.own)
        self.flight = (
            lax.ppermute(right, "z", [(i, i + 1) for i in range(step, count - 1)]),
            lax.ppermute(left, "z", [(i + 1, i) for i in range(count - 1 - step)]),
        )
        self.step += 1

    def land(self, values):
        if values:
            self.from_left.append(values[0])
            self.from_right.append(values[1])
            self.flight = ()

    def slots(self):
        return [*self.from_left[::-1], self.own, *self.from_right]


fence = lax.optimization_barrier


def solution(mesh):
    branches, models, datas = (mesh.shape[name] for name in ("branch", "mp", "dp"))
    cores = 2
    chips = datas // cores
    fine = Mesh(
        mesh.devices.reshape(branches, models, chips, cores), ("branch", "mp", "z", "core")
    )

    def on_device(
        block_input,
        cotangent,
        segments,
        attend_gain,
        attend_shift,
        joined_weight,
        joined_bias,
        dense_weight,
        dense_bias,
        expand_gain,
        expand_shift,
        up_weight,
        up_bias,
        down_weight,
        down_bias,
    ):
        rows, length, width = block_input.shape
        b, m, z, c = (lax.axis_index(name) for name in ("branch", "mp", "z", "core"))
        tokens = rows * length
        span = width // (branches * models)
        column_start = (b * models + m) * span
        heads = branches * cores
        head_columns = joined_weight.shape[1] // heads
        hidden_columns = up_weight.shape[1]
        part = down_weight.shape[0] // branches
        units = chips * part
        head_slot = b * cores + c
        row_share = width // (branches * datas)

        def partner(array, **flips):
            names = tuple(name for name, flip in flips.items() if flip)
            if not names:
                return array
            count = 2 ** len(names)
            return lax.ppermute(array, names, [(i, count - 1 - i) for i in range(count)])

        def swap_core(array):
            return partner(array, core=1)

        def in_core_order(mine, other):
            return jnp.where(c == 0, jnp.concatenate([mine, other]), jnp.concatenate([other, mine]))

        def columns_of(array, start, size):
            return lax.dynamic_slice_in_dim(array, start, size, array.ndim - 1)

        def unit_columns(array, core):
            return jnp.concatenate(
                [
                    columns_of(array, ((k * cores + core) * branches + b) * part, part)
                    for k in range(chips)
                ],
                axis=-1,
            )

        def gather(piece):
            return lax.all_gather(piece, "z", axis=0, tiled=True)

        x_own = block_input.reshape(tokens, width)
        g_piece = cotangent.reshape(tokens, span)
        joined_piece = in_core_order(
            columns_of(joined_weight, head_slot * head_columns, head_columns),
            swap_core(columns_of(joined_weight, (b * cores + 1 - c) * head_columns, head_columns)),
        )
        flips = [(db, dm) for db in range(2) for dm in range(2)]
        g_mine = [partner(g_piece, branch=db, mp=dm) for db, dm in flips]
        x_other = swap_core(x_own)
        segment_rows = jnp.concatenate([segments, swap_core(segments)])
        joined_piece, dense_weight = fence((joined_piece, dense_weight))
        spread_dense = chips == heads and HEAD == cores * dense_weight.shape[0]
        if spread_dense:
            few = HEAD // chips
            per_core = chips // cores
            dense_piece = 0
            for j in range(per_core):
                moves = [
                    (
                        (one * chips + one * cores + to) * cores + at,
                        (one * chips + at * per_core + j) * cores + to,
                    )
                    for one in range(branches)
                    for to in range(cores)
                    for at in range(cores)
                ]
                dense_piece = dense_piece + lax.ppermute(
                    dense_weight[j * few : (j + 1) * few], ("branch", "z", "core"), moves
                )
        else:
            dense_piece = dense_weight

        joined_bias_here = columns_of(joined_bias, (m * heads + head_slot) * head_columns, head_columns)
        up_bias_here = unit_columns(columns_of(up_bias, m * hidden_columns, hidden_columns), c)
        down_piece = lax.dynamic_slice_in_dim(down_weight, b * part, part, 0)

        def flat(vector):
            return vector.reshape(1, -1)

        all_tokens = 2 * tokens
        gains = flat(attend_gain), flat(expand_gain)
        small_tile = min(256, length)
        half_steps = tokens // small_tile
        joined_full = gather(joined_piece)
        x_other, joined_piece, up_weight, dense_piece = fence(
            (x_other, joined_piece, up_weight, dense_piece)
        )
        if spread_dense:
            dense_full = gather(dense_piece)
        else:
            dense_full = lax.all_gather(dense_piece, ("z", "core"), axis=0, tiled=True)
            dense_full = lax.dynamic_slice_in_dim(dense_full, head_slot * HEAD, HEAD, 0)
        up_piece = in_core_order(unit_columns(up_weight, c), swap_core(unit_columns(up_weight, 1 - c)))
        normed, expanded, stats = run(
            functools.partial(norm_body, half_steps),
            2 * half_steps,
            halves(small_tile, width, half_steps) + [whole((1, width))] * 4,
            [(tile(small_tile, width), (all_tokens, width), BF16)] * 2
            + [(tile(small_tile, LANES), (all_tokens, LANES), F32)],
            (x_own, x_other, gains[0], flat(attend_shift), gains[1], flat(expand_shift)),
            20 * all_tokens * width,
        )
        rotary = rotary_tables(segment_rows)
        normed, expanded, rotary, g_mine, up_piece, down_piece = fence(
            (normed, expanded, rotary, g_mine, up_piece, down_piece)
        )
        up_line = Line(up_piece, z, chips)
        up_line.send()
        g_other = [swap_core(piece) for piece in g_mine]
        starts = jnp.stack([((b ^ db) * models + (m ^ dm)) * span for db, dm in flips])
        (g,) = run(
            functools.partial(gather_body, half_steps),
            2 * half_steps,
            [pl.BlockSpec(memory_space=pltpu.SMEM)]
            + [spec for _ in flips for spec in halves(small_tile, span, half_steps)],
            [(tile(small_tile, width), (all_tokens, width), BF16)],
            (starts, *[piece for pair in zip(g_mine, g_other) for piece in pair]),
            all_tokens * width,
        )
        up_line.flight, g, down_piece, joined_full, dense_full = fence(
            (up_line.flight, g, down_piece, joined_full, dense_full)
        )
        up_line.land(up_line.flight)
        up_line.send()

        all_rows = 2 * rows
        mixed, joined_grad, joined_bias_grad = run(
            attention_body,
            all_rows,
            [
                tile(length, width),
                whole((width, head_columns)),
                whole((1, head_columns)),
                tile(length, LANES),
                tile(length, LANES),
                tile(length, LANES),
                pl.BlockSpec((1, length, 1), lambda i: (i, 0, 0)),
                pl.BlockSpec((1, 1, length), lambda i: (i, 0, 0)),
                tile(length, width),
                whole((HEAD, width)),
            ],
            [
                (tile(length, HEAD), (all_tokens, HEAD), BF16),
                (tile(length, head_columns), (all_tokens, head_columns), BF16),
                (whole((1, head_columns)), (1, head_columns), F32),
            ],
            (
                normed,
                joined_full,
                flat(joined_bias_here),
                *rotary,
                segment_rows[:, :, None],
                segment_rows[:, None, :],
                g,
                dense_full,
            ),
            2 * all_tokens * (width * (head_columns + HEAD) + 7 * length * HEAD),
            all_tokens * length,
        )

        live = dict(
            mixed=mixed, joined_grad=joined_grad, normed=normed, expanded=expanded, g=g, down=down_piece
        )

        def step(*landing, hold=()):
            fresh, held, views, outs, kept = fence(
                (
                    dict(live),
                    [chain.flight for chain in landing],
                    [chain.view for chain in waiting],
                    [chain.out for chain in chains],
                    [chain.held for chain in hold],
                )
            )
            for chain, one in zip(hold, kept):
                chain.held = one
            for chain, out in zip(chains, outs):
                chain.out = out
            live.update(fresh)
            for chain, one in zip(landing, held):
                chain.land(one)
            for chain, view in zip(waiting, views):
                chain.view = view
            waiting.clear()

        waiting, chains = [], []
        share_rows = cores * row_share

        def terms(*pairs):
            rows_tile = max(512, share_rows)
            group = rows_tile // share_rows
            groups = chips // group
            columns = sum(right.shape[1] for _, right in pairs)
            ins, args = [], []
            for left, right in pairs:
                ins += [pl.BlockSpec((all_tokens, rows_tile), lambda i: (0, i)), whole(right.shape)]
                args += [left, right]
            (view,) = run(
                terms_body,
                branches * groups,
                ins,
                [
                    (
                        pl.BlockSpec(
                            (group, 1, share_rows, columns), lambda i: (i % groups, i // groups, 0, 0)
                        ),
                        (chips, branches, share_rows, columns),
                        BF16,
                    )
                ],
                args,
                2 * all_tokens * width * columns,
            )
            chain = Chain(view, z, chips)
            waiting.append(chain)
            chains.append(chain)
            return chain

        def spread(chain):
            share = chain.total().reshape(branches * cores * row_share, -1)
            pieces = lax.all_to_all(share, ("branch", "core"), 0, 0, tiled=True)
            return pieces.reshape(branches * cores, row_share, -1)

        unit_flops = 2 * all_tokens * width * units
        big_tile = min(512, length)

        def hidden_values():
            return run(
                hidden_body,
                all_tokens // big_tile,
                [tile(big_tile, width), whole((width, units)), whole((1, units))],
                [(tile(big_tile, units), (all_tokens, units), BF16)] * 2,
                (live["expanded"], up_line, flat(up_bias_here)),
                unit_flops,
                2 * all_tokens * units,
            )

        def hidden_gradient():
            return run(
                hidden_grad_body,
                all_tokens // big_tile,
                [tile(big_tile, width), whole((units, width)), tile(big_tile, units)],
                [
                    (tile(big_tile, units), (all_tokens, units), BF16),
                    (whole((1, units)), (1, units), F32),
                ],
                (live["g"], down_line, live.pop("slope")),
                unit_flops,
            )

        blocks = branches * models

        def of_core(core, columns):
            return pl.BlockSpec((small_tile, columns), lambda i: (core * half_steps + i, 0))

        def out_blocks(pieces):
            steps = half_steps // pieces
            return (
                pl.BlockSpec((1, blocks, small_tile, span), lambda i: (i // steps, 0, i % steps, 0)),
                (pieces, blocks, tokens // pieces, span),
                BF16,
            )

        def input_terms(core, *got):
            return run(
                input_body,
                half_steps,
                [
                    tile(small_tile, width),
                    of_core(core, LANES),
                    of_core(core, head_columns),
                    whole((width, head_columns)),
                    of_core(core, units),
                    whole((width, units)),
                    whole((1, width)),
                    whole((1, width)),
                    *[out_blocks(2)[0]] * len(got),
                ],
                [out_blocks(2), (whole((4, width)), (4, width), F32)],
                (
                    (x_own, x_other)[core],
                    stats,
                    live["joined_grad"],
                    joined_full,
                    live["grad"],
                    up_line,
                    *gains,
                    *got,
                ),
                unit_flops // 2 + all_tokens * width * head_columns,
            )

        def forward_terms(core, *got):
            return run(
                forward_body,
                half_steps,
                [
                    of_core(core, HEAD),
                    whole((HEAD, width)),
                    of_core(core, units),
                    whole((units, width)),
                    *[out_blocks(1)[0]] * len(got),
                ],
                [out_blocks(1)],
                (live["mixed"], dense_full, live["active"], down_line, *got),
                unit_flops // 2 + all_tokens * width * HEAD,
            )[0]

        def block_sum(blocks):
            return lax.psum_scatter(blocks[0], ("branch", "mp"), scatter_dimension=0, tiled=True)[0]

        def first_sends(term):
            one, two = (term[h].reshape(branches, models, tokens // 2, span) for h in range(2))
            return partner(pick(one, 1 - b, 0), branch=1), partner(pick(two, 1 - m, 1), mp=1)

        def first_sum(term, got):
            one, two = (term[h].reshape(branches, models, tokens // 2, span) for h in range(2))
            return add_low(pick(one, b, 0), got[0]), add_low(pick(two, m, 1), got[1])

        def second_sends(pair):
            one, two = pair
            return partner(pick(one, 1 - m, 0), mp=1), partner(pick(two, 1 - b, 0), branch=1)

        def second_sum(pair, got):
            one, two = pair
            return jnp.concatenate(
                [
                    pick(one, m, 0).astype(F32) + got[0].astype(F32),
                    pick(two, b, 0).astype(F32) + got[1].astype(F32),
                ]
            )

        def put(pieces, shapes, layouts):
            return run(
                functools.partial(place_body, layouts),
                1,
                [whole(pieces.shape)],
                [(whole(shape), shape, F32) for shape in shapes],
                [pieces],
                0,
            )

        def unit_layouts(turned):
            return [
                (
                    k * part,
                    part,
                    0,
                    lambda device, k=k: (k * cores + device % cores) * branches + device // cores,
                    turned,
                )
                for k in range(chips)
            ]

        simple = part % LANES != 0 or row_share % 8 != 0

        def place_joined(pieces):
            if simple:
                pieces = pieces.astype(F32)
                joined = pieces[:, :, :head_columns].transpose(1, 0, 2).reshape(row_share, -1)
                return joined, pieces[:, :, head_columns:].transpose(0, 2, 1).reshape(-1, row_share)
            return put(
                pieces,
                [(row_share, heads * head_columns), (heads * HEAD, row_share)],
                [
                    (0, head_columns, 0, lambda device: device, False),
                    (head_columns, HEAD, 1, lambda device: device, True),
                ],
            )

        def place_units(pieces, turned):
            if not simple:
                shape = (hidden_columns, row_share) if turned else (row_share, hidden_columns)
                return put(pieces, [shape], unit_layouts(turned))[0]
            pieces = pieces.astype(F32).reshape(branches, cores, row_share, chips, part)
            if turned:
                return pieces.transpose(3, 1, 0, 4, 2).reshape(hidden_columns, row_share)
            return pieces.transpose(2, 3, 1, 0, 4).reshape(row_share, hidden_columns)

        def finish(chain):
            while chain.step < chips - 1:
                chain.send()
                step(chain)
            return spread(chain)

        step(up_line)
        up_line.send()
        joined_chain = terms((live.pop("normed"), live["joined_grad"]), (live["g"], live["mixed"]))
        joined_chain.send()
        step(up_line)
        down_line = Line(live.pop("down"), z, chips)
        down_line.send()
        live["active"], live["slope"] = hidden_values()
        down_chain = terms((live["g"], live["active"]))
        down_chain.prepare()
        step(down_line, joined_chain)
        down_line.send()
        down_chain.send()
        joined_chain.prepare()
        g_float = g_piece.astype(F32)
        out_slot = lax.dynamic_update_slice(
            jnp.zeros((width,), F32), jnp.sum(g_float, axis=0), (column_start,)
        )
        joined_slot = lax.dynamic_update_slice(
            jnp.zeros_like(joined_bias),
            joined_bias_grad.reshape(-1),
            ((m * heads + head_slot) * head_columns,),
        )
        live["slots"] = jnp.concatenate([out_slot, joined_slot])
        step(down_line, down_chain)
        down_line.send()
        joined_chain.send()
        down_chain.prepare()
        step(down_line, joined_chain)
        joined_chain.send()
        live["out_other"] = forward_terms(1)
        live["grad"], live["bias"] = hidden_gradient()
        step(joined_chain)
        down_chain.send()
        live["out_got"] = swap_core(live.pop("out_other"))
        live["joined_pieces"] = finish(joined_chain)
        up_chain = terms((live.pop("expanded"), live["grad"]))
        live.pop("g")
        up_chain.prepare()
        live["out"] = forward_terms(0, live.pop("out_got"))
        step(down_chain)
        forward_sum = block_sum(live.pop("out"))
        up_chain.send()
        down_chain.prepare()
        live["in_other"], live["sums_other"] = input_terms(1)
        step(up_chain)
        live["forward_sum"] = forward_sum
        down_chain.send()
        live["in_got"] = swap_core(live.pop("in_other"))
        up_chain.prepare()
        live["in"], live["sums_own"] = input_terms(0, live.pop("in_got"))
        up_slot = lax.dynamic_update_slice(
            jnp.zeros((models, chips, cores, branches, part), F32),
            live.pop("bias").reshape(1, chips, 1, 1, part),
            (m, 0, c, b, 0),
        ).reshape(-1)
        live["slots"] = jnp.concatenate([live["slots"], up_slot])
        step(down_chain)
        up_chain.send()
        live["in_got"] = first_sends(live["in"])
        sums = live.pop("sums_own") + live.pop("sums_other")
        small = jnp.concatenate([sums.reshape(-1), live.pop("slots")])
        small = (
            small
            + partner(small, core=1)
            + partner(small, branch=1)
            + partner(small, branch=1, core=1)
        )
        live["joined_out"], live["dense_out"] = place_joined(live.pop("joined_pieces"))
        down_pieces = finish(down_chain)
        step(up_chain)
        up_chain.prepare()
        step()
        live["down_pieces"] = down_pieces
        up_chain.send()
        live["in"] = first_sum(live["in"], live.pop("in_got"))
        live["in_got"] = second_sends(live["in"])
        near = lax.ppermute(small, "z", [(i, i ^ 1) for i in range(chips)])
        far = [
            lax.ppermute(
                small,
                ("mp", "z"),
                [
                    (one * chips + i, (1 - one) * chips + (i ^ flip))
                    for one in range(models)
                    for i in range(chips)
                ],
            )
            for flip in range(2)
        ]
        live["small"] = small + near + far[0] + far[1]
        forward_sum = live["forward_sum"]
        residual = columns_of(x_own, column_start, span).astype(F32)
        column_bias = columns_of(dense_bias + down_bias, column_start, span)
        block_output = (residual + forward_sum + column_bias).astype(BF16)
        live["block_output"] = block_output
        step(up_chain)
        block_output = live["block_output"]
        up_pieces = finish(up_chain)
        small = live["small"]
        flip = 2
        while flip < chips:
            small = small + lax.ppermute(small, "z", [(i, i ^ flip) for i in range(chips)])
            flip *= 2
        input_sum = second_sum(live.pop("in"), live.pop("in_got"))
        joined_out, dense_out = live["joined_out"], live["dense_out"]
        down_out, up_out = place_units(live["down_pieces"], True), place_units(up_pieces, False)

        input_gradient = (g_float + input_sum).astype(BF16)

        w = width
        joined_end = 5 * w + joined_bias.shape[0]
        return (
            block_output.reshape(rows, length, span),
            input_gradient.reshape(rows, length, span),
            small[:w],
            small[w : 2 * w],
            joined_out,
            small[5 * w : joined_end],
            dense_out,
            small[4 * w : 5 * w],
            small[2 * w : 3 * w],
            small[3 * w : 4 * w],
            up_out,
            small[joined_end:],
            down_out,
            small[4 * w : 5 * w],
        )

    data = ("z", "core")
    everything = ("branch", "z", "core")
    in_specs = (
        P(data, None, None),
        P(data, None, ("branch", "mp")),
        P(data, None),
        P(),
        P(),
        P(data, "mp"),
        P(),
        P(("mp", "z", "core"), None),
        P(),
        P(),
        P(),
        P(data, "mp"),
        P(),
        P(("mp", "z", "core"), None),
        P(),
    )
    out_specs = (
        P(data, None, ("branch", "mp")),
        P(data, None, ("branch", "mp")),
        P(),
        P(),
        P(everything, "mp"),
        P(),
        P("mp", everything),
        P(),
        P(),
        P(),
        P(everything, "mp"),
        P(),
        P("mp", everything),
        P(),
    )
    return jax.shard_map(
        on_device, mesh=fine, in_specs=in_specs, out_specs=out_specs, check_vma=False
    )
```

```python
import functools
import math

import jax
import jax.numpy as jnp
from jax import lax
from jax.experimental import pallas as pl
from jax.experimental.pallas import tpu as pltpu
from jax.sharding import Mesh, PartitionSpec as P

HEAD = 256
ROT = 64
LANES = 128
NEGATIVE = -1e30
VMEM_BYTES = 56 * 1024 * 1024
F32 = jnp.float32
BF16 = jnp.bfloat16


def rotary_tables(segment_rows):
    length = segment_rows.shape[1]
    before = jnp.sum(
        (segment_rows[:, None, :] < segment_rows[:, :, None]).astype(jnp.int32), axis=2
    )
    places = (jnp.arange(length, dtype=jnp.int32)[None] - before).astype(F32)
    frequency = 10000.0 ** (-jnp.arange(0, ROT, 2).astype(F32) / ROT)
    angles = (places[:, :, None] * frequency).reshape(-1, ROT // 2)
    cosine, sine = jnp.cos(angles), jnp.sin(angles)
    none = jnp.zeros_like(sine)
    rest = jnp.zeros((angles.shape[0], LANES - ROT), F32)
    return (
        jnp.concatenate([cosine, cosine, rest + 1.0], axis=1),
        jnp.concatenate([-sine, none, rest], axis=1),
        jnp.concatenate([none, sine, rest], axis=1),
    )


def rotate(values, self_factor, right_factor, left_factor):
    half = ROT // 2
    front = values[:, :LANES]
    turned = (
        front * self_factor
        + pltpu.roll(front, LANES - half, 1) * right_factor
        + pltpu.roll(front, half, 1) * left_factor
    )
    return jnp.concatenate([turned, values[:, LANES:]], axis=1)


def dot(left, right, left_dim, right_dim):
    return lax.dot_general(
        left, right, (((left_dim,), (right_dim,)), ((), ())), preferred_element_type=F32
    )


def whole(shape):
    return pl.BlockSpec(shape, lambda i: (0,) * len(shape), pipeline_mode=pl.Buffered(1))


def tile(rows, columns):
    return pl.BlockSpec((rows, columns), lambda i: (i, 0))


def run(body, steps, ins, outs, args, flops, transcendentals=0):
    scratch = []
    if any(isinstance(arg, Line) for arg in args):
        body, ins, args, scratch = put_together(body, ins, args)
    shapes = [jax.ShapeDtypeStruct(shape, dtype) for _, shape, dtype in outs]
    moved = sum(a.size * a.dtype.itemsize for a in list(args) + shapes)
    return pl.pallas_call(
        body,
        grid=(steps,),
        in_specs=ins,
        out_specs=[spec for spec, _, _ in outs],
        out_shape=shapes,
        scratch_shapes=scratch,
        cost_estimate=pl.CostEstimate(
            flops=2 * flops, bytes_accessed=moved, transcendentals=transcendentals
        ),
        compiler_params=pltpu.CompilerParams(vmem_limit_bytes=VMEM_BYTES),
    )(*args)


def put_together(body, ins, args):
    new_ins, new_args, places, scratch = [], [], [], []
    for spec, arg in zip(ins, args):
        if not isinstance(arg, Line):
            new_ins.append(spec)
            new_args.append(arg)
            places.append(None)
        elif arg.full is not None:
            new_ins.append(spec)
            new_args.append(arg.full)
            places.append(None)
        else:
            slots = arg.slots()
            rows, columns = slots[0].shape
            new_ins += [pl.BlockSpec(memory_space=pl.ANY)] * len(slots)
            new_args += slots
            places.append((len(slots), rows, arg.count))
            scratch += [
                pltpu.VMEM((arg.count * rows, columns), slots[0].dtype),
                pltpu.SemaphoreType.DMA((arg.count,)),
            ]
            index = arg.index
    if not scratch:
        return body, new_ins, new_args, []

    def whole_body(index_ref, *refs):
        kept, held = refs[: len(refs) - len(scratch)], refs[len(refs) - len(scratch) :]
        inner, lines, at = [], [], 0
        for place in places:
            if place is None:
                inner.append(kept[at])
                at += 1
            else:
                full_ref, sems = held[2 * len(lines) : 2 * len(lines) + 2]
                lines.append((kept[at : at + place[0]], full_ref, sems, place))
                inner.append(full_ref)
                at += place[0]

        @pl.when(pl.program_id(0) == 0)
        def _():
            for blocks, full_ref, sems, (_, rows, count) in lines:
                for j in range(count):
                    for k, block in enumerate(blocks):

                        @pl.when(count - 1 - index_ref[0] + j == k)
                        def _():
                            pltpu.make_async_copy(
                                block, full_ref.at[pl.ds(j * rows, rows)], sems.at[j]
                            ).start()

            for blocks, full_ref, sems, (_, rows, count) in lines:
                for j in range(count):
                    pltpu.make_async_copy(
                        blocks[0], full_ref.at[pl.ds(j * rows, rows)], sems.at[j]
                    ).wait()

        body(*inner, *kept[at:])

    return (
        whole_body,
        [pl.BlockSpec(memory_space=pltpu.SMEM)] + new_ins,
        [index.reshape(1)] + new_args,
        scratch,
    )


def statistics(x):
    mean = jnp.mean(x, axis=-1, keepdims=True)
    center = x - mean
    inverse = lax.rsqrt(jnp.mean(center * center, axis=-1, keepdims=True) + 1e-05)
    return center * inverse, mean, inverse


def either(steps, mine_ref, other_ref):
    return jnp.where(pl.program_id(0) < steps, mine_ref[...], other_ref[...])


def halves(rows, columns, steps):
    return [
        pl.BlockSpec((rows, columns), lambda i: (jnp.minimum(i, steps - 1), 0)),
        pl.BlockSpec((rows, columns), lambda i: (jnp.maximum(i - steps, 0), 0)),
    ]


def norm_body(steps, mine_ref, other_ref, gain_a, shift_a, gain_e, shift_e, normed_ref, expanded_ref, stats_ref):
    hat, mean, inverse = statistics(either(steps, mine_ref, other_ref).astype(F32))
    lane = lax.broadcasted_iota(jnp.int32, stats_ref.shape, 1)
    stats_ref[...] = jnp.where(lane == 0, mean, inverse)
    normed_ref[...] = (hat * gain_a[...] + shift_a[...]).astype(BF16)
    expanded_ref[...] = (hat * gain_e[...] + shift_e[...]).astype(BF16)


def gather_body(steps, starts_ref, *refs):
    pieces, out_ref = refs[:-1], refs[-1]
    span = pieces[0].shape[1]
    for k in range(len(pieces) // 2):
        columns = pl.ds(pl.multiple_of(starts_ref[k], span), span)
        out_ref[:, columns] = either(steps, pieces[2 * k], pieces[2 * k + 1])


def accumulate(ref, value):
    @pl.when(pl.program_id(0) == 0)
    def _():
        ref[...] = value

    @pl.when(pl.program_id(0) != 0)
    def _():
        ref[...] += value


def attention_body(
    normed_ref, joined_ref, bias_ref, self_ref, right_ref, left_ref, column_ref, row_ref, g_ref, dense_ref,
    mixed_ref, grad_ref, bias_grad_ref,
):
    length = normed_ref.shape[0]
    scale = 1.0 / math.sqrt(HEAD)
    factors = self_ref[...], right_ref[...], left_ref[...]
    raw = dot(normed_ref[...], joined_ref[...], 1, 0) + bias_ref[...]
    queries = (rotate(raw[:, :HEAD], *factors) * scale).astype(BF16)
    keyset = rotate(raw[:, HEAD : 2 * HEAD], *factors).astype(BF16)
    valueset = raw[:, 2 * HEAD :].astype(BF16)
    query_index = lax.broadcasted_iota(jnp.int32, (length, length), 0)
    key_index = lax.broadcasted_iota(jnp.int32, (length, length), 1)
    allowed = (column_ref[0] == row_ref[0]) & (key_index <= query_index)
    scores = jnp.where(allowed, dot(queries, keyset, 1, 1), NEGATIVE)
    shifted = jnp.exp(scores - jnp.max(scores, axis=-1, keepdims=True))
    probs = shifted / jnp.sum(shifted, axis=-1, keepdims=True)
    low = probs.astype(BF16)
    mixed_ref[...] = dot(low, valueset, 1, 0).astype(BF16)
    mixed_grad = dot(g_ref[...], dense_ref[...], 1, 1).astype(BF16)
    probs_grad = dot(mixed_grad, valueset, 1, 1)
    value_grad = dot(low, mixed_grad, 0, 0)
    inner = jnp.sum(probs_grad * probs, axis=-1, keepdims=True)
    score_grad = (probs * (probs_grad - inner)).astype(BF16)
    query_grad = rotate(dot(score_grad, keyset, 1, 0) * scale, *back_factors(factors))
    key_grad = rotate(dot(score_grad, queries, 0, 0), *back_factors(factors))
    joined_grad = jnp.concatenate([query_grad, key_grad, value_grad], axis=1).astype(BF16)
    grad_ref[...] = joined_grad
    accumulate(bias_grad_ref, jnp.sum(joined_grad.astype(F32), axis=0, keepdims=True))


def back_factors(factors):
    return factors[0], -factors[1], -factors[2]


def hidden_body(expanded_ref, up_ref, bias_ref, activated_ref, slope_ref):
    block = up_ref.shape[1] // 4
    for k in range(4):
        columns = pl.ds(k * block, block)
        hidden = dot(expanded_ref[...], up_ref[:, columns], 1, 0) + bias_ref[:, columns]
        below = 0.5 * (1.0 + lax.erf(hidden * math.sqrt(0.5)))
        density = jnp.exp(hidden * hidden * -0.5) * (1.0 / math.sqrt(2.0 * math.pi))
        activated_ref[:, columns] = (hidden * below).astype(BF16)
        slope_ref[:, columns] = (below + hidden * density).astype(BF16)


def terms_body(*refs):
    out_ref, start = refs[-1], 0
    for left_ref, right_ref in zip(refs[:-1:2], refs[1:-1:2]):
        stop = start + right_ref.shape[1]
        term = dot(left_ref[...], right_ref[...], 0, 0).astype(BF16)
        out_ref[:, :, :, start:stop] = term.reshape(*out_ref.shape[:3], stop - start)
        start = stop


def hidden_grad_body(g_ref, down_ref, slope_ref, grad_ref, bias_grad_ref):
    grad = dot(g_ref[...], down_ref[...], 1, 1) * slope_ref[...].astype(F32)
    grad = grad.astype(BF16)
    grad_ref[...] = grad
    accumulate(bias_grad_ref, jnp.sum(grad.astype(F32), axis=0, keepdims=True))


def store_blocks(out_ref, values, got_refs):
    blocks, span = out_ref.shape[1], out_ref.shape[3]
    for k in range(blocks):
        block = values[:, k * span : (k + 1) * span]
        for got_ref in got_refs:
            block = block + got_ref[0, k].astype(F32)
        out_ref[0, k] = block.astype(BF16)


def forward_body(mixed_ref, dense_ref, active_ref, down_ref, *refs):
    total = dot(mixed_ref[...], dense_ref[...], 1, 0)
    total += dot(active_ref[...], down_ref[...], 1, 0)
    store_blocks(refs[-1], total, refs[:-1])


def input_body(
    x_ref, stats_ref, joined_grad_ref, joined_ref, hidden_grad_ref, up_ref, gain_a, gain_e, *refs
):
    got_refs, (out_ref, sums_ref) = refs[:-2], refs[-2:]
    normed_grad = dot(joined_grad_ref[...], joined_ref[...], 1, 1)
    expanded_grad = dot(hidden_grad_ref[...], up_ref[...], 1, 1)
    mean, inverse = stats_ref[:, 0:1], stats_ref[:, 1:2]
    hat = (x_ref[...].astype(F32) - mean) * inverse
    weighted = normed_grad * gain_a[...] + expanded_grad * gain_e[...]
    weighted_mean = jnp.mean(weighted, axis=-1, keepdims=True)
    along = jnp.mean(weighted * hat, axis=-1, keepdims=True)
    store_blocks(out_ref, inverse * (weighted - weighted_mean - hat * along), got_refs)

    def down(values):
        return jnp.sum(values, axis=0, keepdims=True)

    sums = jnp.concatenate(
        [down(normed_grad * hat), down(normed_grad), down(expanded_grad * hat), down(expanded_grad)]
    )
    accumulate(sums_ref, sums)


def place_body(layouts, pieces_ref, *outs):
    for device in range(pieces_ref.shape[0]):
        for start, size, target, where, turned in layouts:
            offset = where(device) * size
            values = pieces_ref[device, :, start : start + size].astype(F32)
            if turned:
                outs[target][offset : offset + size, :] = values.T
            else:
                outs[target][:, offset : offset + size] = values


def pick(array, index, axis):
    return lax.dynamic_index_in_dim(array, index, axis, keepdims=False)


def add_low(left, right):
    return (left.astype(F32) + right.astype(F32)).astype(BF16)


SWAP = [(0, 1), (1, 0)]


class Chain:
    def __init__(self, view, index, count):
        self.view, self.index, self.count, self.step = view, index, count, 0
        self.held = self.flight = ()
        self.out = []

    def term(self, share):
        return pick(self.view, jnp.clip(share, 0, self.count - 1), 0)

    def prepare(self):
        if self.step == self.count - 1:
            return
        self.step += 1
        step, count = self.step, self.count
        self.out = [self.term(self.index + count - step), self.term(self.index - count + step)]
        if self.held:
            self.out = [add_low(one, two) for one, two in zip(self.out, self.held)]

    def send(self):
        if not self.out:
            self.prepare()
        if not self.out:
            return
        step, count = self.step, self.count
        self.flight = (
            lax.ppermute(self.out[0], "z", [(i, i + 1) for i in range(step)]),
            lax.ppermute(self.out[1], "z", [(count - 1 - i, count - 2 - i) for i in range(step)]),
        )
        self.out = []

    def land(self, values):
        if values:
            self.held, self.flight = values, ()

    def total(self):
        own = self.term(self.index).astype(F32)
        return (own + self.held[0].astype(F32) + self.held[1].astype(F32)).astype(BF16)


class Line:
    def __init__(self, piece, index, count):
        self.index, self.count, self.step, self.flight = index, count, 0, ()
        self.from_left, self.from_right, self.own, self.full = [], [], piece, None
        if count > 4:
            self.full = lax.all_gather(piece, "z", axis=0, tiled=True)

    def send(self):
        if self.full is not None or self.step == self.count - 1:
            return
        step, count = self.step, self.count
        right, left = (self.from_left[-1], self.from_right[-1]) if step else (self.own, self.own)
        self.flight = (
            lax.ppermute(right, "z", [(i, i + 1) for i in range(step, count - 1)]),
            lax.ppermute(left, "z", [(i + 1, i) for i in range(count - 1 - step)]),
        )
        self.step += 1

    def land(self, values):
        if values:
            self.from_left.append(values[0])
            self.from_right.append(values[1])
            self.flight = ()

    def slots(self):
        return [*self.from_left[::-1], self.own, *self.from_right]


fence = lax.optimization_barrier


def solution(mesh):
    branches, models, datas = (mesh.shape[name] for name in ("branch", "mp", "dp"))
    cores = 2
    chips = datas // cores
    fine = Mesh(
        mesh.devices.reshape(branches, models, chips, cores), ("branch", "mp", "z", "core")
    )

    def on_device(
        block_input,
        cotangent,
        segments,
        attend_gain,
        attend_shift,
        joined_weight,
        joined_bias,
        dense_weight,
        dense_bias,
        expand_gain,
        expand_shift,
        up_weight,
        up_bias,
        down_weight,
        down_bias,
    ):
        rows, length, width = block_input.shape
        b, m, z, c = (lax.axis_index(name) for name in ("branch", "mp", "z", "core"))
        tokens = rows * length
        span = width // (branches * models)
        column_start = (b * models + m) * span
        heads = branches * cores
        head_columns = joined_weight.shape[1] // heads
        hidden_columns = up_weight.shape[1]
        part = down_weight.shape[0] // branches
        units = chips * part
        head_slot = b * cores + c
        row_share = width // (branches * datas)

        def partner(array, **flips):
            names = tuple(name for name, flip in flips.items() if flip)
            if not names:
                return array
            count = 2 ** len(names)
            return lax.ppermute(array, names, [(i, count - 1 - i) for i in range(count)])

        def swap_core(array):
            return partner(array, core=1)

        def in_core_order(mine, other):
            return jnp.where(c == 0, jnp.concatenate([mine, other]), jnp.concatenate([other, mine]))

        def columns_of(array, start, size):
            return lax.dynamic_slice_in_dim(array, start, size, array.ndim - 1)

        def unit_columns(array, core):
            return jnp.concatenate(
                [
                    columns_of(array, ((k * cores + core) * branches + b) * part, part)
                    for k in range(chips)
                ],
                axis=-1,
            )

        def gather(piece):
            return lax.all_gather(piece, "z", axis=0, tiled=True)

        x_own = block_input.reshape(tokens, width)
        g_piece = cotangent.reshape(tokens, span)
        joined_piece = in_core_order(
            columns_of(joined_weight, head_slot * head_columns, head_columns),
            swap_core(columns_of(joined_weight, (b * cores + 1 - c) * head_columns, head_columns)),
        )
        flips = [(db, dm) for db in range(2) for dm in range(2)]
        g_mine = [partner(g_piece, branch=db, mp=dm) for db, dm in flips]
        x_other = swap_core(x_own)
        segment_rows = jnp.concatenate([segments, swap_core(segments)])
        joined_piece, dense_weight = fence((joined_piece, dense_weight))
        spread_dense = chips == heads and HEAD == cores * dense_weight.shape[0]
        if spread_dense:
            few = HEAD // chips
            per_core = chips // cores
            dense_piece = 0
            for j in range(per_core):
                moves = [
                    (
                        (one * chips + one * cores + to) * cores + at,
                        (one * chips + at * per_core + j) * cores + to,
                    )
                    for one in range(branches)
                    for to in range(cores)
                    for at in range(cores)
                ]
                dense_piece = dense_piece + lax.ppermute(
                    dense_weight[j * few : (j + 1) * few], ("branch", "z", "core"), moves
                )
        else:
            dense_piece = dense_weight

        joined_bias_here = columns_of(joined_bias, (m * heads + head_slot) * head_columns, head_columns)
        up_bias_here = unit_columns(columns_of(up_bias, m * hidden_columns, hidden_columns), c)
        down_piece = lax.dynamic_slice_in_dim(down_weight, b * part, part, 0)

        def flat(vector):
            return vector.reshape(1, -1)

        all_tokens = 2 * tokens
        gains = flat(attend_gain), flat(expand_gain)
        small_tile = min(256, length)
        half_steps = tokens // small_tile
        joined_full = gather(joined_piece)
        x_other, joined_piece, up_weight, dense_piece = fence(
            (x_other, joined_piece, up_weight, dense_piece)
        )
        if spread_dense:
            dense_full = gather(dense_piece)
        else:
            dense_full = lax.all_gather(dense_piece, ("z", "core"), axis=0, tiled=True)
            dense_full = lax.dynamic_slice_in_dim(dense_full, head_slot * HEAD, HEAD, 0)
        up_piece = in_core_order(unit_columns(up_weight, c), swap_core(unit_columns(up_weight, 1 - c)))
        normed, expanded, stats = run(
            functools.partial(norm_body, half_steps),
            2 * half_steps,
            halves(small_tile, width, half_steps) + [whole((1, width))] * 4,
            [(tile(small_tile, width), (all_tokens, width), BF16)] * 2
            + [(tile(small_tile, LANES), (all_tokens, LANES), F32)],
            (x_own, x_other, gains[0], flat(attend_shift), gains[1], flat(expand_shift)),
            20 * all_tokens * width,
        )
        rotary = rotary_tables(segment_rows)
        normed, expanded, rotary, g_mine, up_piece, down_piece = fence(
            (normed, expanded, rotary, g_mine, up_piece, down_piece)
        )
        up_line = Line(up_piece, z, chips)
        up_line.send()
        g_other = [swap_core(piece) for piece in g_mine]
        starts = jnp.stack([((b ^ db) * models + (m ^ dm)) * span for db, dm in flips])
        (g,) = run(
            functools.partial(gather_body, half_steps),
            2 * half_steps,
            [pl.BlockSpec(memory_space=pltpu.SMEM)]
            + [spec for _ in flips for spec in halves(small_tile, span, half_steps)],
            [(tile(small_tile, width), (all_tokens, width), BF16)],
            (starts, *[piece for pair in zip(g_mine, g_other) for piece in pair]),
            all_tokens * width,
        )
        up_line.flight, g, down_piece, joined_full, dense_full = fence(
            (up_line.flight, g, down_piece, joined_full, dense_full)
        )
        up_line.land(up_line.flight)
        up_line.send()

        all_rows = 2 * rows
        mixed, joined_grad, joined_bias_grad = run(
            attention_body,
            all_rows,
            [
                tile(length, width),
                whole((width, head_columns)),
                whole((1, head_columns)),
                tile(length, LANES),
                tile(length, LANES),
                tile(length, LANES),
                pl.BlockSpec((1, length, 1), lambda i: (i, 0, 0)),
                pl.BlockSpec((1, 1, length), lambda i: (i, 0, 0)),
                tile(length, width),
                whole((HEAD, width)),
            ],
            [
                (tile(length, HEAD), (all_tokens, HEAD), BF16),
                (tile(length, head_columns), (all_tokens, head_columns), BF16),
                (whole((1, head_columns)), (1, head_columns), F32),
            ],
            (
                normed,
                joined_full,
                flat(joined_bias_here),
                *rotary,
                segment_rows[:, :, None],
                segment_rows[:, None, :],
                g,
                dense_full,
            ),
            2 * all_tokens * (width * (head_columns + HEAD) + 7 * length * HEAD),
            all_tokens * length,
        )

        live = dict(
            mixed=mixed, joined_grad=joined_grad, normed=normed, expanded=expanded, g=g, down=down_piece
        )

        def step(*landing, hold=()):
            fresh, held, views, outs, kept = fence(
                (
                    dict(live),
                    [chain.flight for chain in landing],
                    [chain.view for chain in waiting],
                    [chain.out for chain in chains],
                    [chain.held for chain in hold],
                )
            )
            for chain, one in zip(hold, kept):
                chain.held = one
            for chain, out in zip(chains, outs):
                chain.out = out
            live.update(fresh)
            for chain, one in zip(landing, held):
                chain.land(one)
            for chain, view in zip(waiting, views):
                chain.view = view
            waiting.clear()

        waiting, chains = [], []
        share_rows = cores * row_share

        def terms(*pairs):
            rows_tile = max(512, share_rows)
            group = rows_tile // share_rows
            groups = chips // group
            columns = sum(right.shape[1] for _, right in pairs)
            ins, args = [], []
            for left, right in pairs:
                ins += [pl.BlockSpec((all_tokens, rows_tile), lambda i: (0, i)), whole(right.shape)]
                args += [left, right]
            (view,) = run(
                terms_body,
                branches * groups,
                ins,
                [
                    (
                        pl.BlockSpec(
                            (group, 1, share_rows, columns), lambda i: (i % groups, i // groups, 0, 0)
                        ),
                        (chips, branches, share_rows, columns),
                        BF16,
                    )
                ],
                args,
                2 * all_tokens * width * columns,
            )
            chain = Chain(view, z, chips)
            waiting.append(chain)
            chains.append(chain)
            return chain

        def spread(chain):
            share = chain.total().reshape(branches * cores * row_share, -1)
            pieces = lax.all_to_all(share, ("branch", "core"), 0, 0, tiled=True)
            return pieces.reshape(branches * cores, row_share, -1)

        unit_flops = 2 * all_tokens * width * units
        big_tile = min(512, length)

        def hidden_values():
            return run(
                hidden_body,
                all_tokens // big_tile,
                [tile(big_tile, width), whole((width, units)), whole((1, units))],
                [(tile(big_tile, units), (all_tokens, units), BF16)] * 2,
                (live["expanded"], up_line, flat(up_bias_here)),
                unit_flops,
                2 * all_tokens * units,
            )

        def hidden_gradient():
            return run(
                hidden_grad_body,
                all_tokens // big_tile,
                [tile(big_tile, width), whole((units, width)), tile(big_tile, units)],
                [
                    (tile(big_tile, units), (all_tokens, units), BF16),
                    (whole((1, units)), (1, units), F32),
                ],
                (live["g"], down_line, live.pop("slope")),
                unit_flops,
            )

        blocks = branches * models

        def of_core(core, columns):
            return pl.BlockSpec((small_tile, columns), lambda i: (core * half_steps + i, 0))

        def out_blocks(pieces):
            steps = half_steps // pieces
            return (
                pl.BlockSpec((1, blocks, small_tile, span), lambda i: (i // steps, 0, i % steps, 0)),
                (pieces, blocks, tokens // pieces, span),
                BF16,
            )

        def input_terms(core, *got):
            return run(
                input_body,
                half_steps,
                [
                    tile(small_tile, width),
                    of_core(core, LANES),
                    of_core(core, head_columns),
                    whole((width, head_columns)),
                    of_core(core, units),
                    whole((width, units)),
                    whole((1, width)),
                    whole((1, width)),
                    *[out_blocks(2)[0]] * len(got),
                ],
                [out_blocks(2), (whole((4, width)), (4, width), F32)],
                (
                    (x_own, x_other)[core],
                    stats,
                    live["joined_grad"],
                    joined_full,
                    live["grad"],
                    up_line,
                    *gains,
                    *got,
                ),
                unit_flops // 2 + all_tokens * width * head_columns,
            )

        def forward_terms(core, *got):
            return run(
                forward_body,
                half_steps,
                [
                    of_core(core, HEAD),
                    whole((HEAD, width)),
                    of_core(core, units),
                    whole((units, width)),
                    *[out_blocks(1)[0]] * len(got),
                ],
                [out_blocks(1)],
                (live["mixed"], dense_full, live["active"], down_line, *got),
                unit_flops // 2 + all_tokens * width * HEAD,
            )[0]

        def block_sum(blocks):
            return lax.psum_scatter(blocks[0], ("branch", "mp"), scatter_dimension=0, tiled=True)[0]

        def first_sends(term):
            one, two = (term[h].reshape(branches, models, tokens // 2, span) for h in range(2))
            return partner(pick(one, 1 - b, 0), branch=1), partner(pick(two, 1 - m, 1), mp=1)

        def first_sum(term, got):
            one, two = (term[h].reshape(branches, models, tokens // 2, span) for h in range(2))
            return add_low(pick(one, b, 0), got[0]), add_low(pick(two, m, 1), got[1])

        def second_sends(pair):
            one, two = pair
            return partner(pick(one, 1 - m, 0), mp=1), partner(pick(two, 1 - b, 0), branch=1)

        def second_sum(pair, got):
            one, two = pair
            return jnp.concatenate(
                [
                    pick(one, m, 0).astype(F32) + got[0].astype(F32),
                    pick(two, b, 0).astype(F32) + got[1].astype(F32),
                ]
            )

        def put(pieces, shapes, layouts):
            return run(
                functools.partial(place_body, layouts),
                1,
                [whole(pieces.shape)],
                [(whole(shape), shape, F32) for shape in shapes],
                [pieces],
                0,
            )

        def unit_layouts(turned):
            return [
                (
                    k * part,
                    part,
                    0,
                    lambda device, k=k: (k * cores + device % cores) * branches + device // cores,
                    turned,
                )
                for k in range(chips)
            ]

        simple = part % LANES != 0 or row_share % 8 != 0

        def place_joined(pieces):
            if simple:
                pieces = pieces.astype(F32)
                joined = pieces[:, :, :head_columns].transpose(1, 0, 2).reshape(row_share, -1)
                return joined, pieces[:, :, head_columns:].transpose(0, 2, 1).reshape(-1, row_share)
            return put(
                pieces,
                [(row_share, heads * head_columns), (heads * HEAD, row_share)],
                [
                    (0, head_columns, 0, lambda device: device, False),
                    (head_columns, HEAD, 1, lambda device: device, True),
                ],
            )

        def place_units(pieces, turned):
            if not simple:
                shape = (hidden_columns, row_share) if turned else (row_share, hidden_columns)
                return put(pieces, [shape], unit_layouts(turned))[0]
            pieces = pieces.astype(F32).reshape(branches, cores, row_share, chips, part)
            if turned:
                return pieces.transpose(3, 1, 0, 4, 2).reshape(hidden_columns, row_share)
            return pieces.transpose(2, 3, 1, 0, 4).reshape(row_share, hidden_columns)

        def finish(chain):
            while chain.step < chips - 1:
                chain.send()
                step(chain)
            return spread(chain)

        step(up_line)
        up_line.send()
        joined_chain = terms((live.pop("normed"), live["joined_grad"]), (live["g"], live["mixed"]))
        joined_chain.send()
        step(up_line)
        down_line = Line(live.pop("down"), z, chips)
        down_line.send()
        live["active"], live["slope"] = hidden_values()
        down_chain = terms((live["g"], live["active"]))
        down_chain.prepare()
        step(down_line, joined_chain)
        down_line.send()
        down_chain.send()
        joined_chain.prepare()
        g_float = g_piece.astype(F32)
        out_slot = lax.dynamic_update_slice(
            jnp.zeros((width,), F32), jnp.sum(g_float, axis=0), (column_start,)
        )
        joined_slot = lax.dynamic_update_slice(
            jnp.zeros_like(joined_bias),
            joined_bias_grad.reshape(-1),
            ((m * heads + head_slot) * head_columns,),
        )
        live["slots"] = jnp.concatenate([out_slot, joined_slot])
        step(down_line, down_chain)
        down_line.send()
        joined_chain.send()
        down_chain.prepare()
        step(down_line, joined_chain)
        joined_chain.send()
        live["out_other"] = forward_terms(1)
        live["grad"], live["bias"] = hidden_gradient()
        step(joined_chain)
        down_chain.send()
        live["out_got"] = swap_core(live.pop("out_other"))
        live["joined_pieces"] = finish(joined_chain)
        up_chain = terms((live.pop("expanded"), live["grad"]))
        live.pop("g")
        up_chain.prepare()
        live["out"] = forward_terms(0, live.pop("out_got"))
        step(down_chain)
        forward_sum = block_sum(live.pop("out"))
        up_chain.send()
        down_chain.prepare()
        live["in_other"], live["sums_other"] = input_terms(1)
        step(up_chain)
        live["forward_sum"] = forward_sum
        down_chain.send()
        live["in_got"] = swap_core(live.pop("in_other"))
        up_chain.prepare()
        live["in"], live["sums_own"] = input_terms(0, live.pop("in_got"))
        up_slot = lax.dynamic_update_slice(
            jnp.zeros((models, chips, cores, branches, part), F32),
            live.pop("bias").reshape(1, chips, 1, 1, part),
            (m, 0, c, b, 0),
        ).reshape(-1)
        live["slots"] = jnp.concatenate([live["slots"], up_slot])
        step(down_chain)
        up_chain.send()
        live["in_got"] = first_sends(live["in"])
        sums = live.pop("sums_own") + live.pop("sums_other")
        small = jnp.concatenate([sums.reshape(-1), live.pop("slots")])
        small = (
            small
            + partner(small, core=1)
            + partner(small, branch=1)
            + partner(small, branch=1, core=1)
        )
        live["joined_out"], live["dense_out"] = place_joined(live.pop("joined_pieces"))
        down_pieces = finish(down_chain)
        step(up_chain)
        up_chain.prepare()
        step()
        live["down_pieces"] = down_pieces
        up_chain.send()
        live["in"] = first_sum(live["in"], live.pop("in_got"))
        live["in_got"] = second_sends(live["in"])
        near = lax.ppermute(small, "z", [(i, i ^ 1) for i in range(chips)])
        far = [
            lax.ppermute(
                small,
                ("mp", "z"),
                [
                    (one * chips + i, (1 - one) * chips + (i ^ flip))
                    for one in range(models)
                    for i in range(chips)
                ],
            )
            for flip in range(2)
        ]
        live["small"] = small + near + far[0] + far[1]
        forward_sum = live["forward_sum"]
        residual = columns_of(x_own, column_start, span).astype(F32)
        column_bias = columns_of(dense_bias + down_bias, column_start, span)
        block_output = (residual + forward_sum + column_bias).astype(BF16)
        live["block_output"] = block_output
        step(up_chain)
        block_output = live["block_output"]
        up_pieces = finish(up_chain)
        small = live["small"]
        flip = 2
        while flip < chips:
            small = small + lax.ppermute(small, "z", [(i, i ^ flip) for i in range(chips)])
            flip *= 2
        input_sum = second_sum(live.pop("in"), live.pop("in_got"))
        joined_out, dense_out = live["joined_out"], live["dense_out"]
        down_out, up_out = place_units(live["down_pieces"], True), place_units(up_pieces, False)

        input_gradient = (g_float + input_sum).astype(BF16)

        w = width
        joined_end = 5 * w + joined_bias.shape[0]
        return (
            block_output.reshape(rows, length, span),
            input_gradient.reshape(rows, length, span),
            small[:w],
            small[w : 2 * w],
            joined_out,
            small[5 * w : joined_end],
            dense_out,
            small[4 * w : 5 * w],
            small[2 * w : 3 * w],
            small[3 * w : 4 * w],
            up_out,
            small[joined_end:],
            down_out,
            small[4 * w : 5 * w],
        )

    data = ("z", "core")
    everything = ("branch", "z", "core")
    in_specs = (
        P(data, None, None),
        P(data, None, ("branch", "mp")),
        P(data, None),
        P(),
        P(),
        P(data, "mp"),
        P(),
        P(("mp", "z", "core"), None),
        P(),
        P(),
        P(),
        P(data, "mp"),
        P(),
        P(("mp", "z", "core"), None),
        P(),
    )
    out_specs = (
        P(data, None, ("branch", "mp")),
        P(data, None, ("branch", "mp")),
        P(),
        P(),
        P(everything, "mp"),
        P(),
        P("mp", everything),
        P(),
        P(),
        P(),
        P(everything, "mp"),
        P(),
        P("mp", everything),
        P(),
    )
    return jax.shard_map(
        on_device, mesh=fine, in_specs=in_specs, out_specs=out_specs, check_vma=False
    )
```
